32 devices in a mesh: dp: 8 (over y, x, core), gen: 4 (over z).
Axes of the slice: x: 2, y: 2, z: 4, core: 2. Of those that a mesh axis runs over, the one named last changes fastest.
Arguments:
- enc_input: bfloat16 [32, 512, 768], P(('dp', 'gen')), may hold values from -6 to 6
- dec_input: bfloat16 [32, 512, 768], P(('dp', 'gen')), may hold values from -6 to 6
- enc_segments: int32 [32, 512], P(('dp', 'gen')), may hold values from 0 to 3, never falling along the last dimension, each value on 1 to 256 neighbouring positions
- dec_segments: int32 [32, 512], P(('dp', 'gen')), may hold values from 0 to 3, never falling along the last dimension, each value on 1 to 256 neighbouring positions
- task_ids: int32 [32], P(('dp', 'gen')), may hold values from 0 to 7
- cotangent: bfloat16 [32, 512, 768], P(('dp', 'gen')), may hold values from -6 to 6
- enc_norms: bfloat16 [2, 768], replicated, may hold values from 0.5 to 1.5
- enc_qkv: bfloat16 [768, 2304], replicated, may hold values from -0.21875 to 0.21875
- enc_proj: bfloat16 [768, 768], replicated, may hold values from -0.875 to 0.875
- enc_up: bfloat16 [768, 3072], replicated, may hold values from -0.21875 to 0.21875
- enc_down: bfloat16 [3072, 768], replicated, may hold values from -0.109375 to 0.109375
- dec_norms: bfloat16 [4, 768], replicated, may hold values from 0.5 to 1.5
- dec_qkv: bfloat16 [768, 2304], replicated, may hold values from -0.21875 to 0.21875
- dec_self_proj: bfloat16 [768, 768], replicated, may hold values from -0.875 to 0.875
- dec_cross_q: bfloat16 [768, 768], replicated, may hold values from -0.21875 to 0.21875
- dec_cross_kv: bfloat16 [768, 1536], replicated, may hold values from -0.21875 to 0.21875
- dec_cross_proj: bfloat16 [768, 768], replicated, may hold values from -0.875 to 0.875
- dec_up: bfloat16 [768, 3072], replicated, may hold values from -0.21875 to 0.21875
- dec_down: bfloat16 [3072, 768], replicated, may hold values from -0.109375 to 0.109375
- task_emb: float32 [8, 64], replicated, may hold values from -6 to 6
- layer_emb: float32 [2, 128], replicated, may hold values from -6 to 6
- proj_task: float32 [64, 128], replicated, may hold values from -0.75 to 0.75
- gen_weight: bfloat16 [128, 48, 768], P(None, None, 'gen'), may hold values from -0.01953125 to 0.01953125
- gen_vector: bfloat16 [128, 3, 768], P(None, None, 'gen'), may hold values from -0.125 to 0.125
Outputs:
- dec_out: bfloat16 [32, 512, 768], P(('dp', 'gen'))
- enc_input_grad: bfloat16 [32, 512, 768], P(('dp', 'gen'))
- dec_input_grad: bfloat16 [32, 512, 768], P(('dp', 'gen'))
- enc_norms_grad: float32 [2, 768], P(None, 'dp')
- enc_qkv_grad: float32 [768, 2304], P('dp')
- enc_proj_grad: float32 [768, 768], P('dp')
- enc_up_grad: float32 [768, 3072], P('dp')
- enc_down_grad: float32 [3072, 768], P('dp')
- dec_norms_grad: float32 [4, 768], P(None, 'dp')
- dec_qkv_grad: float32 [768, 2304], P('dp')
- dec_self_proj_grad: float32 [768, 768], P('dp')
- dec_cross_q_grad: float32 [768, 768], P('dp')
- dec_cross_kv_grad: float32 [768, 1536], P('dp')
- dec_cross_proj_grad: float32 [768, 768], P('dp')
- dec_up_grad: float32 [768, 3072], P('dp')
- dec_down_grad: float32 [3072, 768], P('dp')
- task_emb_grad: float32 [8, 64], replicated
- layer_emb_grad: float32 [2, 128], replicated
- proj_task_grad: float32 [64, 128], replicated
- gen_weight_grad: float32 [128, 48, 768], P(None, None, 'gen')
- gen_vector_grad: float32 [128, 3, 768], P(None, None, 'gen')
The draws below stay inside these ranges and needn't reach their ends.
Inputs may be any that keep to these rules, and one draw needn't show every extreme that they name: `enc_segments`: segment numbers never fall along a row; each row holds all 4 numbers, each on at most 256 positions. `dec_segments`: segment numbers never fall along a row; each row holds all 4 numbers, each on at most 256 positions.
All inputs are finite; a program needn't handle non-finite values.
Results may differ from the reference program's by a relative error of at most 0.025.
Values may be sent and summed in bfloat16 or wider, within the bound.
A program may use at most 320 MiB of HBM per device.

```python
import math
import jax
import jax.numpy as jnp
import numpy as np
from jax import lax

D = 768
H = 12
HD = 64
FF = 3072
AD = 24
TE = 64
HH = 128
TASKS = 8
LAYERS = 2
LEN = 512
DOCS = 4
ROWS = 32


def set_ends(values, rng, least, largest):
    longest = values.shape.index(max(values.shape))
    spots = []
    for shift in (0, 1):
        where = [jax.random.randint(jax.random.fold_in(rng, axis), (), 0, length) for axis, length in enumerate(values.shape)]
        where[longest] = (where[longest] + shift) % values.shape[longest]
        spots.append(tuple(where))
    return values.at[spots[0]].set(least).at[spots[1]].set(largest)


def block_scale(rng, shape, cuts, low, largest):
    def one(dim, parts):
        steps = jax.random.uniform(jax.random.fold_in(jax.random.fold_in(rng, 6), dim), (parts,), jnp.float32, low / len(cuts), largest / len(cuts))
        return jnp.repeat(jnp.exp(steps), shape[dim] // parts).reshape((-1,) + (1,) * (len(shape) - dim - 1))

    factor_of = one(*cuts[0])
    for cut in cuts[1:]:
        factor_of = factor_of * one(*cut)
    return factor_of


def split_up(amount, total, bound, lean):
    weights = [(1 << 20) // math.isqrt(standing ** lean) + 1 for standing in range(2, amount + 1)]
    rest, counts = total - bound - (amount - 1), [1] * (amount - 1)
    while rest > 0:
        movable = [i for i in range(amount - 1) if counts[i] < bound]
        mass, remaining = sum([weights[i] for i in movable]), rest
        for i in movable:
            addition = min(bound - counts[i], max(1, remaining * weights[i] // mass), rest)
            counts[i] = counts[i] + addition
            rest = rest - addition
    return np.array([bound] + counts)


def ragged_sizes(rng, number_of, total, reach, lean):
    if number_of == 2:
        one = jax.random.randint(rng, (), max(1, total - reach), min(reach, total - 1) + 1)
        return jnp.stack([one, total - one])
    tallies = jnp.asarray(split_up(number_of, total, reach, lean), jnp.int32)
    twos = (number_of - 1) // 2
    giver, receiver = tallies[1:1 + 2 * twos:2], tallies[2:2 + 2 * twos:2]
    slack = jnp.minimum(giver - 1, reach - receiver)
    shifted = jax.random.randint(jax.random.fold_in(rng, 1), (twos,), 0, 1 << 20) % (slack + 1)
    tallies = tallies.at[1:1 + 2 * twos:2].set(giver - shifted).at[2:2 + 2 * twos:2].set(receiver + shifted)
    return tallies[jax.random.permutation(jax.random.fold_in(rng, 2), number_of)]


def normal_values(own_key, shape, deviation, bound, shards=(), held_as=jnp.bfloat16):
    entries = deviation * jax.random.normal(own_key, shape, jnp.float32)
    if shards:
        entries = entries * block_scale(own_key, shape, shards, -0.22, 0.18)
    return jnp.clip(entries, -bound, bound).astype(held_as)


def setup_inputs(seed: int = 0) -> dict:
    arg_keys = jax.random.split(jax.random.key(seed), 25)
    enc_input = normal_values(arg_keys[0], (ROWS, LEN, D), 1.0, 6.0, ((0, 32),))
    dec_input = normal_values(arg_keys[1], (ROWS, LEN, D), 1.0, 6.0, ((0, 32),))
    enc_segments = jax.vmap(lambda own: jnp.searchsorted(jnp.cumsum(ragged_sizes(own, DOCS, LEN, LEN // 2, 0)), jnp.arange(LEN), side="right"))(jax.random.split(arg_keys[2], ROWS)).reshape((ROWS, LEN)).astype(jnp.int32)
    dec_segments = jax.vmap(lambda own: jnp.searchsorted(jnp.cumsum(ragged_sizes(own, DOCS, LEN, LEN // 2, 0)), jnp.arange(LEN), side="right"))(jax.random.split(arg_keys[3], ROWS)).reshape((ROWS, LEN)).astype(jnp.int32)
    task_ids = set_ends(jax.random.randint(arg_keys[4], (ROWS,), 0, TASKS), jax.random.fold_in(arg_keys[4], 1), 0, TASKS - 1).astype(jnp.int32)
    cotangent = normal_values(arg_keys[5], (ROWS, LEN, D), 1.0, 6.0, ((0, 32),))
    enc_norms = jnp.clip(1.0 + 0.1 * jax.random.normal(arg_keys[6], (2, D), jnp.float32), 0.5, 1.5).astype(jnp.bfloat16)
    enc_qkv = normal_values(arg_keys[7], (D, 3 * D), D ** -0.5, 0.21875)
    enc_proj = normal_values(arg_keys[8], (D, D), (D // 16) ** -0.5, 0.875)
    enc_up = normal_values(arg_keys[9], (D, FF), D ** -0.5, 0.21875)
    enc_down = normal_values(arg_keys[10], (FF, D), FF ** -0.5, 0.109375)
    dec_norms = jnp.clip(1.0 + 0.1 * jax.random.normal(arg_keys[11], (4, D), jnp.float32), 0.5, 1.5).astype(jnp.bfloat16)
    dec_qkv = normal_values(arg_keys[12], (D, 3 * D), D ** -0.5, 0.21875)
    dec_self_proj = normal_values(arg_keys[13], (D, D), (D // 16) ** -0.5, 0.875)
    dec_cross_q = normal_values(arg_keys[14], (D, D), D ** -0.5, 0.21875)
    dec_cross_kv = normal_values(arg_keys[15], (D, 2 * D), D ** -0.5, 0.21875)
    dec_cross_proj = normal_values(arg_keys[16], (D, D), (D // 16) ** -0.5, 0.875)
    dec_up = normal_values(arg_keys[17], (D, FF), D ** -0.5, 0.21875)
    dec_down = normal_values(arg_keys[18], (FF, D), FF ** -0.5, 0.109375)
    task_emb = normal_values(arg_keys[19], (TASKS, TE), 1.0, 6.0, (), jnp.float32)
    layer_emb = normal_values(arg_keys[20], (LAYERS, HH), 1.0, 6.0, (), jnp.float32)
    proj_task = normal_values(arg_keys[21], (TE, HH), TE ** -0.5, 0.75, (), jnp.float32)
    gen_weight = normal_values(arg_keys[22], (HH, 2 * AD, D), (HH * D) ** -0.5, 0.01953125, ((2, 4),))
    gen_vector = normal_values(arg_keys[23], (HH, 3, D), (HH * 16) ** -0.5, 0.125, ((2, 4),))
    return {"enc_input": enc_input, "dec_input": dec_input, "enc_segments": enc_segments, "dec_segments": dec_segments, "task_ids": task_ids, "cotangent": cotangent, "enc_norms": enc_norms, "enc_qkv": enc_qkv, "enc_proj": enc_proj, "enc_up": enc_up, "enc_down": enc_down, "dec_norms": dec_norms, "dec_qkv": dec_qkv, "dec_self_proj": dec_self_proj, "dec_cross_q": dec_cross_q, "dec_cross_kv": dec_cross_kv, "dec_cross_proj": dec_cross_proj, "dec_up": dec_up, "dec_down": dec_down, "task_emb": task_emb, "layer_emb": layer_emb, "proj_task": proj_task, "gen_weight": gen_weight, "gen_vector": gen_vector}


@jax.custom_vjp
def low(v):
    return lax.optimization_barrier(v.astype(jnp.bfloat16)).astype(jnp.float32)

@jax.custom_vjp
def low_back(v):
    return v

def low_keep(v):
    return (low(v), None)

def low_pass(kept, grad):
    return (grad,)

def back_keep(v):
    return (v, None)

def back_low(kept, grad):
    return (low(grad),)
low.defvjp(low_keep, low_pass)
low_back.defvjp(back_keep, back_low)

def matmul_high(left_side, right_side):
    return jnp.dot(left_side, right_side, precision=lax.Precision.HIGHEST)

def rms_norm(values, norm_gain):
    return values * lax.rsqrt(lax.optimization_barrier(jnp.mean(values * values, axis=-1, keepdims=True)) + 1e-06) * norm_gain

def layer_norm(values, norm_gain, norm_shift):
    centred = values - lax.optimization_barrier(jnp.mean(values, axis=-1, keepdims=True))
    return centred * lax.rsqrt(lax.optimization_barrier(jnp.mean(centred * centred, axis=-1, keepdims=True)) + 1e-05) * norm_gain + norm_shift

def gelu_exact(values):
    return jax.nn.gelu(values, approximate=False)

def split_heads(matrix):
    return matrix.reshape(matrix.shape[0], H, HD)

def attend(queries, key_set, value_set, allowed):
    scores = low_back(jnp.einsum('qhd,khd->hqk', queries, key_set, precision=lax.Precision.HIGHEST) * HD ** (-0.5))
    scores = jnp.where(allowed[None], scores, -1e+30)
    weights = jax.nn.softmax(scores, axis=-1)
    mixed_out = jnp.einsum('hqk,khd->qhd', low(weights), value_set, precision=lax.Precision.HIGHEST)
    return low(low_back(mixed_out.reshape(queries.shape[0], D)))

def self_branch(normed, w_joint, w_output, allowed):
    joint_proj = low(low_back(matmul_high(low(normed), w_joint)))
    mixed_out = attend(split_heads(joint_proj[:, :D]), split_heads(joint_proj[:, D:2 * D]), split_heads(joint_proj[:, 2 * D:]), allowed)
    return low_back(matmul_high(mixed_out, w_output))

def feed_forward(normed, w_up, w_down):
    hidden = low(gelu_exact(low_back(matmul_high(low(normed), w_up))))
    return low_back(matmul_high(hidden, w_down))

def adapter(values, weights, vector):
    normed = low(layer_norm(values, 1.0 + vector[1], vector[2]))
    inner_pre = gelu_exact(low_back(matmul_high(normed, weights[:AD].T)))
    return low_back(matmul_high(low(inner_pre), weights[AD:])) * (D / AD) ** 0.5 + vector[0]

def generate(task_emb, layer_emb, proj_task, gen_weight, gen_vector):
    source = gelu_exact(matmul_high(task_emb, proj_task)[:, None, :] + layer_emb[None, :, :])
    source = low(source.reshape(TASKS * LAYERS, HH))
    weights = low(jnp.einsum('th,hkd->tkd', source, gen_weight, precision=lax.Precision.HIGHEST))
    vectors = low(jnp.einsum('th,hkd->tkd', source, gen_vector, precision=lax.Precision.HIGHEST))
    return (weights, vectors)

def reference(enc_input, dec_input, enc_segments, dec_segments, task_ids, cotangent, enc_norms, enc_qkv, enc_proj, enc_up, enc_down, dec_norms, dec_qkv, dec_self_proj, dec_cross_q, dec_cross_kv, dec_cross_proj, dec_up, dec_down, task_emb, layer_emb, proj_task, gen_weight, gen_vector):
    floats = tuple((argument.astype(jnp.float32) for argument in (enc_input, dec_input, enc_norms, enc_qkv, enc_proj, enc_up, enc_down, dec_norms, dec_qkv, dec_self_proj, dec_cross_q, dec_cross_kv, dec_cross_proj, dec_up, dec_down, task_emb, layer_emb, proj_task, gen_weight, gen_vector)))

    def forward(enc_rows, dec_rows, enc_norms, enc_qkv, enc_proj, enc_up, enc_down, dec_norms, dec_qkv, dec_self_proj, dec_cross_q, dec_cross_kv, dec_cross_proj, dec_up, dec_down, task_emb, layer_emb, proj_task, gen_weight, gen_vector):
        adapter_weights, adapter_vectors = generate(task_emb, layer_emb, proj_task, gen_weight, gen_vector)

        def one_row(carried, row_items):
            enc_row, dec_row, enc_seg, dec_seg, task_row = row_items
            places = jnp.arange(enc_seg.shape[0])
            same_enc = enc_seg[:, None] == enc_seg[None, :]
            hidden = enc_row + self_branch(rms_norm(enc_row, enc_norms[0]), enc_qkv, enc_proj, same_enc)
            ffn_out = feed_forward(rms_norm(hidden, enc_norms[1]), enc_up, enc_down)
            first_pair = (task_row * LAYERS).astype(jnp.int32)
            encoded = hidden + ffn_out + adapter(ffn_out, adapter_weights[first_pair], adapter_vectors[first_pair])
            causal = (dec_seg[:, None] == dec_seg[None, :]) & (places[:, None] >= places[None, :])
            hidden = dec_row + self_branch(rms_norm(dec_row, dec_norms[0]), dec_qkv, dec_self_proj, causal)
            queries = low(low_back(matmul_high(low(rms_norm(hidden, dec_norms[1])), dec_cross_q)))
            memory = low(low_back(matmul_high(low(rms_norm(encoded, dec_norms[3])), dec_cross_kv)))
            crossed = attend(split_heads(queries), split_heads(memory[:, :D]), split_heads(memory[:, D:]), dec_seg[:, None] == enc_seg[None, :])
            hidden = hidden + low_back(matmul_high(crossed, dec_cross_proj))
            ffn_out = feed_forward(rms_norm(hidden, dec_norms[2]), dec_up, dec_down)
            result = hidden + ffn_out + adapter(ffn_out, adapter_weights[first_pair + 1], adapter_vectors[first_pair + 1])
            return (carried, result)
        _, outputs = lax.scan(jax.checkpoint(one_row), jnp.zeros((), jnp.float32), (enc_rows, dec_rows, enc_segments, dec_segments, task_ids))
        return outputs
    outputs, pull = jax.vjp(forward, *floats)
    gradients = pull(cotangent.astype(jnp.float32))
    return (outputs.astype(jnp.bfloat16), gradients[0].astype(jnp.bfloat16), gradients[1].astype(jnp.bfloat16), gradients[2], gradients[3], gradients[4], gradients[5], gradients[6], gradients[7], gradients[8], gradients[9], gradients[10], gradients[11], gradients[12], gradients[13], gradients[14], gradients[15], gradients[16], gradients[17], gradients[18], gradients[19])
```

```python
import functools
from typing import NamedTuple

import jax
import jax.numpy as jnp
from jax import lax
from jax.experimental import pallas as pl
from jax.experimental.pallas import tpu as pltpu
from jax.sharding import PartitionSpec as P

H = 12
HD = 64
GROUP = 4 * HD
WIDE_GROUP = 6 * HD
VMEM_LIMIT = 60 * 1024 * 1024
LAGS = (2, 2, 2, 2)
HIGHEST = lax.Precision.HIGHEST
LOW = jnp.bfloat16
WIDE = jnp.float32


def dot_nn(left_side, right_side):
    return jnp.dot(left_side, right_side, preferred_element_type=WIDE)


def dot_nt(left_side, right_side):
    return lax.dot_general(
        left_side, right_side, (((1,), (1,)), ((), ())), preferred_element_type=WIDE
    )


def gelu_parts(values):
    size = jnp.abs(values)
    density = jnp.exp(values * values * -0.5) * 0.3989422804014327
    bottom = 1.0 + 0.2316419 * size
    inverse = pl.reciprocal(bottom, approx=True)
    inverse = inverse * (2.0 - bottom * inverse)
    series = 1.330274429 * inverse - 1.821255978
    series = series * inverse + 1.781477937
    series = series * inverse - 0.356563782
    series = series * inverse + 0.31938153
    tail = series * inverse * density
    return jnp.where(values < 0.0, tail, 1.0 - tail), density


def rms_scale(values):
    return lax.rsqrt(jnp.mean(values * values, axis=-1, keepdims=True) + 1e-06)


def rms_backward(values, norm_gain, grad):
    scale = rms_scale(values)
    normed = values * scale
    pulled = grad * norm_gain
    inner = jnp.mean(normed * pulled, axis=-1, keepdims=True)
    grad_values = scale * (pulled - normed * inner)
    return grad_values, jnp.sum(grad * normed, axis=0, keepdims=True)


def segment_bias(seg_query, seg_key, causal):
    length = seg_query.shape[1]
    column = jnp.broadcast_to(seg_query.astype(WIDE), (128, length)).T[:, :1]
    allowed = column == seg_key.astype(WIDE)
    if causal:
        query_place = lax.broadcasted_iota(jnp.int32, (length, length), 0)
        key_place = lax.broadcasted_iota(jnp.int32, (length, length), 1)
        allowed = allowed & (query_place >= key_place)
    return jnp.where(allowed, 0.0, -1e30)


def row_of(ref, row):
    return ref[row : row + 1].astype(WIDE)


def first_half(shape):
    return lax.broadcasted_iota(jnp.int32, shape, 1) < HD


class Attended(NamedTuple):
    x_t: object
    memory_t: object
    q_t: object
    keys: object
    values: object
    mixed_t: object
    probs: object


class Fed(NamedTuple):
    ffn: object
    x_t: object
    active_t: object
    slope: object


class Gather:
    def __init__(self, n_gen, bottleneck, refs):
        self.n_gen, self.bottleneck, self.line = n_gen, bottleneck, lax.axis_index("gen")
        (
            self.weights, self.pieces, self.more, self.adapters, self.vectors,
            self.asked, self.chosen, self.arrived, self.sems,
        ) = refs

    @staticmethod
    def scratch(n_gen, features):
        return (
            pltpu.VMEM((n_gen, 8, 128), WIDE),
            pltpu.VMEM((n_gen, 2, 64, features), LOW),
            pltpu.VMEM((n_gen, 2, 64, features), LOW),
            pltpu.SemaphoreType.DMA((4, max(n_gen - 1, 1))),
        )

    def ask(self, k):
        sems = self.sems
        return gen_copy(
            self.weights, self.asked, sems.at[0], sems.at[1], self.line, k, self.n_gen
        )

    def answer(self, k):
        sems = self.sems
        return gen_copy(
            self.chosen.at[k], self.arrived, sems.at[2], sems.at[3], self.line, k, self.n_gen
        )

    def pick(self, target, weights):
        for layer in range(2):
            start = 0
            for source in (self.pieces, self.more):
                pairs, rows, features = source.shape
                total = jnp.zeros((rows, features), WIDE)
                for pair in range(pairs):
                    weight = weights[layer : layer + 1, pair : pair + 1]
                    total = total + weight * source[pair].astype(WIDE)
                target[layer, start : start + rows] = total.astype(LOW)
                start += rows

    def step(self, step):
        n_gen, size = self.n_gen, self.bottleneck

        @pl.when(step == 0)
        def _():
            if n_gen > 1:
                gen_barrier(self.line, n_gen)
            for k in range(1, n_gen):
                self.ask(k).start()

        @pl.when(step == 1)
        def _():
            for k in range(1, n_gen):
                self.ask(k).wait()
            for k in range(1, n_gen):
                self.pick(self.chosen.at[k], self.asked[(self.line + k) % n_gen])
                self.answer(k).start()
            self.pick(self.arrived.at[self.line], self.weights[...])

    def finish(self):
        n_gen, size = self.n_gen, self.bottleneck

        @pl.when(pl.program_id(0) == pl.num_programs(0) - 1)
        def _():
            for k in range(1, n_gen):
                self.answer(k).wait()
            rows = 2 * size + 3
            self.adapters[...] = jnp.zeros_like(self.adapters)
            for layer in range(2):
                joined = jnp.concatenate(
                    [self.arrived[j, layer, 0:rows].astype(WIDE) for j in range(n_gen)], axis=1
                ).astype(LOW)
                self.adapters[layer, 0, 0:size] = joined[0:size]
                self.adapters[layer, 1, 0:size] = joined[size : 2 * size]
                self.vectors[layer] = joined[2 * size : 2 * size + 3]


def attention_forward_kernel(
    cross, causal, gather, gain_rows,
    x_ref, gain_ref, memory_ref, memory_gain_ref, seg_q_ref, seg_k_ref,
    wq_ref, wk_ref, wv_ref, wo_ref, *refs,
):
    step = pl.program_id(0)
    more_in = refs[:3] if gather else ()
    refs = refs[len(more_in) :]
    hidden_ref, x_t_ref, memory_t_ref, q_t_ref, k_ref, v_ref, mixed_t_ref, probs_ref = refs[:8]
    more_out = refs[8:10] if gather else ()
    refs = refs[8 + len(more_out) :]
    x_low, memory_low, bias = refs[:3]
    if gather:
        work = Gather(*gather, more_in + more_out + refs[3:])
        work.step(step)

    @pl.when(step == 0)
    def _():
        values = x_ref[...].astype(WIDE)
        hidden_ref[...] = values
        normed = (values * rms_scale(values) * row_of(gain_ref, gain_rows[0])).astype(LOW)
        x_low[...] = normed
        x_t_ref[...] = normed.T
        if cross:
            values = memory_ref[...].astype(WIDE)
            normed = (values * rms_scale(values) * row_of(memory_gain_ref, gain_rows[1])).astype(LOW)
            memory_low[...] = normed
            memory_t_ref[...] = normed.T
        bias[...] = segment_bias(seg_q_ref[...], seg_k_ref[...], causal)

    source_low = memory_low if cross else x_low
    queries = dot_nn(x_low[...], wq_ref[...]).astype(LOW)
    q_t_ref[...] = queries.T
    k_ref[...] = dot_nn(source_low[...], wk_ref[...]).astype(LOW)
    v_ref[...] = dot_nn(source_low[...], wv_ref[...]).astype(LOW)
    scaled = queries * LOW(HD ** (-0.5))
    length = scaled.shape[0]
    lanes = first_half((length, 2 * HD))
    heads = range(scaled.shape[1] // HD)

    def pair_of(ref, head):
        pair = head // 2
        return ref[:, pair * 2 * HD : (pair + 1) * 2 * HD]

    scores = []
    for head in heads:
        mine = jnp.where(lanes if head % 2 == 0 else ~lanes, pair_of(scaled, head), LOW(0))
        scores.append(dot_nt(mine, pair_of(k_ref, head)))
    scores = jnp.stack(scores) + bias[...][None]
    raised = jnp.exp(scores - jnp.max(scores, axis=-1, keepdims=True))
    total = jnp.sum(raised, axis=-1, keepdims=True)
    probs = (raised * (1.0 / total)).astype(LOW)
    probs_ref[...] = probs
    halves = [dot_nn(probs[head], pair_of(v_ref, head)) for head in heads]
    parts = [
        jnp.where(lanes, halves[head], halves[head + 1]).astype(LOW) for head in heads[::2]
    ]
    mixed = jnp.concatenate(parts, axis=1)
    mixed_t_ref[...] = mixed.T
    hidden_ref[...] += dot_nn(mixed, wo_ref[...])
    if gather:
        work.finish()


def whole(shape):
    return pl.BlockSpec(shape, lambda *_: (0,) * len(shape))


def attention_forward(
    x, gains, gain_rows, memory, seg_q, seg_k, weights, w_out, causal, gather=None
):
    n_gen = lax.axis_size("gen")
    more_in, more_out, more_scratch, asked = (), (), (), None
    if gather is not None:
        wanted, pieces, more_pieces, bottleneck = gather
        more_in = (wanted, pieces, more_pieces)
        padded = -bottleneck % 16 + bottleneck
        more_out = (
            jax.ShapeDtypeStruct((2, 2, padded, x.shape[1]), LOW),
            jax.ShapeDtypeStruct((2, 3, x.shape[1]), LOW),
        )
        more_scratch = Gather.scratch(n_gen, pieces.shape[2])
        asked = (n_gen, bottleneck)
    remote = gather is not None and n_gen > 1
    cross = memory is not None
    length, width = x.shape
    groups = width // WIDE_GROUP
    if not cross:
        memory = x
    shape = jax.ShapeDtypeStruct
    columns = pl.BlockSpec((length, WIDE_GROUP), lambda g: (0, g))
    rows = pl.BlockSpec((WIDE_GROUP, length), lambda g: (g, 0))

    def weight_spec(offset):
        return pl.BlockSpec((width, WIDE_GROUP), lambda g: (0, offset + g))

    memory_spec = whole((length, width)) if cross else whole((16, 128))
    memory_t_shape = (width, length) if cross else (16, 128)
    outs = pl.pallas_call(
        functools.partial(attention_forward_kernel, cross, causal, asked, gain_rows),
        grid=(groups,),
        in_specs=[
            whole((length, width)),
            whole(gains.shape),
            memory_spec,
            whole(gains.shape),
            whole((1, length)),
            whole((1, length)),
            weight_spec(weights[0][1] * groups),
            weight_spec(weights[1][1] * groups),
            weight_spec(weights[2][1] * groups),
            pl.BlockSpec((WIDE_GROUP, width), lambda g: (g, 0)),
        ]
        + [whole(one.shape) for one in more_in],
        out_specs=[
            whole((length, width)),
            whole((width, length)),
            whole(memory_t_shape),
            rows,
            columns,
            columns,
            rows,
            pl.BlockSpec((6, length, length), lambda g: (g, 0, 0)),
        ]
        + [whole(one.shape) for one in more_out],
        out_shape=[
            shape((length, width), WIDE),
            shape((width, length), LOW),
            shape(memory_t_shape, LOW),
            shape((width, length), LOW),
            shape((length, width), LOW),
            shape((length, width), LOW),
            shape((width, length), LOW),
            shape((H, length, length), LOW),
            *more_out,
        ],
        scratch_shapes=[
            pltpu.VMEM((length, width), LOW),
            pltpu.VMEM((length, width) if cross else (16, 128), LOW),
            pltpu.VMEM((length, length), WIDE),
            *more_scratch,
        ],
        compiler_params=pltpu.CompilerParams(
            vmem_limit_bytes=VMEM_LIMIT,
            **(dict(collective_id=1, has_side_effects=True) if remote else {}),
        ),
        cost_estimate=pl.CostEstimate(
            flops=2 * length * width * (4 * width + 2 * length),
            bytes_accessed=2 * (4 * width * width + H * length * length + 8 * length * width),
            transcendentals=H * length * length,
        ),
        name="attention_forward",
    )(x, gains, memory, gains, seg_q, seg_k,
      weights[0][0], weights[1][0], weights[2][0], w_out, *more_in)
    hidden, x_t, memory_t, q_t, keys, values, mixed_t, probs = outs[:8]
    stored = Attended(x_t, memory_t if cross else None, q_t, keys, values, mixed_t, probs)
    return (hidden, stored) + tuple(outs[8:])


def layer_parts(values):
    centred = values - jnp.mean(values, axis=-1, keepdims=True)
    scale = lax.rsqrt(jnp.mean(centred * centred, axis=-1, keepdims=True) + 1e-05)
    return centred * scale, scale


def feed_forward_kernel(
    up_scale, layer, gain_row,
    x_ref, gain_ref, up_ref, down_ref, adapter_ref, vector_ref,
    out_ref, ffn_ref, x_t_ref, active_t_ref, slope_ref,
    x_low, total,
):
    step = pl.program_id(0)

    @pl.when(step == 0)
    def _():
        values = x_ref[...]
        normed = (values * rms_scale(values) * row_of(gain_ref, gain_row)).astype(LOW)
        x_low[...] = normed
        x_t_ref[...] = normed.T
        total[...] = jnp.zeros_like(total)

    before = dot_nn(x_low[...], up_ref[...])
    cumulative, density = gelu_parts(before)
    active = (before * cumulative).astype(LOW)
    slope_ref[...] = (cumulative + before * density).astype(LOW)
    active_t_ref[...] = active.T
    total[...] += dot_nn(active, down_ref[...])

    @pl.when(step == pl.num_programs(0) - 1)
    def _():
        ffn = total[...]
        ffn_ref[...] = ffn
        normed, _ = layer_parts(ffn)
        vectors = vector_ref[layer].astype(WIDE)
        low = (normed * (1.0 + vectors[1:2]) + vectors[2:3]).astype(LOW)
        inner = dot_nt(low, adapter_ref[layer, 0])
        gate = (inner * gelu_parts(inner)[0]).astype(LOW)
        adapted = dot_nn(gate, adapter_ref[layer, 1]) * up_scale + vectors[0:1]
        out_ref[...] = (x_ref[...] + ffn + adapted).astype(out_ref.dtype)


def feed_forward(
    x, gains, gain_row, w_up, w_down, adapter, vectors, layer, up_scale, out_dtype, blocks=2
):
    length, width = x.shape
    inner = w_up.shape[1]
    block = inner // blocks
    shape = jax.ShapeDtypeStruct
    out, ffn, x_t, active_t, slope = pl.pallas_call(
        functools.partial(feed_forward_kernel, up_scale, layer, gain_row),
        grid=(blocks,),
        in_specs=[
            whole((length, width)),
            whole(gains.shape),
            pl.BlockSpec((width, block), lambda j: (0, j)),
            pl.BlockSpec((block, width), lambda j: (j, 0)),
            whole(adapter.shape),
            whole(vectors.shape),
        ],
        out_specs=[
            whole((length, width)),
            whole((length, width)),
            whole((width, length)),
            pl.BlockSpec((block, length), lambda j: (j, 0)),
            pl.BlockSpec((length, block), lambda j: (0, j)),
        ],
        out_shape=[
            shape((length, width), out_dtype),
            shape((length, width), WIDE),
            shape((width, length), LOW),
            shape((inner, length), LOW),
            shape((length, inner), LOW),
        ],
        scratch_shapes=[pltpu.VMEM((length, width), LOW), pltpu.VMEM((length, width), WIDE)],
        compiler_params=pltpu.CompilerParams(vmem_limit_bytes=VMEM_LIMIT),
        cost_estimate=pl.CostEstimate(
            flops=4 * length * width * inner,
            bytes_accessed=4 * width * inner + 4 * length * inner + 12 * length * width,
            transcendentals=length * inner,
        ),
        name="feed_forward",
    )(x, gains, w_up, w_down, adapter, vectors)
    return out, Fed(ffn, x_t, active_t, slope)


def join_rows(ref):
    blocks, _, rows, columns = ref.shape
    if rows % 16 == 0:
        return ref[...].reshape(blocks * rows, columns)
    parts = [ref[i, 0].astype(WIDE) for i in range(blocks)]
    return jnp.concatenate(parts, axis=0).astype(LOW)


def power_of_two(least):
    return 1 << (least - 1).bit_length()


class TransferRefs(NamedTuple):
    unit: object
    held: object
    into: object
    total: object
    line: object
    send: object
    recv: object


class Transfer:
    def __init__(self, units, small, n_dp, n_gen, rows, width, lags):
        self.units, self.small, self.n_dp, self.n_gen = units, small, n_dp, n_gen
        self.rows, self.width = rows, width
        self.bits = n_dp.bit_length() - 1
        self.final = self.bits + max(n_gen - 1, 0)
        first, between, last, along = lags
        self.lags = [first] + [between] * (self.bits - 2) + [last] + [along] * (n_gen - 1)
        self.at = [sum(self.lags[:s]) for s in range(self.final + 1)]
        self.slots = units + self.at[self.final]
        self.ring = power_of_two(2 * max(first, between, last) + 1)
        self.line_ring = power_of_two(max(2 * along + 1, along * (n_gen - 1)))
        self.unit_ring = power_of_two(first + 1)
        self.sum_ring = power_of_two(along * max(n_gen - 1, 1) + 1)

    def scratch(self):
        block = (self.rows, self.width)
        bits, lags, ring = self.bits, self.lags, self.ring
        stages = max(bits + self.n_gen - 1, 1)
        return TransferRefs(
            unit=pltpu.VMEM((self.unit_ring, self.n_dp) + block, LOW),
            held=[pltpu.VMEM((lags[s], self.n_dp >> s) + block, LOW) for s in range(1, bits)],
            into=[pltpu.VMEM((ring, self.n_dp >> (s + 1)) + block, LOW) for s in range(bits)],
            total=pltpu.VMEM((self.sum_ring,) + block, LOW),
            line=[pltpu.VMEM((self.line_ring,) + block, LOW) for _ in range(self.n_gen - 1)],
            send=pltpu.SemaphoreType.DMA((stages, max(ring, self.line_ring))),
            recv=pltpu.SemaphoreType.DMA((stages, max(ring, self.line_ring))),
        )

    def bind(self, refs):
        self.refs = refs
        self.place = lax.axis_index("dp")
        self.at_line = lax.axis_index("gen")
        self.core = self.place % 2
        self.partners = [self.partner(step) for step in range(self.bits)]
        self.positions = [self.position(index) for index in range(self.n_dp)]

    def partner(self, step):
        if step == 0:
            return self.place + 1 - 2 * self.core
        one, other = 1 << step, 1 << (self.bits - step)
        flipped = [self.place + power * (1 - 2 * ((self.place // power) % 2)) for power in (one, other)]
        return jnp.where(self.core == 0, *flipped)

    def position(self, index):
        if self.bits == 0:
            return 0
        core = index % 2
        place = jnp.where(self.core == core, 1 << (self.bits - 1), 0)
        for step in range(1, self.bits):
            power = 1 << (step if core == 0 else self.bits - step)
            differs = (self.place // power + index // power) % 2
            place = place + differs * (1 << (self.bits - 1 - step))
        return place

    def barrier(self):
        if self.bits + self.n_gen == 1:
            return
        semaphore = pltpu.get_barrier_semaphore()
        for k in range(1, self.n_dp):
            pl.semaphore_signal(
                semaphore, inc=1,
                device_id={"dp": (self.place + k) % self.n_dp, "gen": self.at_line},
                device_id_type=pl.DeviceIdType.MESH,
            )
        amount = self.n_dp - 1
        if self.n_gen > 1:
            ends = ((self.at_line > 0, -1), (self.at_line < self.n_gen - 1, 1))
            for there, towards in ends:
                @pl.when(there)
                def _():
                    pl.semaphore_signal(
                        semaphore, inc=1,
                        device_id={"dp": self.place, "gen": self.at_line + towards},
                        device_id_type=pl.DeviceIdType.MESH,
                    )
                amount = amount + jnp.where(there, 1, 0)
        pl.semaphore_wait(semaphore, amount)

    def sized(self, unit, act):
        if isinstance(unit, int):
            act(16 if unit in self.small else self.rows)
            return
        is_small = unit == self.small[0]
        for one in self.small[1:]:
            is_small = is_small | (unit == one)
        pl.when(is_small)(functools.partial(act, 16))
        pl.when(~is_small)(functools.partial(act, self.rows))

    def halving(self, step, unit, rows):
        refs, many = self.refs, self.n_dp >> (step + 1)
        if step == 0:
            source = refs.unit.at[unit % self.unit_ring, pl.ds(0, many), pl.ds(0, rows)]
        else:
            source = refs.held[step - 1].at[unit % self.lags[step], pl.ds(many, many), pl.ds(0, rows)]
        slot = unit % self.ring
        return pltpu.make_async_remote_copy(
            src_ref=source,
            dst_ref=refs.into[step].at[slot, :, pl.ds(0, rows)],
            send_sem=refs.send.at[step, slot],
            recv_sem=refs.recv.at[step, slot],
            device_id={"dp": self.partners[step], "gen": self.at_line},
            device_id_type=pl.DeviceIdType.MESH,
        )

    def along(self, i, unit, towards, rows):
        slot = unit % self.line_ring
        step = self.bits + i
        return pltpu.make_async_remote_copy(
            src_ref=self.refs.total.at[unit % self.sum_ring, pl.ds(0, rows)],
            dst_ref=self.refs.line[i].at[slot, pl.ds(0, rows)],
            send_sem=self.refs.send.at[step, slot],
            recv_sem=self.refs.recv.at[step, slot],
            device_id={"dp": self.place, "gen": self.at_line + towards},
            device_id_type=pl.DeviceIdType.MESH,
        )

    def roles(self, i):
        count = self.n_gen
        half = count // 2
        if i < half - 1:
            return [(i, 1), (count - 1 - i, -1)], [i + 1, count - 2 - i], True
        if i == half - 1:
            return [(half - 1, 1), (half, -1)], [half - 1, half], True
        j = count - 2 - i
        return [(j + 1, -1), (count - 2 - j, 1)], [j, count - 1 - j], False

    def stage(self, s, unit, out_ref):
        refs, bits = self.refs, self.bits
        if s == 0:
            if bits:
                self.sized(unit, lambda rows: self.halving(0, unit, rows).start())
            return
        if s <= bits:
            self.sized(unit, lambda rows: self.halving(s - 1, unit, rows).wait())
            received = refs.into[s - 1].at[unit % self.ring]
            many = self.n_dp >> s
            if s == 1:
                kept = refs.unit.at[unit % self.unit_ring, pl.ds(many, many)]
            else:
                kept = refs.held[s - 2].at[unit % self.lags[s - 1], pl.ds(0, many)]
            if s < bits:
                refs.held[s - 1][unit % self.lags[s]] = kept[...] + received[...]
                self.sized(unit, lambda rows: self.halving(s, unit, rows).start())
                return
            refs.total[unit % self.sum_ring] = kept[0] + received[0]
        i = s - bits
        total = refs.total.at[unit % self.sum_ring]
        if i > 0:
            senders, receivers, adds = self.roles(i - 1)
            for sender, towards in senders:
                @pl.when(self.at_line == sender)
                def _():
                    self.sized(
                        unit, lambda rows: self.along(i - 1, unit, towards, rows).wait_send()
                    )

            @pl.when((self.at_line == receivers[0]) | (self.at_line == receivers[1]))
            def _():
                back = jnp.where(self.at_line == 0, 1, -1)
                self.sized(unit, lambda rows: self.along(i - 1, unit, back, rows).wait_recv())
                incoming = refs.line[i - 1].at[unit % self.line_ring]
                if adds:
                    total[...] = total[...] + incoming[...]
                else:
                    total[...] = incoming[...]
        if i < self.n_gen - 1:
            senders, _, _ = self.roles(i)
            for sender, towards in senders:
                @pl.when(self.at_line == sender)
                def _():
                    self.sized(unit, lambda rows: self.along(i, unit, towards, rows).start())
        else:
            out_ref[unit] = total[...]

    def put(self, unit, values, start=0):
        target = self.refs.unit.at[unit % self.unit_ring]
        stop = start + values.shape[1]
        for i in range(self.n_dp):
            part = values[i * self.rows : (i + 1) * self.rows].astype(LOW)
            target[self.positions[i], :, start:stop] = part

    def send(self, unit, out_ref):
        if self.bits + self.n_gen == 1:
            out_ref[unit] = self.refs.unit[unit % self.unit_ring, 0]
            return
        self.slot(unit, out_ref)
        self.stage(0, unit, out_ref)

    def drain(self, out_ref):
        def one(t, carried):
            self.slot(t, out_ref)
            return carried

        if self.bits + self.n_gen > 1:
            lax.fori_loop(self.units, self.slots, one, 0)

    def slot(self, t, out_ref):
        for s in reversed(range(1, self.final + 1)):
            unit = t - self.at[s]

            @pl.when((unit >= 0) & (unit < self.units))
            def _():
                self.stage(s, unit, out_ref)


class Shared:
    def __init__(self, plan, refs):
        self.plan, (self.own, self.all, self.sends, self.recvs) = plan, refs

    @staticmethod
    def scratch(n_dp, rows, features):
        many = max(n_dp - 1, 1)
        return (
            pltpu.VMEM((rows, features), LOW),
            pltpu.VMEM((n_dp, rows, features), LOW),
            pltpu.SemaphoreType.DMA((many,)),
            pltpu.SemaphoreType.DMA((many,)),
        )

    def copy(self, k):
        plan = self.plan
        return pltpu.make_async_remote_copy(
            src_ref=self.own,
            dst_ref=self.all.at[plan.place],
            send_sem=self.sends.at[k - 1],
            recv_sem=self.recvs.at[k - 1],
            device_id={"dp": (plan.place + k) % plan.n_dp, "gen": plan.at_line},
            device_id_type=pl.DeviceIdType.MESH,
        )

    def start(self, weights, vectors):
        plan = self.plan
        features = self.own.shape[1]
        rows, more = weights.shape[0], vectors.shape[0]
        for j in range(plan.n_gen):
            @pl.when(plan.at_line == j)
            def _():
                columns = slice(j * features, (j + 1) * features)
                self.own[:rows] = weights[:, columns]
                self.own[rows : rows + more] = vectors[:, columns]
        for k in range(1, plan.n_dp):
            self.copy(k).start()
        self.all[plan.place] = self.own[...]

    def finish(self, weights_ref, vectors_ref):
        for k in range(1, self.plan.n_dp):
            self.copy(k).wait()
        rows = self.plan.rows
        weights_ref[...] = self.all[:, :rows]
        vectors_ref[...] = self.all[:, rows:]


def gen_barrier(line, n_gen):
    semaphore = pltpu.get_barrier_semaphore()
    for k in range(1, n_gen):
        pl.semaphore_signal(
            semaphore, inc=1, device_id={"gen": (line + k) % n_gen},
            device_id_type=pl.DeviceIdType.MESH,
        )
    pl.semaphore_wait(semaphore, n_gen - 1)


def gen_copy(source, target, sends, recvs, line, k, n_gen):
    return pltpu.make_async_remote_copy(
        src_ref=source,
        dst_ref=target.at[line],
        send_sem=sends.at[k - 1],
        recv_sem=recvs.at[k - 1],
        device_id={"gen": (line + k) % n_gen},
        device_id_type=pl.DeviceIdType.MESH,
    )


def sum_gen_kernel(n_gen, part_ref, out_ref, parts, sends, recvs):
    line = lax.axis_index("gen")
    gen_barrier(line, n_gen)
    for k in range(1, n_gen):
        gen_copy(part_ref, parts, sends, recvs, line, k, n_gen).start()
    parts[line] = part_ref[...]
    for k in range(1, n_gen):
        gen_copy(part_ref, parts, sends, recvs, line, k, n_gen).wait()
    total = parts[0]
    for j in range(1, n_gen):
        total = total + parts[j]
    out_ref[...] = total


def sum_gen(part):
    n_gen = lax.axis_size("gen")
    if n_gen == 1:
        return part
    return pl.pallas_call(
        functools.partial(sum_gen_kernel, n_gen),
        in_specs=[pl.BlockSpec(memory_space=pltpu.VMEM)],
        out_specs=pl.BlockSpec(memory_space=pltpu.VMEM),
        out_shape=jax.ShapeDtypeStruct(part.shape, part.dtype),
        scratch_shapes=[
            pltpu.VMEM((n_gen,) + part.shape, part.dtype),
            pltpu.SemaphoreType.DMA((n_gen - 1,)),
            pltpu.SemaphoreType.DMA((n_gen - 1,)),
        ],
        compiler_params=pltpu.CompilerParams(collective_id=2, has_side_effects=True),
        name="sum_gen",
    )(part)


class Operands(NamedTuple):
    cotangent: object
    cross_hidden: object
    dec_hidden: object
    encoded: object
    enc_hidden: object
    dec_rows: object
    enc_rows: object
    enc_qkv: object
    enc_proj: object
    enc_up: object
    enc_down: object
    dec_qkv: object
    dec_self_proj: object
    dec_cross_q: object
    dec_cross_kv: object
    dec_cross_proj: object
    dec_up: object
    dec_down: object
    enc_attn: Attended
    dec_attn: Attended
    cross_attn: Attended
    enc_ffn: Fed
    dec_ffn: Fed
    small: object


class Small(NamedTuple):
    enc_norms: object
    dec_norms: object
    adapters: object
    vectors: object
    wanted: object


class Results(NamedTuple):
    sums: object
    pair_weights: object
    pair_vectors: object
    grad_dec_rows: object
    grad_enc_rows: object


class Held(NamedTuple):
    total: object
    total_memory: object
    grad_low: object
    grad_a: object
    grad_b: object
    adapters: object
    vectors: object
    gains: object
    transfer: TransferRefs
    shared: object


class Backward:
    def __init__(self, plan, up_scale, bottleneck, tasks, refs, small, scratch, out_ref):
        self.plan, self.up_scale, self.bottleneck, self.tasks = plan, up_scale, bottleneck, tasks
        self.refs, self.small, self.scratch, self.out_ref = refs, small, scratch, out_ref

    def send(self, unit):
        self.plan.send(unit, self.out_ref)

    def attention(
        self, first_unit, grad_ref, gain_rows, x, memory, stored, weights, finish, after_first=None
    ):
        cross = memory is not None
        plan, scratch = self.plan, self.scratch
        total_x, total_memory, grad_low = scratch.total, scratch.total_memory, scratch.grad_low
        length, width = x.shape
        groups = width // GROUP
        columns = pl.BlockSpec((length, GROUP), lambda g: (0, g))
        rows = pl.BlockSpec((GROUP, length), lambda g: (g, 0))

        def weight_spec(offset):
            return pl.BlockSpec((width, GROUP), lambda g: (0, offset + g))

        def body(
            x_ref, x_t_ref, q_t_ref, k_ref, v_ref, mixed_t_ref, probs_ref,
            wq_ref, wk_ref, wv_ref, wo_ref, *more,
        ):
            memory_ref, memory_t_ref = more if cross else (x_ref, x_t_ref)
            step = pl.program_id(0)

            @pl.when(step == 0)
            def _():
                grad_low[...] = grad_ref[...].astype(LOW)
                total_x[...] = jnp.zeros_like(total_x)
                if cross:
                    total_memory[...] = jnp.zeros_like(total_memory)
                plan.put(first_unit, dot_nn(mixed_t_ref[...], grad_low[...]))
                self.send(first_unit)
                if after_first is not None:
                    after_first()

            grad_mixed = dot_nt(grad_low[...], wo_ref[...]).astype(LOW)
            grad_mixed_t = grad_mixed.T
            lanes = first_half((length, 2 * HD))
            heads = range(4)

            def pair_of(ref, head):
                pair = head // 2
                return ref[:, pair * 2 * HD : (pair + 1) * 2 * HD]

            def rows_of(ref, head):
                return ref[head * HD : (head + 1) * HD, :]

            grad_probs = []
            for head in heads:
                mine = jnp.where(
                    lanes if head % 2 == 0 else ~lanes, pair_of(grad_mixed, head), LOW(0)
                )
                grad_probs.append(dot_nt(mine, pair_of(v_ref, head)))
            probs = probs_ref[...].astype(WIDE)
            product = probs * jnp.stack(grad_probs)
            grad_scores = (
                product - probs * jnp.sum(product, axis=-1, keepdims=True)
            ).astype(LOW)
            halves = [dot_nn(grad_scores[head], pair_of(k_ref, head)) for head in heads]
            grad_q = [
                jnp.where(lanes, halves[head], halves[head + 1]) * HD ** (-0.5)
                for head in heads[::2]
            ]
            grad_k = [
                dot_nn(rows_of(q_t_ref, head), grad_scores[head]) * HD ** (-0.5) for head in heads
            ]
            grad_v = [dot_nn(rows_of(grad_mixed_t, head), probs_ref[head]) for head in heads]
            low_q = jnp.concatenate(grad_q, axis=1).astype(LOW)
            low_k = jnp.concatenate(grad_k, axis=0).astype(LOW).T
            low_v = jnp.concatenate(grad_v, axis=0).astype(LOW).T
            unit = first_unit + 1 + step
            plan.put(unit, dot_nn(x_t_ref[...], low_q), 0)
            plan.put(unit, dot_nn(memory_t_ref[...], low_k), GROUP)
            plan.put(unit, dot_nn(memory_t_ref[...], low_v), 2 * GROUP)
            self.send(unit)
            total_x[...] += dot_nt(low_q, wq_ref[...])
            total_source = total_memory if cross else total_x
            total_source[...] += dot_nt(low_k, wk_ref[...]) + dot_nt(low_v, wv_ref[...])

            @pl.when(step == groups - 1)
            def _():
                x_gain, memory_gain = gain_rows
                grad_values, grad_gain = rms_backward(
                    x_ref[...].astype(WIDE), self.gain(x_gain), total_x[...]
                )
                scratch.gains[x_gain : x_gain + 1] = grad_gain
                finish(grad_ref[...] + grad_values)
                if cross:
                    grad_values, grad_gain = rms_backward(
                        memory_ref[...], self.gain(memory_gain), total_memory[...]
                    )
                    scratch.gains[memory_gain : memory_gain + 1] = grad_gain
                    scratch.grad_b[...] = grad_values

        whole_tokens, whole_turned = whole((length, width)), whole((width, length))
        pltpu.emit_pipeline(
            body,
            grid=(groups,),
            in_specs=[
                whole_tokens, whole_turned, rows, columns, columns, whole_turned,
                pl.BlockSpec((4, length, length), lambda g: (g, 0, 0)),
                weight_spec(weights[0][1] * groups),
                weight_spec(weights[1][1] * groups),
                weight_spec(weights[2][1] * groups),
                pl.BlockSpec((GROUP, width), lambda g: (g, 0)),
            ]
            + ([whole_tokens, whole_turned] if cross else []),
        )(
            x, stored.x_t, stored.q_t, stored.keys, stored.values, stored.mixed_t, stored.probs,
            weights[0][0], weights[1][0], weights[2][0], weights[3],
            *([memory, stored.memory_t] if cross else []),
        )

    def gain(self, row):
        small = self.small
        return row_of(small.enc_norms, row) if row < 2 else row_of(small.dec_norms, row - 2)

    def feed_forward(
        self, first_unit, grad, x, gain_row, layer, w_up, w_down, stored, finish, after_adapter=None
    ):
        plan, small, scratch, up_scale = self.plan, self.small, self.scratch, self.up_scale
        total, grad_low = scratch.total, scratch.grad_low
        length, width = x.shape
        n_dp, blocks, rows, _ = stored.active_t.shape

        def body(x_ref, ffn_ref, x_t_ref, up_ref, down_ref, active_t_ref, slope_ref, *more):
            grad_ref = more[0] if more else scratch.grad_b
            step = pl.program_id(0)

            @pl.when(step == 0)
            def _():
                grad = grad_ref[...].astype(WIDE)
                vectors = small.vectors[layer].astype(WIDE)
                lower, upper = small.adapters[layer, 0], small.adapters[layer, 1]
                normed, scale = layer_parts(ffn_ref[...])
                gain = 1.0 + vectors[1:2]
                low = (normed * gain + vectors[2:3]).astype(LOW)
                inner = dot_nt(low, lower)
                cumulative, density = gelu_parts(inner)
                gate = (inner * cumulative).astype(LOW)
                scaled = (grad * up_scale).astype(LOW)
                scratch.adapters[layer, 1] = dot_nn(gate.T, scaled)
                grad_gate = dot_nt(scaled, upper)
                grad_inner = (grad_gate * (cumulative + inner * density)).astype(LOW)
                scratch.adapters[layer, 0] = dot_nn(grad_inner.T, low)
                grad_normed = dot_nn(grad_inner, lower)
                keep = scratch.vectors
                keep[3 * layer : 3 * layer + 1] = jnp.sum(grad, axis=0, keepdims=True)
                keep[3 * layer + 1 : 3 * layer + 2] = jnp.sum(
                    grad_normed * normed, axis=0, keepdims=True
                )
                keep[3 * layer + 2 : 3 * layer + 3] = jnp.sum(grad_normed, axis=0, keepdims=True)
                pulled = grad_normed * gain
                pulled = scale * (
                    pulled
                    - jnp.mean(pulled, axis=-1, keepdims=True)
                    - normed * jnp.mean(pulled * normed, axis=-1, keepdims=True)
                )
                grad_low[...] = (grad + pulled).astype(LOW)
                total[...] = jnp.zeros_like(total)
                if after_adapter is not None:
                    after_adapter()

            unit = first_unit + 2 * step
            plan.put(unit, dot_nn(join_rows(active_t_ref), grad_low[...]))
            self.send(unit)
            grad_active = dot_nt(grad_low[...], down_ref[...])
            grad_before = (grad_active * slope_ref[...].astype(WIDE)).astype(LOW)
            plan.put(unit + 1, dot_nn(x_t_ref[...], grad_before))
            self.send(unit + 1)
            total[...] += dot_nt(grad_before, up_ref[...])

            @pl.when(step == blocks - 1)
            def _():
                grad_values, grad_gain = rms_backward(
                    x_ref[...], self.gain(gain_row), total[...]
                )
                scratch.gains[gain_row : gain_row + 1] = grad_gain
                finish(grad_ref[...].astype(WIDE) + grad_values)

        tokens = whole((length, width))
        pltpu.emit_pipeline(
            body,
            grid=(blocks,),
            in_specs=[
                tokens, tokens, whole((width, length)),
                pl.BlockSpec((width, width), lambda j: (0, j)),
                pl.BlockSpec((width, width), lambda j: (j, 0)),
                pl.BlockSpec((n_dp, 1, rows, length), lambda j: (0, j, 0, 0)),
                pl.BlockSpec((length, width), lambda j: (0, j)),
            ]
            + ([] if grad is None else [tokens]),
        )(
            x, stored.ffn, stored.x_t, w_up, w_down, stored.active_t, stored.slope,
            *([] if grad is None else [grad]),
        )

    def own_rows(self, values, rows_per_task, first, count):
        parts = []
        while count:
            task, offset = divmod(first, rows_per_task)
            some = min(count, rows_per_task - offset)
            if task < self.tasks:
                weight = self.small.wanted[0:1, 2 * task : 2 * task + 1]
                parts.append(values[offset : offset + some] * weight)
            else:
                parts.append(jnp.zeros((some, values.shape[1]), WIDE))
            first, count = first + some, count - some
        return parts[0] if len(parts) == 1 else jnp.concatenate(parts, axis=0)

    def send_adapters(self, unit):
        plan, kept, size = self.plan, self.scratch.adapters, self.bottleneck
        values = jnp.concatenate(
            [kept[layer, part, :size] for layer in range(kept.shape[0]) for part in range(2)], axis=0
        )
        target = plan.refs.unit.at[unit % plan.unit_ring]
        for i in range(plan.n_dp):
            part = self.own_rows(values, values.shape[0], i * plan.rows, plan.rows)
            target[plan.positions[i]] = part.astype(LOW)
        self.send(unit)

    def send_vectors(self, unit, vector_rows):
        plan = self.plan
        values = self.scratch.vectors[:6]
        spare = -vector_rows % 16
        for i in range(plan.n_dp):
            part = self.own_rows(values, 6, i * vector_rows, vector_rows)
            if spare:
                part = jnp.concatenate([part, jnp.zeros((spare, plan.width), WIDE)], axis=0)
            target = plan.refs.unit.at[unit % plan.unit_ring, plan.positions[i]]
            target[: part.shape[0]] = part.astype(LOW)
        self.send(unit)

    def send_gains(self, unit):
        plan = self.plan
        rows, width = plan.rows, plan.width
        for i in range(plan.n_dp):
            part = self.scratch.gains[:6, i * rows : (i + 1) * rows]
            if rows < width:
                part = jnp.concatenate([part, jnp.zeros((6, width - rows), WIDE)], axis=1)
            part = jnp.concatenate([part, jnp.zeros((10, width), WIDE)], axis=0)
            target = plan.refs.unit.at[unit % plan.unit_ring, plan.positions[i]]
            target[0:16] = part.astype(LOW)
        self.send(unit)


def backward_kernel(plan, up_scale, bottleneck, tasks, vector_rows, trees, *leaves):
    counts = [tree.num_leaves for tree in trees]
    parts, start = [], 0
    for tree, count in zip(trees, counts):
        parts.append(jax.tree.unflatten(tree, leaves[start : start + count]))
        start += count
    refs, out, scratch = parts
    plan.bind(scratch.transfer)
    plan.barrier()
    work = Backward(plan, up_scale, bottleneck, tasks, refs, refs.small, scratch, out.sums)
    shared = Shared(plan, scratch.shared)
    grad_a, grad_b = scratch.grad_a, scratch.grad_b

    def into(ref):
        def finish(values):
            ref[...] = values.astype(ref.dtype)

        return finish

    def adapters():
        work.send_adapters(12)
        work.send_vectors(13, vector_rows)

    def share():
        shared.start(out.sums.at[12], out.sums.at[13, pl.ds(0, 16)])

    early = 13 + plan.at[plan.final] <= 26
    work.feed_forward(
        0, refs.cotangent, refs.cross_hidden, 4, 1, refs.dec_up, refs.dec_down, refs.dec_ffn,
        into(grad_a),
    )
    work.attention(
        8, grad_a, (3, 5), refs.dec_hidden, refs.encoded, refs.cross_attn,
        ((refs.dec_cross_q, 0), (refs.dec_cross_kv, 0), (refs.dec_cross_kv, 1), refs.dec_cross_proj),
        into(grad_a),
    )
    work.feed_forward(
        14, None, refs.enc_hidden, 1, 0, refs.enc_up, refs.enc_down, refs.enc_ffn, into(grad_b),
        after_adapter=adapters,
    )
    work.attention(
        22, grad_a, (2, None), refs.dec_rows, None, refs.dec_attn,
        ((refs.dec_qkv, 0), (refs.dec_qkv, 1), (refs.dec_qkv, 2), refs.dec_self_proj),
        into(out.grad_dec_rows),
    )
    work.attention(
        26, grad_b, (0, None), refs.enc_rows, None, refs.enc_attn,
        ((refs.enc_qkv, 0), (refs.enc_qkv, 1), (refs.enc_qkv, 2), refs.enc_proj),
        into(out.grad_enc_rows), after_first=share if early else None,
    )
    work.send_gains(30)
    plan.drain(out.sums)
    if not early:
        share()
    shared.finish(out.pair_weights, out.pair_vectors)


def backward(operands, features, up_scale, bottleneck, tasks, vector_rows):
    n_dp, n_gen = lax.axis_size("dp"), lax.axis_size("gen")
    length, width = operands.enc_rows.shape
    rows = width // n_dp
    plan = Transfer(31, (13, 30), n_dp, n_gen, rows, width, LAGS)

    def blocked(fed):
        return fed._replace(active_t=fed.active_t.reshape(n_dp, -1, rows, length))

    operands = operands._replace(
        enc_ffn=blocked(operands.enc_ffn), dec_ffn=blocked(operands.dec_ffn)
    )
    tokens = pltpu.VMEM((length, width), WIDE)
    shared_rows = rows + 16
    held = Held(
        total=tokens,
        total_memory=tokens,
        grad_low=pltpu.VMEM((length, width), LOW),
        grad_a=tokens,
        grad_b=tokens,
        adapters=pltpu.VMEM(operands.small.adapters.shape, WIDE),
        vectors=pltpu.VMEM((8, width), WIDE),
        gains=pltpu.VMEM((8, width), WIDE),
        transfer=plan.scratch(),
        shared=Shared.scratch(n_dp, shared_rows, features),
    )
    shape = jax.ShapeDtypeStruct
    results = Results(
        sums=shape((plan.units, rows, width), LOW),
        pair_weights=shape((n_dp, rows, features), LOW),
        pair_vectors=shape((n_dp, 16, features), LOW),
        grad_dec_rows=shape((length, width), LOW),
        grad_enc_rows=shape((length, width), LOW),
    )
    in_vmem = pl.BlockSpec(memory_space=pltpu.VMEM)
    in_hbm = pl.BlockSpec(memory_space=pl.ANY)
    specs = jax.tree.map(lambda _: in_hbm, operands)
    specs = specs._replace(small=jax.tree.map(lambda _: in_vmem, operands.small))
    flat, in_tree = jax.tree.flatten(operands)
    scratch, scratch_tree = jax.tree.flatten(held)
    out, out_tree = jax.tree.flatten(results)
    remote = n_dp * n_gen > 1
    outs = pl.pallas_call(
        functools.partial(
            backward_kernel, plan, up_scale, bottleneck, tasks, vector_rows,
            (in_tree, out_tree, scratch_tree),
        ),
        in_specs=jax.tree.leaves(specs),
        out_specs=[in_vmem] * len(out),
        out_shape=out,
        scratch_shapes=scratch,
        compiler_params=pltpu.CompilerParams(
            vmem_limit_bytes=VMEM_LIMIT,
            **(dict(collective_id=0, has_side_effects=True) if remote else {}),
        ),
        cost_estimate=pl.CostEstimate(
            flops=100 * length * width * width, bytes_accessed=160 * width * width,
            transcendentals=0,
        ),
        name="backward",
    )(*flat)
    return jax.tree.unflatten(out_tree, outs)


class Gradients(NamedTuple):
    enc_norms: object
    enc_qkv: object
    enc_proj: object
    enc_up: object
    enc_down: object
    dec_norms: object
    dec_qkv: object
    dec_self_proj: object
    dec_cross_q: object
    dec_cross_kv: object
    dec_cross_proj: object
    dec_up: object
    dec_down: object


def unpack_kernel(sums_ref, dec_ref, enc_ref, *outs):
    out = Gradients(*outs[:13])
    outs[13][...] = dec_ref[...]
    outs[14][...] = enc_ref[...]
    size = out.enc_norms.shape[1]
    gains = sums_ref[30, 0:16, :].astype(WIDE)

    @pl.when(pl.program_id(0) == 0)
    def _():
        out.enc_norms[...] = gains[0:2, :size]
        out.dec_norms[...] = gains[2:6, :size]

    def plain(target, unit):
        target[...] = sums_ref[unit].astype(WIDE)

    def joint(target, first, parts):
        for at, part in enumerate(parts):
            for g in range(3):
                start = (3 * at + g) * GROUP
                target[:, start : start + GROUP] = sums_ref[
                    first + g, :, part * GROUP : (part + 1) * GROUP
                ].astype(WIDE)

    def beside(target, first):
        width = sums_ref.shape[2]
        for j in range(target.shape[1] // width):
            target[:, j * width : (j + 1) * width] = sums_ref[first + 2 * j].astype(WIDE)

    def below(target, first):
        for j in range(target.shape[0]):
            target[j] = sums_ref[first + 2 * j].astype(WIDE)

    below(out.dec_down, 0)
    beside(out.dec_up, 1)
    plain(out.dec_cross_proj, 8)
    joint(out.dec_cross_q, 9, (0,))
    joint(out.dec_cross_kv, 9, (1, 2))
    below(out.enc_down, 14)
    beside(out.enc_up, 15)
    plain(out.dec_self_proj, 22)
    joint(out.dec_qkv, 23, (0, 1, 2))
    plain(out.enc_proj, 26)
    joint(out.enc_qkv, 27, (0, 1, 2))


def unpack(sums, grad_dec_rows, grad_enc_rows, inner):
    units, rows, width = sums.shape
    length = grad_dec_rows.shape[0]
    steps = rows // 32 if rows % 32 == 0 else 1
    block = rows // steps
    while length % (16 * steps):
        steps, block = 1, rows
    shape = jax.ShapeDtypeStruct

    def matrix(columns):
        return shape((rows, columns), WIDE), pl.BlockSpec((block, columns), lambda i: (i, 0))

    downs = inner // width
    down = (
        shape((downs, rows, width), WIDE),
        pl.BlockSpec((downs, block, width), lambda i: (0, i, 0)),
    )
    tokens = pl.BlockSpec((length // steps, width), lambda i: (i, 0))

    def norms(count):
        return shape((count, rows), WIDE), whole((count, rows))

    made = Gradients(
        enc_norms=norms(2), enc_qkv=matrix(3 * width), enc_proj=matrix(width),
        enc_up=matrix(inner), enc_down=down, dec_norms=norms(4), dec_qkv=matrix(3 * width),
        dec_self_proj=matrix(width), dec_cross_q=matrix(width), dec_cross_kv=matrix(2 * width),
        dec_cross_proj=matrix(width), dec_up=matrix(inner), dec_down=down,
    )
    outs = pl.pallas_call(
        unpack_kernel,
        grid=(steps,),
        in_specs=[pl.BlockSpec((units, block, width), lambda i: (0, i, 0)), tokens, tokens],
        out_specs=[spec for _, spec in made] + [tokens, tokens],
        out_shape=[one for one, _ in made] + [shape((length, width), LOW)] * 2,
        compiler_params=pltpu.CompilerParams(vmem_limit_bytes=VMEM_LIMIT),
        cost_estimate=pl.CostEstimate(
            flops=0, bytes_accessed=6 * units * rows * width, transcendentals=0
        ),
        name="unpack",
    )(sums, grad_dec_rows, grad_enc_rows)
    grads = Gradients(*outs[:13])
    grads = grads._replace(
        enc_down=grads.enc_down.reshape(-1, width), dec_down=grads.dec_down.reshape(-1, width)
    )
    return grads, outs[13], outs[14]


def gelu_exact(values):
    return jax.nn.gelu(values, approximate=False)


def body(
    enc_input,
    dec_input,
    enc_segments,
    dec_segments,
    task_ids,
    cotangent,
    enc_norms,
    enc_qkv,
    enc_proj,
    enc_up,
    enc_down,
    dec_norms,
    dec_qkv,
    dec_self_proj,
    dec_cross_q,
    dec_cross_kv,
    dec_cross_proj,
    dec_up,
    dec_down,
    task_emb,
    layer_emb,
    proj_task,
    gen_weight,
    gen_vector,
):
    _, length, width = enc_input.shape
    layer_count = layer_emb.shape[0]
    pair_count = task_emb.shape[0] * layer_count
    bottleneck = gen_weight.shape[1] // 2
    up_scale = (width / bottleneck) ** 0.5

    def source_of(task_table, layer_table, projection):
        mixed_in = (
            jnp.dot(task_table, projection, precision=HIGHEST)[:, None, :] + layer_table[None, :, :]
        )
        return gelu_exact(mixed_in).reshape(pair_count, -1)

    source, source_pull = jax.vjp(source_of, task_emb, layer_emb, proj_task)
    source_low = source.astype(LOW)
    pieces, more_pieces = [
        jnp.einsum("th,hkd->tkd", source_low, part, preferred_element_type=WIDE).astype(LOW)
        for part in (gen_weight, gen_vector)
    ]
    first_pair = task_ids[0] * layer_count
    wanted = jnp.arange(8)[:, None] + first_pair == jnp.arange(128)[None, :]
    wanted = wanted.astype(WIDE)

    enc_rows, dec_rows = enc_input[0], dec_input[0]
    enc_joint = [(enc_qkv, 0), (enc_qkv, 1), (enc_qkv, 2)]
    dec_joint = [(dec_qkv, 0), (dec_qkv, 1), (dec_qkv, 2)]
    cross_joint = [(dec_cross_q, 0), (dec_cross_kv, 0), (dec_cross_kv, 1)]
    enc_hidden, enc_stored, adapters, vectors = attention_forward(
        enc_rows, enc_norms, (0, 0), None, enc_segments, enc_segments, enc_joint, enc_proj, False,
        gather=(wanted, pieces, more_pieces, bottleneck),
    )
    dec_hidden, dec_stored = attention_forward(
        dec_rows, dec_norms, (0, 0), None, dec_segments, dec_segments, dec_joint, dec_self_proj, True
    )
    encoded, enc_ffn_stored = feed_forward(
        enc_hidden, enc_norms, 1, enc_up, enc_down, adapters, vectors, 0, up_scale, WIDE
    )
    cross_hidden, cross_stored = attention_forward(
        dec_hidden, dec_norms, (1, 3), encoded, dec_segments, enc_segments, cross_joint,
        dec_cross_proj, False,
    )
    decoded, dec_ffn_stored = feed_forward(
        cross_hidden, dec_norms, 2, dec_up, dec_down, adapters, vectors, 1, up_scale, LOW
    )

    n_dp = lax.axis_size("dp")
    rows = width // n_dp
    features = gen_weight.shape[2]
    vector_rows = -(-pair_count * 3 // n_dp)
    small = Small(enc_norms, dec_norms, adapters, vectors, wanted)
    operands = Operands(
        cotangent[0], cross_hidden, dec_hidden, encoded, enc_hidden, dec_rows, enc_rows,
        enc_qkv, enc_proj, enc_up, enc_down, dec_qkv, dec_self_proj, dec_cross_q, dec_cross_kv,
        dec_cross_proj, dec_up, dec_down,
        enc_stored, dec_stored, cross_stored, enc_ffn_stored, dec_ffn_stored, small,
    )
    result = backward(
        operands, features, up_scale, bottleneck, task_emb.shape[0], vector_rows
    )
    pair_weights = result.pair_weights.reshape(pair_count, 2 * bottleneck, features)
    pair_vectors = result.pair_vectors[:, :vector_rows].reshape(-1, features)
    pair_vectors = pair_vectors[: pair_count * 3].reshape(pair_count, 3, features)
    grad_gen_weight, grad_gen_vector = [
        jnp.einsum("th,tkd->hkd", source_low, part, preferred_element_type=WIDE)
        for part in (pair_weights, pair_vectors)
    ]
    part_source = sum(
        jnp.einsum("tkd,hkd->th", part, made, preferred_element_type=WIDE)
        for part, made in ((pair_weights, gen_weight), (pair_vectors, gen_vector))
    )
    grad_source = sum_gen(part_source)
    grad_task_emb, grad_layer_emb, grad_proj_task = source_pull(grad_source)

    grads, grad_dec_rows, grad_enc_rows = unpack(
        result.sums, result.grad_dec_rows, result.grad_enc_rows, enc_up.shape[1]
    )
    return (
        decoded[None],
        grad_enc_rows[None],
        grad_dec_rows[None],
        *grads,
        grad_task_emb,
        grad_layer_emb,
        grad_proj_task,
        grad_gen_weight,
        grad_gen_vector,
    )


def solution(mesh):
    in_specs = (
        P(("dp", "gen"), None, None),
        P(("dp", "gen"), None, None),
        P(("dp", "gen"), None),
        P(("dp", "gen"), None),
        P(("dp", "gen")),
        P(("dp", "gen"), None, None),
        P(),
        P(),
        P(),
        P(),
        P(),
        P(),
        P(),
        P(),
        P(),
        P(),
        P(),
        P(),
        P(),
        P(),
        P(),
        P(),
        P(None, None, "gen"),
        P(None, None, "gen"),
    )
    out_specs = (
        P(("dp", "gen"), None, None),
        P(("dp", "gen"), None, None),
        P(("dp", "gen"), None, None),
        P(None, "dp"),
        P("dp", None),
        P("dp", None),
        P("dp", None),
        P("dp", None),
        P(None, "dp"),
        P("dp", None),
        P("dp", None),
        P("dp", None),
        P("dp", None),
        P("dp", None),
        P("dp", None),
        P("dp", None),
        P(),
        P(),
        P(),
        P(None, None, "gen"),
        P(None, None, "gen"),
    )
    return jax.shard_map(body, mesh=mesh, in_specs=in_specs, out_specs=out_specs, check_vma=False)
```

```python
import functools
from typing import NamedTuple

import jax
import jax.numpy as jnp
from jax import lax
from jax.experimental import pallas as pl
from jax.experimental.pallas import tpu as pltpu
from jax.sharding import PartitionSpec as P

H = 12
HD = 64
GROUP = 4 * HD
VMEM_LIMIT = 62 * 1024 * 1024
LAGS = (2, 2, 2, 2)
HIGHEST = lax.Precision.HIGHEST
LOW = jnp.bfloat16
WIDE = jnp.float32


def dot_nn(left_side, right_side):
    return jnp.dot(left_side, right_side, preferred_element_type=WIDE)


def dot_nt(left_side, right_side):
    return lax.dot_general(
        left_side, right_side, (((1,), (1,)), ((), ())), preferred_element_type=WIDE
    )


def gelu_parts(values):
    size = jnp.abs(values)
    density = jnp.exp(values * values * -0.5) * 0.3989422804014327
    bottom = 1.0 + 0.2316419 * size
    inverse = pl.reciprocal(bottom, approx=True)
    inverse = inverse * (2.0 - bottom * inverse)
    series = 1.330274429 * inverse - 1.821255978
    series = series * inverse + 1.781477937
    series = series * inverse - 0.356563782
    series = series * inverse + 0.31938153
    tail = series * inverse * density
    return jnp.where(values < 0.0, tail, 1.0 - tail), density


def rms_scale(values):
    return lax.rsqrt(jnp.mean(values * values, axis=-1, keepdims=True) + 1e-06)


def rms_backward(values, norm_gain, grad):
    scale = rms_scale(values)
    normed = values * scale
    pulled = grad * norm_gain
    inner = jnp.mean(normed * pulled, axis=-1, keepdims=True)
    grad_values = scale * (pulled - normed * inner)
    return grad_values, jnp.sum(grad * normed, axis=0, keepdims=True)


def segment_bias(seg_query, seg_key, causal):
    length = seg_query.shape[1]
    column = jnp.broadcast_to(seg_query.astype(WIDE), (128, length)).T[:, :1]
    allowed = column == seg_key.astype(WIDE)
    if causal:
        query_place = lax.broadcasted_iota(jnp.int32, (length, length), 0)
        key_place = lax.broadcasted_iota(jnp.int32, (length, length), 1)
        allowed = allowed & (query_place >= key_place)
    return jnp.where(allowed, 0.0, -1e30)


def row_of(ref, row):
    return ref[row : row + 1].astype(WIDE)


def first_half(shape):
    return lax.broadcasted_iota(jnp.int32, shape, 1) < HD


class Attended(NamedTuple):
    x_t: object
    memory_t: object
    q_t: object
    keys: object
    values: object
    mixed_t: object
    probs: object


class Fed(NamedTuple):
    ffn: object
    x_t: object
    active_t: object
    slope: object


class Gather:
    def __init__(self, n_gen, bottleneck, refs):
        self.n_gen, self.bottleneck, self.line = n_gen, bottleneck, lax.axis_index("gen")
        (
            self.weights, self.pieces, self.more, self.adapters, self.vectors,
            self.asked, self.chosen, self.arrived, self.sems,
        ) = refs

    @staticmethod
    def scratch(n_gen, features):
        return (
            pltpu.VMEM((n_gen, 8, 128), WIDE),
            pltpu.VMEM((n_gen, 2, 64, features), LOW),
            pltpu.VMEM((n_gen, 2, 64, features), LOW),
            pltpu.SemaphoreType.DMA((4, max(n_gen - 1, 1))),
        )

    def ask(self, k):
        sems = self.sems
        return gen_copy(
            self.weights, self.asked, sems.at[0], sems.at[1], self.line, k, self.n_gen
        )

    def answer(self, k):
        sems = self.sems
        return gen_copy(
            self.chosen.at[k], self.arrived, sems.at[2], sems.at[3], self.line, k, self.n_gen
        )

    def pick(self, target, weights):
        for layer in range(2):
            start = 0
            for source in (self.pieces, self.more):
                pairs, rows, features = source.shape
                total = jnp.zeros((rows, features), WIDE)
                for pair in range(pairs):
                    weight = weights[layer : layer + 1, pair : pair + 1]
                    total = total + weight * source[pair].astype(WIDE)
                target[layer, start : start + rows] = total.astype(LOW)
                start += rows

    def begin(self, step):
        if self.n_gen > 1:
            pl.when(step == 0)(lambda: gen_greet(self.line, self.n_gen))

    def end(self, step, steps):
        n_gen, size = self.n_gen, self.bottleneck

        @pl.when(step == 0)
        def _():
            if n_gen > 1:
                gen_greeted(n_gen)
            for k in range(1, n_gen):
                self.ask(k).start()

        @pl.when(step == 1)
        def _():
            for k in range(1, n_gen):
                self.ask(k).wait()
            for k in range(1, n_gen):
                self.pick(self.chosen.at[k], self.asked[(self.line + k) % n_gen])
                self.answer(k).start()
            self.pick(self.arrived.at[self.line], self.weights[...])

        @pl.when(step == steps - 1)
        def _():
            for k in range(1, n_gen):
                self.answer(k).wait()
            rows = 2 * size + 3
            self.adapters[...] = jnp.zeros_like(self.adapters)
            for layer in range(2):
                joined = jnp.concatenate(
                    [self.arrived[j, layer, 0:rows].astype(WIDE) for j in range(n_gen)], axis=1
                ).astype(LOW)
                self.adapters[layer, 0, 0:size] = joined[0:size]
                self.adapters[layer, 1, 0:size] = joined[size : 2 * size]
                self.vectors[layer] = joined[2 * size : 2 * size + 3]


def attention_forward_kernel(
    cross, causal, gather, gain_rows,
    x_ref, gain_ref, memory_ref, memory_gain_ref, seg_q_ref, seg_k_ref,
    wq_ref, wk_ref, wv_ref, wo_ref, *refs,
):
    step = pl.program_id(0)
    more_in = refs[:3] if gather else ()
    refs = refs[len(more_in) :]
    hidden_ref, x_t_ref, memory_t_ref, q_t_ref, k_ref, v_ref, mixed_t_ref, probs_ref = refs[:8]
    more_out = refs[8:10] if gather else ()
    refs = refs[8 + len(more_out) :]
    x_low, memory_low, bias = refs[:3]
    if gather:
        work = Gather(*gather, more_in + more_out + refs[3:])
        work.begin(step)

    @pl.when(step == 0)
    def _():
        values = x_ref[...].astype(WIDE)
        hidden_ref[...] = values
        normed = (values * rms_scale(values) * row_of(gain_ref, gain_rows[0])).astype(LOW)
        x_low[...] = normed
        x_t_ref[...] = normed.T
        if cross:
            values = memory_ref[...].astype(WIDE)
            normed = (values * rms_scale(values) * row_of(memory_gain_ref, gain_rows[1])).astype(LOW)
            memory_low[...] = normed
            memory_t_ref[...] = normed.T
        bias[...] = segment_bias(seg_q_ref[...], seg_k_ref[...], causal)

    source_low = memory_low if cross else x_low
    queries = dot_nn(x_low[...], wq_ref[...]).astype(LOW)
    q_t_ref[...] = queries.T
    k_ref[...] = dot_nn(source_low[...], wk_ref[...]).astype(LOW)
    v_ref[...] = dot_nn(source_low[...], wv_ref[...]).astype(LOW)
    scaled = queries * LOW(HD ** (-0.5))
    length = scaled.shape[0]
    lanes = first_half((length, 2 * HD))
    parts = []
    for pair in range(2):
        columns = slice(pair * 2 * HD, (pair + 1) * 2 * HD)
        two = scaled[:, columns]
        keys = k_ref[:, columns]
        values = v_ref[:, columns]
        halves = []
        for side in range(2):
            mine = jnp.where(lanes if side == 0 else ~lanes, two, LOW(0))
            scores = dot_nt(mine, keys) + bias[...]
            raised = jnp.exp(scores - jnp.max(scores, axis=-1, keepdims=True))
            total = jnp.sum(raised, axis=-1, keepdims=True)
            probs = (raised * (1.0 / total)).astype(LOW)
            probs_ref[2 * pair + side] = probs
            halves.append(dot_nn(probs, values))
        parts.append(jnp.where(lanes, halves[0], halves[1]).astype(LOW))
    mixed = jnp.concatenate(parts, axis=1)
    mixed_t_ref[...] = mixed.T
    hidden_ref[...] += dot_nn(mixed, wo_ref[...])
    if gather:
        work.end(step, pl.num_programs(0))


def whole(shape):
    return pl.BlockSpec(shape, lambda *_: (0,) * len(shape))


def attention_forward(
    x, gains, gain_rows, memory, seg_q, seg_k, weights, w_out, causal, gather=None
):
    n_gen = lax.axis_size("gen")
    more_in, more_out, more_scratch, asked = (), (), (), None
    if gather is not None:
        wanted, pieces, more_pieces, bottleneck = gather
        more_in = (wanted, pieces, more_pieces)
        padded = -bottleneck % 16 + bottleneck
        more_out = (
            jax.ShapeDtypeStruct((2, 2, padded, x.shape[1]), LOW),
            jax.ShapeDtypeStruct((2, 3, x.shape[1]), LOW),
        )
        more_scratch = Gather.scratch(n_gen, pieces.shape[2])
        asked = (n_gen, bottleneck)
    remote = gather is not None and n_gen > 1
    cross = memory is not None
    length, width = x.shape
    groups = width // GROUP
    if not cross:
        memory = x
    shape = jax.ShapeDtypeStruct
    columns = pl.BlockSpec((length, GROUP), lambda g: (0, g))
    rows = pl.BlockSpec((GROUP, length), lambda g: (g, 0))

    def weight_spec(offset):
        return pl.BlockSpec((width, GROUP), lambda g: (0, offset + g))

    memory_spec = whole((length, width)) if cross else whole((16, 128))
    memory_t_shape = (width, length) if cross else (16, 128)
    outs = pl.pallas_call(
        functools.partial(attention_forward_kernel, cross, causal, asked, gain_rows),
        grid=(groups,),
        in_specs=[
            whole((length, width)),
            whole(gains.shape),
            memory_spec,
            whole(gains.shape),
            whole((1, length)),
            whole((1, length)),
            weight_spec(weights[0][1] * groups),
            weight_spec(weights[1][1] * groups),
            weight_spec(weights[2][1] * groups),
            pl.BlockSpec((GROUP, width), lambda g: (g, 0)),
        ]
        + [whole(one.shape) for one in more_in],
        out_specs=[
            whole((length, width)),
            whole((width, length)),
            whole(memory_t_shape),
            rows,
            columns,
            columns,
            rows,
            pl.BlockSpec((4, length, length), lambda g: (g, 0, 0)),
        ]
        + [whole(one.shape) for one in more_out],
        out_shape=[
            shape((length, width), WIDE),
            shape((width, length), LOW),
            shape(memory_t_shape, LOW),
            shape((width, length), LOW),
            shape((length, width), LOW),
            shape((length, width), LOW),
            shape((width, length), LOW),
            shape((H, length, length), LOW),
            *more_out,
        ],
        scratch_shapes=[
            pltpu.VMEM((length, width), LOW),
            pltpu.VMEM((length, width) if cross else (16, 128), LOW),
            pltpu.VMEM((length, length), WIDE),
            *more_scratch,
        ],
        compiler_params=pltpu.CompilerParams(
            vmem_limit_bytes=VMEM_LIMIT,
            **(dict(collective_id=1, has_side_effects=True) if remote else {}),
        ),
        cost_estimate=pl.CostEstimate(
            flops=2 * length * width * (4 * width + 2 * length),
            bytes_accessed=2 * (4 * width * width + H * length * length + 8 * length * width),
            transcendentals=H * length * length,
        ),
        name="attention_forward",
    )(x, gains, memory, gains, seg_q, seg_k,
      weights[0][0], weights[1][0], weights[2][0], w_out, *more_in)
    hidden, x_t, memory_t, q_t, keys, values, mixed_t, probs = outs[:8]
    stored = Attended(x_t, memory_t if cross else None, q_t, keys, values, mixed_t, probs)
    return (hidden, stored) + tuple(outs[8:])


def layer_parts(values):
    centred = values - jnp.mean(values, axis=-1, keepdims=True)
    scale = lax.rsqrt(jnp.mean(centred * centred, axis=-1, keepdims=True) + 1e-05)
    return centred * scale, scale


def feed_forward_kernel(
    up_scale, layer, gain_row,
    x_ref, gain_ref, up_ref, down_ref, adapter_ref, vector_ref,
    out_ref, ffn_ref, x_t_ref, active_t_ref, slope_ref,
    x_low, total,
):
    step = pl.program_id(0)

    @pl.when(step == 0)
    def _():
        values = x_ref[...]
        normed = (values * rms_scale(values) * row_of(gain_ref, gain_row)).astype(LOW)
        x_low[...] = normed
        x_t_ref[...] = normed.T
        total[...] = jnp.zeros_like(total)

    before = dot_nn(x_low[...], up_ref[...])
    cumulative, density = gelu_parts(before)
    active = (before * cumulative).astype(LOW)
    slope_ref[...] = (cumulative + before * density).astype(LOW)
    active_t_ref[...] = active.T
    total[...] += dot_nn(active, down_ref[...])

    @pl.when(step == pl.num_programs(0) - 1)
    def _():
        ffn = total[...]
        ffn_ref[...] = ffn
        normed, _ = layer_parts(ffn)
        vectors = vector_ref[layer].astype(WIDE)
        low = (normed * (1.0 + vectors[1:2]) + vectors[2:3]).astype(LOW)
        inner = dot_nt(low, adapter_ref[layer, 0])
        gate = (inner * gelu_parts(inner)[0]).astype(LOW)
        adapted = dot_nn(gate, adapter_ref[layer, 1]) * up_scale + vectors[0:1]
        out_ref[...] = (x_ref[...] + ffn + adapted).astype(out_ref.dtype)


def feed_forward(
    x, gains, gain_row, w_up, w_down, adapter, vectors, layer, up_scale, out_dtype, blocks=4
):
    length, width = x.shape
    inner = w_up.shape[1]
    block = inner // blocks
    shape = jax.ShapeDtypeStruct
    out, ffn, x_t, active_t, slope = pl.pallas_call(
        functools.partial(feed_forward_kernel, up_scale, layer, gain_row),
        grid=(blocks,),
        in_specs=[
            whole((length, width)),
            whole(gains.shape),
            pl.BlockSpec((width, block), lambda j: (0, j)),
            pl.BlockSpec((block, width), lambda j: (j, 0)),
            whole(adapter.shape),
            whole(vectors.shape),
        ],
        out_specs=[
            whole((length, width)),
            whole((length, width)),
            whole((width, length)),
            pl.BlockSpec((block, length), lambda j: (j, 0)),
            pl.BlockSpec((length, block), lambda j: (0, j)),
        ],
        out_shape=[
            shape((length, width), out_dtype),
            shape((length, width), WIDE),
            shape((width, length), LOW),
            shape((inner, length), LOW),
            shape((length, inner), LOW),
        ],
        scratch_shapes=[pltpu.VMEM((length, width), LOW), pltpu.VMEM((length, width), WIDE)],
        compiler_params=pltpu.CompilerParams(vmem_limit_bytes=VMEM_LIMIT),
        cost_estimate=pl.CostEstimate(
            flops=4 * length * width * inner,
            bytes_accessed=4 * width * inner + 4 * length * inner + 12 * length * width,
            transcendentals=length * inner,
        ),
        name="feed_forward",
    )(x, gains, w_up, w_down, adapter, vectors)
    return out, Fed(ffn, x_t, active_t, slope)


def join_rows(ref):
    blocks, _, rows, columns = ref.shape
    if rows % 16 == 0:
        return ref[...].reshape(blocks * rows, columns)
    parts = [ref[i, 0].astype(WIDE) for i in range(blocks)]
    return jnp.concatenate(parts, axis=0).astype(LOW)


def power_of_two(least):
    return 1 << (least - 1).bit_length()


class TransferRefs(NamedTuple):
    unit: object
    held: object
    into: object
    total: object
    line: object
    send: object
    recv: object


class Transfer:
    def __init__(self, units, extra, small, n_dp, n_gen, rows, width, lags):
        self.units, self.extra, self.small = units, extra, small
        self.n_dp, self.n_gen = n_dp, n_gen
        self.rows, self.width = rows, width
        self.bits = n_dp.bit_length() - 1
        self.final = self.bits + max(n_gen - 1, 0)
        first, between, last, along = lags
        self.lags = [first] + [between] * (self.bits - 2) + [last] + [along] * (n_gen - 1)
        self.at = [sum(self.lags[:s]) for s in range(self.final + 1)]
        self.slots = extra + 1 + self.at[self.final]
        self.ring = 2 * max(first, between, last) + 1
        self.line_ring = max(2 * along + 1, along * (n_gen - 1))
        self.unit_ring = power_of_two(first + 1)
        self.sum_ring = power_of_two(along * max(n_gen - 1, 1) + 1)

    def scratch(self):
        block = (self.rows, self.width)
        bits, lags, ring = self.bits, self.lags, self.ring
        stages = max(bits + self.n_gen - 1, 1)
        return TransferRefs(
            unit=pltpu.VMEM((self.unit_ring, self.n_dp) + block, LOW),
            held=[pltpu.VMEM((lags[s], self.n_dp >> s) + block, LOW) for s in range(1, bits)],
            into=[pltpu.VMEM((ring, self.n_dp >> (s + 1)) + block, LOW) for s in range(bits)],
            total=pltpu.VMEM((self.sum_ring,) + block, LOW),
            line=[pltpu.VMEM((self.line_ring,) + block, LOW) for _ in range(self.n_gen - 1)],
            send=pltpu.SemaphoreType.DMA((stages, max(ring, self.line_ring))),
            recv=pltpu.SemaphoreType.DMA((stages, max(ring, self.line_ring))),
        )

    def bind(self, refs):
        self.refs = refs
        self.place = lax.axis_index("dp")
        self.at_line = lax.axis_index("gen")
        self.core = self.place % 2
        self.partners = [self.partner(step) for step in range(self.bits)]
        self.positions = [self.position(index) for index in range(self.n_dp)]

    def partner(self, step):
        if step == 0:
            return self.place + 1 - 2 * self.core
        one, other = 1 << step, 1 << (self.bits - step)
        flipped = [self.place + power * (1 - 2 * ((self.place // power) % 2)) for power in (one, other)]
        return jnp.where(self.core == 0, *flipped)

    def position(self, index):
        if self.bits == 0:
            return 0
        core = index % 2
        place = jnp.where(self.core == core, 1 << (self.bits - 1), 0)
        for step in range(1, self.bits):
            power = 1 << (step if core == 0 else self.bits - step)
            differs = (self.place // power + index // power) % 2
            place = place + differs * (1 << (self.bits - 1 - step))
        return place

    def barrier(self):
        if self.bits + self.n_gen == 1:
            return
        semaphore = pltpu.get_barrier_semaphore()
        for k in range(1, self.n_dp):
            pl.semaphore_signal(
                semaphore, inc=1,
                device_id={"dp": (self.place + k) % self.n_dp, "gen": self.at_line},
                device_id_type=pl.DeviceIdType.MESH,
            )
        amount = self.n_dp - 1
        if self.n_gen > 1:
            ends = ((self.at_line > 0, -1), (self.at_line < self.n_gen - 1, 1))
            for there, towards in ends:
                @pl.when(there)
                def _():
                    pl.semaphore_signal(
                        semaphore, inc=1,
                        device_id={"dp": self.place, "gen": self.at_line + towards},
                        device_id_type=pl.DeviceIdType.MESH,
                    )
                amount = amount + jnp.where(there, 1, 0)
        pl.semaphore_wait(semaphore, amount)

    def sized(self, unit, act):
        if isinstance(unit, int):
            act(16 if unit in self.small else self.rows)
            return
        is_small = unit == self.small[0]
        for one in self.small[1:]:
            is_small = is_small | (unit == one)
        pl.when(is_small)(functools.partial(act, 16))
        pl.when(~is_small)(functools.partial(act, self.rows))

    def halving(self, step, unit, rows):
        refs, many = self.refs, self.n_dp >> (step + 1)
        if step == 0:
            source = refs.unit.at[unit % self.unit_ring, pl.ds(0, many), pl.ds(0, rows)]
        else:
            source = refs.held[step - 1].at[unit % self.lags[step], pl.ds(many, many), pl.ds(0, rows)]
        slot = unit % self.ring
        return pltpu.make_async_remote_copy(
            src_ref=source,
            dst_ref=refs.into[step].at[slot, :, pl.ds(0, rows)],
            send_sem=refs.send.at[step, slot],
            recv_sem=refs.recv.at[step, slot],
            device_id={"dp": self.partners[step], "gen": self.at_line},
            device_id_type=pl.DeviceIdType.MESH,
        )

    def along(self, i, unit, towards, rows):
        slot = unit % self.line_ring
        step = self.bits + i
        return pltpu.make_async_remote_copy(
            src_ref=self.refs.total.at[unit % self.sum_ring, pl.ds(0, rows)],
            dst_ref=self.refs.line[i].at[slot, pl.ds(0, rows)],
            send_sem=self.refs.send.at[step, slot],
            recv_sem=self.refs.recv.at[step, slot],
            device_id={"dp": self.place, "gen": self.at_line + towards},
            device_id_type=pl.DeviceIdType.MESH,
        )

    def roles(self, i):
        count = self.n_gen
        half = count // 2
        if i < half - 1:
            return [(i, 1), (count - 1 - i, -1)], [i + 1, count - 2 - i], True
        if i == half - 1:
            return [(half - 1, 1), (half, -1)], [half - 1, half], True
        j = count - 2 - i
        return [(j + 1, -1), (count - 2 - j, 1)], [j, count - 1 - j], False

    def stage(self, s, unit, out_ref):
        refs, bits = self.refs, self.bits
        if s == 0:
            if bits:
                self.sized(unit, lambda rows: self.halving(0, unit, rows).start())
            return
        if s <= bits:
            self.sized(unit, lambda rows: self.halving(s - 1, unit, rows).wait())
            received = refs.into[s - 1].at[unit % self.ring]
            many = self.n_dp >> s
            if s == 1:
                kept = refs.unit.at[unit % self.unit_ring, pl.ds(many, many)]
            else:
                kept = refs.held[s - 2].at[unit % self.lags[s - 1], pl.ds(0, many)]
            if s < bits:
                refs.held[s - 1][unit % self.lags[s]] = kept[...] + received[...]
                self.sized(unit, lambda rows: self.halving(s, unit, rows).start())
                return
            refs.total[unit % self.sum_ring] = kept[0] + received[0]
        i = s - bits
        total = refs.total.at[unit % self.sum_ring]
        if i > 0:
            senders, receivers, adds = self.roles(i - 1)
            for sender, towards in senders:
                @pl.when(self.at_line == sender)
                def _():
                    self.sized(
                        unit, lambda rows: self.along(i - 1, unit, towards, rows).wait_send()
                    )

            @pl.when((self.at_line == receivers[0]) | (self.at_line == receivers[1]))
            def _():
                back = jnp.where(self.at_line == 0, 1, -1)
                self.sized(unit, lambda rows: self.along(i - 1, unit, back, rows).wait_recv())
                incoming = refs.line[i - 1].at[unit % self.line_ring]
                if adds:
                    total[...] = total[...] + incoming[...]
                else:
                    total[...] = incoming[...]
        if i < self.n_gen - 1:
            senders, _, _ = self.roles(i)
            for sender, towards in senders:
                @pl.when(self.at_line == sender)
                def _():
                    self.sized(unit, lambda rows: self.along(i, unit, towards, rows).start())
        else:
            out_ref[jnp.minimum(unit, self.units)] = total[...]

    def put(self, unit, values, start=0):
        target = self.refs.unit.at[unit % self.unit_ring]
        stop = start + values.shape[1]
        for i in range(self.n_dp):
            part = values[i * self.rows : (i + 1) * self.rows].astype(LOW)
            target[self.positions[i], :, start:stop] = part

    def send(self, unit, out_ref):
        if self.bits + self.n_gen == 1:
            out_ref[unit] = self.refs.unit[unit % self.unit_ring, 0]
            return
        self.slot(unit, out_ref)
        self.stage(0, unit, out_ref)

    def drain(self, out_ref):
        def one(t, carried):
            self.slot(t, out_ref)
            return carried

        if self.bits + self.n_gen > 1:
            lax.fori_loop(self.extra + 1, self.slots, one, 0)

    def slot(self, t, out_ref):
        for s in reversed(range(1, self.final + 1)):
            unit = t - self.at[s]

            @pl.when(((unit >= 0) & (unit < self.units)) | (unit == self.extra))
            def _():
                self.stage(s, unit, out_ref)


class Shared:
    def __init__(self, plan, refs):
        self.plan, (self.own, self.all, self.sends, self.recvs) = plan, refs

    @staticmethod
    def scratch(n_dp, rows, features):
        many = max(n_dp - 1, 1)
        return (
            pltpu.VMEM((rows, features), LOW),
            pltpu.VMEM((n_dp, rows, features), LOW),
            pltpu.SemaphoreType.DMA((many,)),
            pltpu.SemaphoreType.DMA((many,)),
        )

    def copy(self, k):
        plan = self.plan
        return pltpu.make_async_remote_copy(
            src_ref=self.own,
            dst_ref=self.all.at[plan.place],
            send_sem=self.sends.at[k - 1],
            recv_sem=self.recvs.at[k - 1],
            device_id={"dp": (plan.place + k) % plan.n_dp, "gen": plan.at_line},
            device_id_type=pl.DeviceIdType.MESH,
        )

    def start(self, weights, vectors):
        plan = self.plan
        features = self.own.shape[1]
        rows, more = weights.shape[0], vectors.shape[0]
        for j in range(plan.n_gen):
            @pl.when(plan.at_line == j)
            def _():
                columns = slice(j * features, (j + 1) * features)
                self.own[:rows] = weights[:, columns]
                self.own[rows : rows + more] = vectors[:, columns]
        for k in range(1, plan.n_dp):
            self.copy(k).start()
        self.all[plan.place] = self.own[...]

    def finish(self, weights_ref, vectors_ref):
        for k in range(1, self.plan.n_dp):
            self.copy(k).wait()
        rows = self.plan.rows
        weights_ref[...] = self.all[:, :rows]
        vectors_ref[...] = self.all[:, rows:]


def gen_greet(line, n_gen):
    semaphore = pltpu.get_barrier_semaphore()
    for k in range(1, n_gen):
        pl.semaphore_signal(
            semaphore, inc=1, device_id={"gen": (line + k) % n_gen},
            device_id_type=pl.DeviceIdType.MESH,
        )


def gen_greeted(n_gen):
    pl.semaphore_wait(pltpu.get_barrier_semaphore(), n_gen - 1)


def gen_copy(source, target, sends, recvs, line, k, n_gen):
    return pltpu.make_async_remote_copy(
        src_ref=source,
        dst_ref=target.at[line],
        send_sem=sends.at[k - 1],
        recv_sem=recvs.at[k - 1],
        device_id={"gen": (line + k) % n_gen},
        device_id_type=pl.DeviceIdType.MESH,
    )


def sum_gen_kernel(n_gen, part_ref, out_ref, parts, sends, recvs):
    line = lax.axis_index("gen")
    gen_greet(line, n_gen)
    gen_greeted(n_gen)
    for k in range(1, n_gen):
        gen_copy(part_ref, parts, sends, recvs, line, k, n_gen).start()
    parts[line] = part_ref[...]
    for k in range(1, n_gen):
        gen_copy(part_ref, parts, sends, recvs, line, k, n_gen).wait()
    total = parts[0]
    for j in range(1, n_gen):
        total = total + parts[j]
    out_ref[...] = total


def sum_gen(part):
    n_gen = lax.axis_size("gen")
    if n_gen == 1:
        return part
    return pl.pallas_call(
        functools.partial(sum_gen_kernel, n_gen),
        in_specs=[pl.BlockSpec(memory_space=pltpu.VMEM)],
        out_specs=pl.BlockSpec(memory_space=pltpu.VMEM),
        out_shape=jax.ShapeDtypeStruct(part.shape, part.dtype),
        scratch_shapes=[
            pltpu.VMEM((n_gen,) + part.shape, part.dtype),
            pltpu.SemaphoreType.DMA((n_gen - 1,)),
            pltpu.SemaphoreType.DMA((n_gen - 1,)),
        ],
        compiler_params=pltpu.CompilerParams(collective_id=2, has_side_effects=True),
        name="sum_gen",
    )(part)


class Operands(NamedTuple):
    cotangent: object
    cross_hidden: object
    dec_hidden: object
    encoded: object
    enc_hidden: object
    dec_rows: object
    enc_rows: object
    enc_qkv: object
    enc_proj: object
    enc_up: object
    enc_down: object
    dec_qkv: object
    dec_self_proj: object
    dec_cross_q: object
    dec_cross_kv: object
    dec_cross_proj: object
    dec_up: object
    dec_down: object
    enc_attn: Attended
    dec_attn: Attended
    cross_attn: Attended
    enc_ffn: Fed
    dec_ffn: Fed
    small: object


class Small(NamedTuple):
    enc_norms: object
    dec_norms: object
    adapters: object
    vectors: object
    wanted: object


class Results(NamedTuple):
    sums: object
    pair_weights: object
    pair_vectors: object
    grad_dec_rows: object
    grad_enc_rows: object


class Held(NamedTuple):
    total: object
    joint_dec: object
    joint_enc: object
    grad_low: object
    grad_a: object
    grad_b: object
    adapters: object
    vectors: object
    gains: object
    transfer: TransferRefs
    shared: object


class Backward:
    def __init__(self, plan, up_scale, bottleneck, tasks, refs, small, scratch, out_ref):
        self.plan, self.up_scale, self.bottleneck, self.tasks = plan, up_scale, bottleneck, tasks
        self.refs, self.small, self.scratch, self.out_ref = refs, small, scratch, out_ref

    def send(self, unit):
        self.plan.send(unit, self.out_ref)

    def attention(
        self, first_unit, grad_ref, gain_rows, x, memory, stored, weights, finish, after_first=None
    ):
        cross = memory is not None
        plan, scratch = self.plan, self.scratch
        total_x, total_memory, grad_low = scratch.total, scratch.grad_b, scratch.grad_low
        length, width = x.shape
        groups = width // GROUP
        columns = pl.BlockSpec((length, GROUP), lambda g: (0, g))
        rows = pl.BlockSpec((GROUP, length), lambda g: (g, 0))

        def weight_spec(offset):
            return pl.BlockSpec((width, GROUP), lambda g: (0, offset + g))

        def body(x_t_ref, q_t_ref, k_ref, v_ref, mixed_t_ref, probs_ref, wo_ref, *more):
            if cross:
                x_ref, wq_ref, wk_ref, wv_ref, memory_ref, memory_t_ref = more
            else:
                memory_t_ref = x_t_ref
            step = pl.program_id(0)

            @pl.when(step == 0)
            def _():
                grad_low[...] = grad_ref[...].astype(LOW)
                if cross:
                    total_x[...] = jnp.zeros_like(total_x)
                    total_memory[...] = jnp.zeros_like(total_memory)
                plan.put(first_unit, dot_nn(mixed_t_ref[...], grad_low[...]))
                self.send(first_unit)
                if after_first is not None:
                    after_first()

            grad_mixed = dot_nt(grad_low[...], wo_ref[...]).astype(LOW)
            grad_mixed_t = grad_mixed.T
            lanes = first_half((length, 2 * HD))
            heads = range(4)

            def pair_of(ref, head):
                pair = head // 2
                return ref[:, pair * 2 * HD : (pair + 1) * 2 * HD]

            def rows_of(ref, head):
                return ref[head * HD : (head + 1) * HD, :]

            grad_probs = []
            for head in heads:
                mine = jnp.where(
                    lanes if head % 2 == 0 else ~lanes, pair_of(grad_mixed, head), LOW(0)
                )
                grad_probs.append(dot_nt(mine, pair_of(v_ref, head)))
            mixed_rows = mixed_t_ref[pl.ds(pl.multiple_of(step * GROUP, GROUP), GROUP), :]
            pulled = grad_mixed_t.astype(WIDE) * mixed_rows.astype(WIDE)
            inner = [
                jnp.sum(rows_of(pulled, head), axis=0, keepdims=True) for head in heads
            ]
            inner = jnp.concatenate(inner + inner, axis=0).T
            inner = jnp.stack([inner[:, head : head + 1] for head in heads])
            probs = probs_ref[...].astype(WIDE)
            grad_scores = (probs * (jnp.stack(grad_probs) - inner)).astype(LOW)
            halves = [dot_nn(grad_scores[head], pair_of(k_ref, head)) for head in heads]
            grad_q = [
                jnp.where(lanes, halves[head], halves[head + 1]) * HD ** (-0.5)
                for head in heads[::2]
            ]
            grad_k = [
                dot_nn(rows_of(q_t_ref, head), grad_scores[head]) * HD ** (-0.5) for head in heads
            ]
            grad_v = [dot_nn(rows_of(grad_mixed_t, head), probs_ref[head]) for head in heads]
            low_q = jnp.concatenate(grad_q, axis=1).astype(LOW)
            low_k = jnp.concatenate(grad_k, axis=0).astype(LOW).T
            low_v = jnp.concatenate(grad_v, axis=0).astype(LOW).T
            unit = first_unit + 1 + step
            plan.put(unit, dot_nn(x_t_ref[...], low_q), 0)
            plan.put(unit, dot_nn(memory_t_ref[...], low_k), GROUP)
            plan.put(unit, dot_nn(memory_t_ref[...], low_v), 2 * GROUP)
            self.send(unit)
            if not cross:
                for part, low in enumerate((low_q, low_k, low_v)):
                    finish[part * groups + step] = low
                return
            total_x[...] += dot_nt(low_q, wq_ref[...])
            total_memory[...] += dot_nt(low_k, wk_ref[...]) + dot_nt(low_v, wv_ref[...])

            @pl.when(step == groups - 1)
            def _():
                x_gain, memory_gain = gain_rows
                grad_values, grad_gain = rms_backward(
                    x_ref[...].astype(WIDE), self.gain(x_gain), total_x[...]
                )
                scratch.gains[x_gain : x_gain + 1] = grad_gain
                finish(grad_ref[...] + grad_values)
                grad_values, grad_gain = rms_backward(
                    memory_ref[...], self.gain(memory_gain), total_memory[...]
                )
                scratch.gains[memory_gain : memory_gain + 1] = grad_gain
                scratch.grad_b[...] = grad_values

        whole_tokens, whole_turned = whole((length, width)), whole((width, length))
        pltpu.emit_pipeline(
            body,
            grid=(groups,),
            in_specs=[
                whole_turned, rows, columns, columns, whole_turned,
                pl.BlockSpec((4, length, length), lambda g: (g, 0, 0)),
                pl.BlockSpec((GROUP, width), lambda g: (g, 0)),
            ]
            + (
                [whole_tokens]
                + [weight_spec(offset * groups) for _, offset in weights[:3]]
                + [whole_tokens, whole_turned]
                if cross
                else []
            ),
        )(
            stored.x_t, stored.q_t, stored.keys, stored.values, stored.mixed_t, stored.probs,
            weights[3],
            *(
                [x] + [array for array, _ in weights[:3]] + [memory, stored.memory_t]
                if cross
                else []
            ),
        )

    def input_grad(self, first_slot, joint, grad_ref, gain_row, x, w_joint, target):
        scratch, total = self.scratch, self.scratch.total
        length, width = x.shape
        groups = width // GROUP

        def body(x_ref, wq_ref, wk_ref, wv_ref):
            step = pl.program_id(0)
            self.plan.slot(first_slot + step, self.out_ref)
            result = sum(
                dot_nt(joint[part * groups + step], weight[...])
                for part, weight in enumerate((wq_ref, wk_ref, wv_ref))
            )
            total[...] = jnp.where(step == 0, 0.0, total[...]) + result

            @pl.when(step == groups - 1)
            def _():
                grad_values, grad_gain = rms_backward(
                    x_ref[...].astype(WIDE), self.gain(gain_row), total[...]
                )
                scratch.gains[gain_row : gain_row + 1] = grad_gain
                target[...] = (grad_ref[...] + grad_values).astype(target.dtype)

        def weight_spec(part):
            return pl.BlockSpec((width, GROUP), lambda g: (0, part * groups + g))

        pltpu.emit_pipeline(
            body,
            grid=(groups,),
            in_specs=[whole((length, width))] + [weight_spec(part) for part in range(3)],
        )(x, w_joint, w_joint, w_joint)

    def gain(self, row):
        small = self.small
        return row_of(small.enc_norms, row) if row < 2 else row_of(small.dec_norms, row - 2)

    def feed_forward(
        self, first_unit, grad, x, gain_row, layer, w_up, w_down, stored, finish, after_adapter=None
    ):
        plan, small, scratch, up_scale = self.plan, self.small, self.scratch, self.up_scale
        total, grad_low = scratch.total, scratch.grad_low
        length, width = x.shape
        n_dp, blocks, rows, _ = stored.active_t.shape

        def body(x_ref, ffn_ref, x_t_ref, up_ref, down_ref, active_t_ref, slope_ref, *more):
            grad_ref = more[0] if more else scratch.grad_b
            step = pl.program_id(0)

            @pl.when(step == 0)
            def _():
                grad = grad_ref[...].astype(WIDE)
                vectors = small.vectors[layer].astype(WIDE)
                lower, upper = small.adapters[layer, 0], small.adapters[layer, 1]
                normed, scale = layer_parts(ffn_ref[...])
                gain = 1.0 + vectors[1:2]
                low = (normed * gain + vectors[2:3]).astype(LOW)
                inner = dot_nt(low, lower)
                cumulative, density = gelu_parts(inner)
                gate = (inner * cumulative).astype(LOW)
                scaled = (grad * up_scale).astype(LOW)
                scratch.adapters[layer, 1] = dot_nn(gate.T, scaled)
                grad_gate = dot_nt(scaled, upper)
                grad_inner = (grad_gate * (cumulative + inner * density)).astype(LOW)
                scratch.adapters[layer, 0] = dot_nn(grad_inner.T, low)
                grad_normed = dot_nn(grad_inner, lower)
                keep = scratch.vectors
                keep[3 * layer : 3 * layer + 1] = jnp.sum(grad, axis=0, keepdims=True)
                keep[3 * layer + 1 : 3 * layer + 2] = jnp.sum(
                    grad_normed * normed, axis=0, keepdims=True
                )
                keep[3 * layer + 2 : 3 * layer + 3] = jnp.sum(grad_normed, axis=0, keepdims=True)
                pulled = grad_normed * gain
                pulled = scale * (
                    pulled
                    - jnp.mean(pulled, axis=-1, keepdims=True)
                    - normed * jnp.mean(pulled * normed, axis=-1, keepdims=True)
                )
                grad_low[...] = (grad + pulled).astype(LOW)
                total[...] = jnp.zeros_like(total)
                if after_adapter is not None:
                    after_adapter()

            unit = first_unit + 2 * step
            plan.put(unit, dot_nn(join_rows(active_t_ref), grad_low[...]))
            self.send(unit)
            grad_active = dot_nt(grad_low[...], down_ref[...])
            grad_before = (grad_active * slope_ref[...].astype(WIDE)).astype(LOW)
            plan.put(unit + 1, dot_nn(x_t_ref[...], grad_before))
            self.send(unit + 1)
            total[...] += dot_nt(grad_before, up_ref[...])

            @pl.when(step == blocks - 1)
            def _():
                grad_values, grad_gain = rms_backward(
                    x_ref[...], self.gain(gain_row), total[...]
                )
                scratch.gains[gain_row : gain_row + 1] = grad_gain
                finish(grad_ref[...].astype(WIDE) + grad_values)

        tokens = whole((length, width))
        pltpu.emit_pipeline(
            body,
            grid=(blocks,),
            in_specs=[
                tokens, tokens, whole((width, length)),
                pl.BlockSpec((width, width), lambda j: (0, j)),
                pl.BlockSpec((width, width), lambda j: (j, 0)),
                pl.BlockSpec((n_dp, 1, rows, length), lambda j: (0, j, 0, 0)),
                pl.BlockSpec((length, width), lambda j: (0, j)),
            ]
            + ([] if grad is None else [tokens]),
        )(
            x, stored.ffn, stored.x_t, w_up, w_down, stored.active_t, stored.slope,
            *([] if grad is None else [grad]),
        )

    def own_rows(self, values, rows_per_task, first, count):
        parts = []
        while count:
            task, offset = divmod(first, rows_per_task)
            some = min(count, rows_per_task - offset)
            if task < self.tasks:
                weight = self.small.wanted[0:1, 2 * task : 2 * task + 1]
                parts.append(values[offset : offset + some] * weight)
            else:
                parts.append(jnp.zeros((some, values.shape[1]), WIDE))
            first, count = first + some, count - some
        return parts[0] if len(parts) == 1 else jnp.concatenate(parts, axis=0)

    def send_adapters(self, unit):
        plan, kept, size = self.plan, self.scratch.adapters, self.bottleneck
        values = jnp.concatenate(
            [kept[layer, part, :size] for layer in range(kept.shape[0]) for part in range(2)], axis=0
        )
        target = plan.refs.unit.at[unit % plan.unit_ring]
        for i in range(plan.n_dp):
            part = self.own_rows(values, values.shape[0], i * plan.rows, plan.rows)
            target[plan.positions[i]] = part.astype(LOW)
        self.send(unit)

    def send_vectors(self, unit, vector_rows):
        plan = self.plan
        values = self.scratch.vectors[:6]
        spare = -vector_rows % 16
        for i in range(plan.n_dp):
            part = self.own_rows(values, 6, i * vector_rows, vector_rows)
            if spare:
                part = jnp.concatenate([part, jnp.zeros((spare, plan.width), WIDE)], axis=0)
            target = plan.refs.unit.at[unit % plan.unit_ring, plan.positions[i]]
            target[: part.shape[0]] = part.astype(LOW)
        self.send(unit)

    def send_gains(self, unit):
        plan = self.plan
        rows, width = plan.rows, plan.width
        for i in range(plan.n_dp):
            part = self.scratch.gains[:6, i * rows : (i + 1) * rows]
            if rows < width:
                part = jnp.concatenate([part, jnp.zeros((6, width - rows), WIDE)], axis=1)
            part = jnp.concatenate([part, jnp.zeros((10, width), WIDE)], axis=0)
            target = plan.refs.unit.at[unit % plan.unit_ring, plan.positions[i]]
            target[0:16] = part.astype(LOW)
        self.send(unit)


def backward_kernel(plan, up_scale, bottleneck, tasks, vector_rows, trees, *leaves):
    counts = [tree.num_leaves for tree in trees]
    parts, start = [], 0
    for tree, count in zip(trees, counts):
        parts.append(jax.tree.unflatten(tree, leaves[start : start + count]))
        start += count
    refs, out, scratch = parts
    plan.bind(scratch.transfer)
    plan.barrier()
    work = Backward(plan, up_scale, bottleneck, tasks, refs, refs.small, scratch, out.sums)
    shared = Shared(plan, scratch.shared)
    grad_a, grad_b = scratch.grad_a, scratch.grad_b

    def into(ref):
        def finish(values):
            ref[...] = values.astype(ref.dtype)

        return finish

    def adapters():
        work.send_adapters(12)
        work.send_vectors(13, vector_rows)

    def share():
        shared.start(out.sums.at[12], out.sums.at[13, pl.ds(0, 16)])

    early = 13 + plan.at[plan.final] <= 26
    work.feed_forward(
        0, refs.cotangent, refs.cross_hidden, 4, 1, refs.dec_up, refs.dec_down, refs.dec_ffn,
        into(grad_a),
    )
    work.attention(
        8, grad_a, (3, 5), refs.dec_hidden, refs.encoded, refs.cross_attn,
        ((refs.dec_cross_q, 0), (refs.dec_cross_kv, 0), (refs.dec_cross_kv, 1), refs.dec_cross_proj),
        into(grad_a),
    )
    work.feed_forward(
        14, None, refs.enc_hidden, 1, 0, refs.enc_up, refs.enc_down, refs.enc_ffn, into(grad_b),
        after_adapter=adapters,
    )
    work.attention(
        22, grad_a, None, refs.dec_rows, None, refs.dec_attn, (None, None, None, refs.dec_self_proj),
        scratch.joint_dec,
    )
    work.attention(
        26, grad_b, None, refs.enc_rows, None, refs.enc_attn, (None, None, None, refs.enc_proj),
        scratch.joint_enc, after_first=share if early else None,
    )
    work.input_grad(
        30, scratch.joint_dec, grad_a, 2, refs.dec_rows, refs.dec_qkv, out.grad_dec_rows
    )
    work.input_grad(
        33, scratch.joint_enc, grad_b, 0, refs.enc_rows, refs.enc_qkv, out.grad_enc_rows
    )
    work.send_gains(plan.extra)
    plan.drain(out.sums)
    if not early:
        share()
    shared.finish(out.pair_weights, out.pair_vectors)


def backward(operands, features, up_scale, bottleneck, tasks, vector_rows):
    n_dp, n_gen = lax.axis_size("dp"), lax.axis_size("gen")
    length, width = operands.enc_rows.shape
    rows = width // n_dp
    plan = Transfer(30, 36, (13, 36), n_dp, n_gen, rows, width, LAGS)

    def blocked(fed):
        return fed._replace(active_t=fed.active_t.reshape(n_dp, -1, rows, length))

    operands = operands._replace(
        enc_ffn=blocked(operands.enc_ffn), dec_ffn=blocked(operands.dec_ffn)
    )
    tokens = pltpu.VMEM((length, width), WIDE)
    joint = pltpu.VMEM((3 * width // GROUP, length, GROUP), LOW)
    shared_rows = rows + 16
    held = Held(
        total=tokens,
        joint_dec=joint,
        joint_enc=joint,
        grad_low=pltpu.VMEM((length, width), LOW),
        grad_a=tokens,
        grad_b=tokens,
        adapters=pltpu.VMEM(operands.small.adapters.shape, WIDE),
        vectors=pltpu.VMEM((8, width), WIDE),
        gains=pltpu.VMEM((8, width), WIDE),
        transfer=plan.scratch(),
        shared=Shared.scratch(n_dp, shared_rows, features),
    )
    shape = jax.ShapeDtypeStruct
    results = Results(
        sums=shape((plan.units + 1, rows, width), LOW),
        pair_weights=shape((n_dp, rows, features), LOW),
        pair_vectors=shape((n_dp, 16, features), LOW),
        grad_dec_rows=shape((length, width), LOW),
        grad_enc_rows=shape((length, width), LOW),
    )
    in_vmem = pl.BlockSpec(memory_space=pltpu.VMEM)
    in_hbm = pl.BlockSpec(memory_space=pl.ANY)
    specs = jax.tree.map(lambda _: in_hbm, operands)
    specs = specs._replace(small=jax.tree.map(lambda _: in_vmem, operands.small))
    flat, in_tree = jax.tree.flatten(operands)
    scratch, scratch_tree = jax.tree.flatten(held)
    out, out_tree = jax.tree.flatten(results)
    remote = n_dp * n_gen > 1
    outs = pl.pallas_call(
        functools.partial(
            backward_kernel, plan, up_scale, bottleneck, tasks, vector_rows,
            (in_tree, out_tree, scratch_tree),
        ),
        in_specs=jax.tree.leaves(specs),
        out_specs=[in_vmem] * len(out),
        out_shape=out,
        scratch_shapes=scratch,
        compiler_params=pltpu.CompilerParams(
            vmem_limit_bytes=VMEM_LIMIT,
            **(dict(collective_id=0, has_side_effects=True) if remote else {}),
        ),
        cost_estimate=pl.CostEstimate(
            flops=100 * length * width * width, bytes_accessed=160 * width * width,
            transcendentals=0,
        ),
        name="backward",
    )(*flat)
    return jax.tree.unflatten(out_tree, outs)


class Gradients(NamedTuple):
    enc_norms: object
    enc_qkv: object
    enc_proj: object
    enc_up: object
    enc_down: object
    dec_norms: object
    dec_qkv: object
    dec_self_proj: object
    dec_cross_q: object
    dec_cross_kv: object
    dec_cross_proj: object
    dec_up: object
    dec_down: object


def unpack_kernel(sums_ref, dec_ref, enc_ref, *outs):
    out = Gradients(*outs[:13])
    outs[13][...] = dec_ref[...]
    outs[14][...] = enc_ref[...]
    size = out.enc_norms.shape[1]
    gains = sums_ref[30, 0:16, :].astype(WIDE)

    @pl.when(pl.program_id(0) == 0)
    def _():
        out.enc_norms[...] = gains[0:2, :size]
        out.dec_norms[...] = gains[2:6, :size]

    def plain(target, unit):
        target[...] = sums_ref[unit].astype(WIDE)

    def joint(target, first, parts):
        for at, part in enumerate(parts):
            for g in range(3):
                start = (3 * at + g) * GROUP
                target[:, start : start + GROUP] = sums_ref[
                    first + g, :, part * GROUP : (part + 1) * GROUP
                ].astype(WIDE)

    def beside(target, first):
        width = sums_ref.shape[2]
        for j in range(target.shape[1] // width):
            target[:, j * width : (j + 1) * width] = sums_ref[first + 2 * j].astype(WIDE)

    def below(target, first):
        for j in range(target.shape[0]):
            target[j] = sums_ref[first + 2 * j].astype(WIDE)

    below(out.dec_down, 0)
    beside(out.dec_up, 1)
    plain(out.dec_cross_proj, 8)
    joint(out.dec_cross_q, 9, (0,))
    joint(out.dec_cross_kv, 9, (1, 2))
    below(out.enc_down, 14)
    beside(out.enc_up, 15)
    plain(out.dec_self_proj, 22)
    joint(out.dec_qkv, 23, (0, 1, 2))
    plain(out.enc_proj, 26)
    joint(out.enc_qkv, 27, (0, 1, 2))


def unpack(sums, grad_dec_rows, grad_enc_rows, inner):
    units, rows, width = sums.shape
    length = grad_dec_rows.shape[0]
    steps = rows // 32 if rows % 32 == 0 else 1
    block = rows // steps
    while length % (16 * steps):
        steps, block = 1, rows
    shape = jax.ShapeDtypeStruct

    def matrix(columns):
        return shape((rows, columns), WIDE), pl.BlockSpec((block, columns), lambda i: (i, 0))

    downs = inner // width
    down = (
        shape((downs, rows, width), WIDE),
        pl.BlockSpec((downs, block, width), lambda i: (0, i, 0)),
    )
    tokens = pl.BlockSpec((length // steps, width), lambda i: (i, 0))

    def norms(count):
        return shape((count, rows), WIDE), whole((count, rows))

    made = Gradients(
        enc_norms=norms(2), enc_qkv=matrix(3 * width), enc_proj=matrix(width),
        enc_up=matrix(inner), enc_down=down, dec_norms=norms(4), dec_qkv=matrix(3 * width),
        dec_self_proj=matrix(width), dec_cross_q=matrix(width), dec_cross_kv=matrix(2 * width),
        dec_cross_proj=matrix(width), dec_up=matrix(inner), dec_down=down,
    )
    outs = pl.pallas_call(
        unpack_kernel,
        grid=(steps,),
        in_specs=[pl.BlockSpec((units, block, width), lambda i: (0, i, 0)), tokens, tokens],
        out_specs=[spec for _, spec in made] + [tokens, tokens],
        out_shape=[one for one, _ in made] + [shape((length, width), LOW)] * 2,
        compiler_params=pltpu.CompilerParams(vmem_limit_bytes=VMEM_LIMIT),
        cost_estimate=pl.CostEstimate(
            flops=0, bytes_accessed=6 * units * rows * width, transcendentals=0
        ),
        name="unpack",
    )(sums, grad_dec_rows, grad_enc_rows)
    grads = Gradients(*outs[:13])
    grads = grads._replace(
        enc_down=grads.enc_down.reshape(-1, width), dec_down=grads.dec_down.reshape(-1, width)
    )
    return grads, outs[13], outs[14]


def gelu_exact(values):
    return jax.nn.gelu(values, approximate=False)


def body(
    enc_input,
    dec_input,
    enc_segments,
    dec_segments,
    task_ids,
    cotangent,
    enc_norms,
    enc_qkv,
    enc_proj,
    enc_up,
    enc_down,
    dec_norms,
    dec_qkv,
    dec_self_proj,
    dec_cross_q,
    dec_cross_kv,
    dec_cross_proj,
    dec_up,
    dec_down,
    task_emb,
    layer_emb,
    proj_task,
    gen_weight,
    gen_vector,
):
    _, length, width = enc_input.shape
    layer_count = layer_emb.shape[0]
    pair_count = task_emb.shape[0] * layer_count
    bottleneck = gen_weight.shape[1] // 2
    up_scale = (width / bottleneck) ** 0.5

    def source_of(task_table, layer_table, projection):
        mixed_in = (
            jnp.dot(task_table, projection, precision=HIGHEST)[:, None, :] + layer_table[None, :, :]
        )
        return gelu_exact(mixed_in).reshape(pair_count, -1)

    source, source_pull = jax.vjp(source_of, task_emb, layer_emb, proj_task)
    source_low = source.astype(LOW)
    pieces, more_pieces = [
        jnp.einsum("th,hkd->tkd", source_low, part, preferred_element_type=WIDE).astype(LOW)
        for part in (gen_weight, gen_vector)
    ]
    first_pair = task_ids[0] * layer_count
    wanted = jnp.arange(8)[:, None] + first_pair == jnp.arange(128)[None, :]
    wanted = wanted.astype(WIDE)

    enc_rows, dec_rows = enc_input[0], dec_input[0]
    enc_joint = [(enc_qkv, 0), (enc_qkv, 1), (enc_qkv, 2)]
    dec_joint = [(dec_qkv, 0), (dec_qkv, 1), (dec_qkv, 2)]
    cross_joint = [(dec_cross_q, 0), (dec_cross_kv, 0), (dec_cross_kv, 1)]
    enc_hidden, enc_stored, adapters, vectors = attention_forward(
        enc_rows, enc_norms, (0, 0), None, enc_segments, enc_segments, enc_joint, enc_proj, False,
        gather=(wanted, pieces, more_pieces, bottleneck),
    )
    dec_hidden, dec_stored = attention_forward(
        dec_rows, dec_norms, (0, 0), None, dec_segments, dec_segments, dec_joint, dec_self_proj, True
    )
    encoded, enc_ffn_stored = feed_forward(
        enc_hidden, enc_norms, 1, enc_up, enc_down, adapters, vectors, 0, up_scale, WIDE
    )
    cross_hidden, cross_stored = attention_forward(
        dec_hidden, dec_norms, (1, 3), encoded, dec_segments, enc_segments, cross_joint,
        dec_cross_proj, False,
    )
    decoded, dec_ffn_stored = feed_forward(
        cross_hidden, dec_norms, 2, dec_up, dec_down, adapters, vectors, 1, up_scale, LOW
    )

    n_dp = lax.axis_size("dp")
    rows = width // n_dp
    features = gen_weight.shape[2]
    vector_rows = -(-pair_count * 3 // n_dp)
    small = Small(enc_norms, dec_norms, adapters, vectors, wanted)
    operands = Operands(
        cotangent[0], cross_hidden, dec_hidden, encoded, enc_hidden, dec_rows, enc_rows,
        enc_qkv, enc_proj, enc_up, enc_down, dec_qkv, dec_self_proj, dec_cross_q, dec_cross_kv,
        dec_cross_proj, dec_up, dec_down,
        enc_stored, dec_stored, cross_stored, enc_ffn_stored, dec_ffn_stored, small,
    )
    result = backward(
        operands, features, up_scale, bottleneck, task_emb.shape[0], vector_rows
    )
    pair_weights = result.pair_weights.reshape(pair_count, 2 * bottleneck, features)
    pair_vectors = result.pair_vectors[:, :vector_rows].reshape(-1, features)
    pair_vectors = pair_vectors[: pair_count * 3].reshape(pair_count, 3, features)
    grad_gen_weight, grad_gen_vector = [
        jnp.einsum("th,tkd->hkd", source_low, part, preferred_element_type=WIDE)
        for part in (pair_weights, pair_vectors)
    ]
    part_source = sum(
        jnp.einsum("tkd,hkd->th", part, made, preferred_element_type=WIDE)
        for part, made in ((pair_weights, gen_weight), (pair_vectors, gen_vector))
    )
    grad_source = sum_gen(part_source)
    grad_task_emb, grad_layer_emb, grad_proj_task = source_pull(grad_source)

    grads, grad_dec_rows, grad_enc_rows = unpack(
        result.sums, result.grad_dec_rows, result.grad_enc_rows, enc_up.shape[1]
    )
    return (
        decoded[None],
        grad_enc_rows[None],
        grad_dec_rows[None],
        *grads,
        grad_task_emb,
        grad_layer_emb,
        grad_proj_task,
        grad_gen_weight,
        grad_gen_vector,
    )


def solution(mesh):
    in_specs = (
        P(("dp", "gen"), None, None),
        P(("dp", "gen"), None, None),
        P(("dp", "gen"), None),
        P(("dp", "gen"), None),
        P(("dp", "gen")),
        P(("dp", "gen"), None, None),
        P(),
        P(),
        P(),
        P(),
        P(),
        P(),
        P(),
        P(),
        P(),
        P(),
        P(),
        P(),
        P(),
        P(),
        P(),
        P(),
        P(None, None, "gen"),
        P(None, None, "gen"),
    )
    out_specs = (
        P(("dp", "gen"), None, None),
        P(("dp", "gen"), None, None),
        P(("dp", "gen"), None, None),
        P(None, "dp"),
        P("dp", None),
        P("dp", None),
        P("dp", None),
        P("dp", None),
        P(None, "dp"),
        P("dp", None),
        P("dp", None),
        P("dp", None),
        P("dp", None),
        P("dp", None),
        P("dp", None),
        P("dp", None),
        P(),
        P(),
        P(),
        P(None, None, "gen"),
        P(None, None, "gen"),
    )
    return jax.shard_map(body, mesh=mesh, in_specs=in_specs, out_specs=out_specs, check_vma=False)
```

```python
import functools
from typing import NamedTuple

import jax
import jax.numpy as jnp
from jax import lax
from jax.experimental import pallas as pl
from jax.experimental.pallas import tpu as pltpu
from jax.sharding import PartitionSpec as P

H = 12
HD = 64
GROUP = 4 * HD
VMEM_LIMIT = 62 * 1024 * 1024
LAGS = (2, 2, 2, 2)
HIGHEST = lax.Precision.HIGHEST
LOW = jnp.bfloat16
WIDE = jnp.float32


def dot_nn(left_side, right_side):
    return jnp.dot(left_side, right_side, preferred_element_type=WIDE)


def dot_nt(left_side, right_side):
    return lax.dot_general(
        left_side, right_side, (((1,), (1,)), ((), ())), preferred_element_type=WIDE
    )


def gelu_parts(values):
    size = jnp.abs(values)
    density = jnp.exp(values * values * -0.5) * 0.3989422804014327
    bottom = 1.0 + 0.2316419 * size
    inverse = pl.reciprocal(bottom, approx=True)
    inverse = inverse * (2.0 - bottom * inverse)
    series = 1.330274429 * inverse - 1.821255978
    series = series * inverse + 1.781477937
    series = series * inverse - 0.356563782
    series = series * inverse + 0.31938153
    tail = series * inverse * density
    return jnp.where(values < 0.0, tail, 1.0 - tail), density


def rms_scale(values):
    return lax.rsqrt(jnp.mean(values * values, axis=-1, keepdims=True) + 1e-06)


def rms_backward(values, norm_gain, grad):
    scale = rms_scale(values)
    normed = values * scale
    pulled = grad * norm_gain
    inner = jnp.mean(normed * pulled, axis=-1, keepdims=True)
    grad_values = scale * (pulled - normed * inner)
    return grad_values, jnp.sum(grad * normed, axis=0, keepdims=True)


def segment_bias(seg_query, seg_key, causal):
    length = seg_query.shape[1]
    column = jnp.broadcast_to(seg_query.astype(WIDE), (128, length)).T[:, :1]
    allowed = column == seg_key.astype(WIDE)
    if causal:
        query_place = lax.broadcasted_iota(jnp.int32, (length, length), 0)
        key_place = lax.broadcasted_iota(jnp.int32, (length, length), 1)
        allowed = allowed & (query_place >= key_place)
    return jnp.where(allowed, 0.0, -1e30)


def row_of(ref, row):
    return ref[row : row + 1].astype(WIDE)


def first_half(shape):
    return lax.broadcasted_iota(jnp.int32, shape, 1) < HD


class Attended(NamedTuple):
    x_t: object
    memory_t: object
    q_t: object
    keys: object
    values: object
    mixed_t: object
    probs: object


class Fed(NamedTuple):
    ffn: object
    x_t: object
    active_t: object
    slope: object


class Gather:
    def __init__(self, n_gen, bottleneck, refs):
        self.n_gen, self.bottleneck, self.line = n_gen, bottleneck, lax.axis_index("gen")
        (
            self.weights, self.pieces, self.more, self.adapters, self.vectors,
            self.asked, self.chosen, self.arrived, self.sems,
        ) = refs

    @staticmethod
    def scratch(n_gen, features):
        return (
            pltpu.VMEM((n_gen, 8, 128), WIDE),
            pltpu.VMEM((n_gen, 2, 64, features), LOW),
            pltpu.VMEM((n_gen, 2, 64, features), LOW),
            pltpu.SemaphoreType.DMA((4, max(n_gen - 1, 1))),
        )

    def ask(self, k):
        sems = self.sems
        return gen_copy(
            self.weights, self.asked, sems.at[0], sems.at[1], self.line, k, self.n_gen
        )

    def answer(self, k):
        sems = self.sems
        return gen_copy(
            self.chosen.at[k], self.arrived, sems.at[2], sems.at[3], self.line, k, self.n_gen
        )

    def pick(self, target, weights):
        for layer in range(2):
            start = 0
            for source in (self.pieces, self.more):
                pairs, rows, features = source.shape
                total = jnp.zeros((rows, features), WIDE)
                for pair in range(pairs):
                    weight = weights[layer : layer + 1, pair : pair + 1]
                    total = total + weight * source[pair].astype(WIDE)
                target[layer, start : start + rows] = total.astype(LOW)
                start += rows

    def begin(self, step):
        if self.n_gen > 1:
            pl.when(step == 0)(lambda: gen_greet(self.line, self.n_gen))

    def end(self, step, steps):
        n_gen, size = self.n_gen, self.bottleneck

        @pl.when(step == 0)
        def _():
            if n_gen > 1:
                gen_greeted(n_gen)
            for k in range(1, n_gen):
                self.ask(k).start()

        @pl.when(step == 1)
        def _():
            for k in range(1, n_gen):
                self.ask(k).wait()
            for k in range(1, n_gen):
                self.pick(self.chosen.at[k], self.asked[(self.line + k) % n_gen])
                self.answer(k).start()
            self.pick(self.arrived.at[self.line], self.weights[...])

        @pl.when(step == steps - 1)
        def _():
            for k in range(1, n_gen):
                self.answer(k).wait()
            rows = 2 * size + 3
            self.adapters[...] = jnp.zeros_like(self.adapters)
            for layer in range(2):
                joined = jnp.concatenate(
                    [self.arrived[j, layer, 0:rows].astype(WIDE) for j in range(n_gen)], axis=1
                ).astype(LOW)
                self.adapters[layer, 0, 0:size] = joined[0:size]
                self.adapters[layer, 1, 0:size] = joined[size : 2 * size]
                self.vectors[layer] = joined[2 * size : 2 * size + 3]


def attention_forward_kernel(
    cross, causal, gather, gain_rows,
    x_ref, gain_ref, memory_ref, memory_gain_ref, seg_q_ref, seg_k_ref,
    wq_ref, wk_ref, wv_ref, wo_ref, *refs,
):
    step = pl.program_id(0)
    more_in = refs[:3] if gather else ()
    refs = refs[len(more_in) :]
    hidden_ref, x_t_ref, memory_t_ref, q_t_ref, k_ref, v_ref, mixed_t_ref, probs_ref = refs[:8]
    more_out = refs[8:10] if gather else ()
    refs = refs[8 + len(more_out) :]
    x_low, memory_low, bias = refs[:3]
    if gather:
        work = Gather(*gather, more_in + more_out + refs[3:])
        work.begin(step)

    @pl.when(step == 0)
    def _():
        values = x_ref[...].astype(WIDE)
        hidden_ref[...] = values
        normed = (values * rms_scale(values) * row_of(gain_ref, gain_rows[0])).astype(LOW)
        x_low[...] = normed
        x_t_ref[...] = normed.T
        if cross:
            values = memory_ref[...].astype(WIDE)
            normed = (values * rms_scale(values) * row_of(memory_gain_ref, gain_rows[1])).astype(LOW)
            memory_low[...] = normed
            memory_t_ref[...] = normed.T
        bias[...] = segment_bias(seg_q_ref[...], seg_k_ref[...], causal)

    source_low = memory_low if cross else x_low
    queries = dot_nn(x_low[...], wq_ref[...]).astype(LOW)
    q_t_ref[...] = queries.T
    k_ref[...] = dot_nn(source_low[...], wk_ref[...]).astype(LOW)
    v_ref[...] = dot_nn(source_low[...], wv_ref[...]).astype(LOW)
    scaled = queries * LOW(HD ** (-0.5))
    length = scaled.shape[0]
    lanes = first_half((length, 2 * HD))
    parts = []
    for pair in range(2):
        columns = slice(pair * 2 * HD, (pair + 1) * 2 * HD)
        two = scaled[:, columns]
        keys = k_ref[:, columns]
        values = v_ref[:, columns]
        halves = []
        for side in range(2):
            mine = jnp.where(lanes if side == 0 else ~lanes, two, LOW(0))
            scores = dot_nt(mine, keys) + bias[...]
            raised = jnp.exp(scores - jnp.max(scores, axis=-1, keepdims=True))
            total = jnp.sum(raised, axis=-1, keepdims=True)
            probs = (raised * (1.0 / total)).astype(LOW)
            probs_ref[2 * pair + side] = probs
            halves.append(dot_nn(probs, values))
        parts.append(jnp.where(lanes, halves[0], halves[1]).astype(LOW))
    mixed = jnp.concatenate(parts, axis=1)
    mixed_t_ref[...] = mixed.T
    hidden_ref[...] += dot_nn(mixed, wo_ref[...])
    if gather:
        work.end(step, pl.num_programs(0))


def whole(shape):
    return pl.BlockSpec(shape, lambda *_: (0,) * len(shape))


def attention_forward(
    x, gains, gain_rows, memory, seg_q, seg_k, weights, w_out, causal, gather=None
):
    n_gen = lax.axis_size("gen")
    more_in, more_out, more_scratch, asked = (), (), (), None
    if gather is not None:
        wanted, pieces, more_pieces, bottleneck = gather
        more_in = (wanted, pieces, more_pieces)
        padded = -bottleneck % 16 + bottleneck
        more_out = (
            jax.ShapeDtypeStruct((2, 2, padded, x.shape[1]), LOW),
            jax.ShapeDtypeStruct((2, 3, x.shape[1]), LOW),
        )
        more_scratch = Gather.scratch(n_gen, pieces.shape[2])
        asked = (n_gen, bottleneck)
    remote = gather is not None and n_gen > 1
    cross = memory is not None
    length, width = x.shape
    groups = width // GROUP
    if not cross:
        memory = x
    shape = jax.ShapeDtypeStruct
    columns = pl.BlockSpec((length, GROUP), lambda g: (0, g))
    rows = pl.BlockSpec((GROUP, length), lambda g: (g, 0))

    def weight_spec(offset):
        return pl.BlockSpec((width, GROUP), lambda g: (0, offset + g))

    memory_spec = whole((length, width)) if cross else whole((16, 128))
    memory_t_shape = (width, length) if cross else (16, 128)
    outs = pl.pallas_call(
        functools.partial(attention_forward_kernel, cross, causal, asked, gain_rows),
        grid=(groups,),
        in_specs=[
            whole((length, width)),
            whole(gains.shape),
            memory_spec,
            whole(gains.shape),
            whole((1, length)),
            whole((1, length)),
            weight_spec(weights[0][1] * groups),
            weight_spec(weights[1][1] * groups),
            weight_spec(weights[2][1] * groups),
            pl.BlockSpec((GROUP, width), lambda g: (g, 0)),
        ]
        + [whole(one.shape) for one in more_in],
        out_specs=[
            whole((length, width)),
            whole((width, length)),
            whole(memory_t_shape),
            rows,
            columns,
            columns,
            rows,
            pl.BlockSpec((4, length, length), lambda g: (g, 0, 0)),
        ]
        + [whole(one.shape) for one in more_out],
        out_shape=[
            shape((length, width), WIDE),
            shape((width, length), LOW),
            shape(memory_t_shape, LOW),
            shape((width, length), LOW),
            shape((length, width), LOW),
            shape((length, width), LOW),
            shape((width, length), LOW),
            shape((H, length, length), LOW),
            *more_out,
        ],
        scratch_shapes=[
            pltpu.VMEM((length, width), LOW),
            pltpu.VMEM((length, width) if cross else (16, 128), LOW),
            pltpu.VMEM((length, length), WIDE),
            *more_scratch,
        ],
        compiler_params=pltpu.CompilerParams(
            vmem_limit_bytes=VMEM_LIMIT,
            **(dict(collective_id=1, has_side_effects=True) if remote else {}),
        ),
        cost_estimate=pl.CostEstimate(
            flops=2 * length * width * (4 * width + 2 * length),
            bytes_accessed=2 * (4 * width * width + H * length * length + 8 * length * width),
            transcendentals=H * length * length,
        ),
        name="attention_forward",
    )(x, gains, memory, gains, seg_q, seg_k,
      weights[0][0], weights[1][0], weights[2][0], w_out, *more_in)
    hidden, x_t, memory_t, q_t, keys, values, mixed_t, probs = outs[:8]
    stored = Attended(x_t, memory_t if cross else None, q_t, keys, values, mixed_t, probs)
    return (hidden, stored) + tuple(outs[8:])


def layer_parts(values):
    centred = values - jnp.mean(values, axis=-1, keepdims=True)
    scale = lax.rsqrt(jnp.mean(centred * centred, axis=-1, keepdims=True) + 1e-05)
    return centred * scale, scale


def feed_forward_kernel(
    up_scale, layer, gain_row,
    x_ref, gain_ref, up_ref, down_ref, adapter_ref, vector_ref,
    out_ref, ffn_ref, x_t_ref, active_t_ref, slope_ref,
    x_low, total,
):
    step = pl.program_id(0)

    @pl.when(step == 0)
    def _():
        values = x_ref[...]
        normed = (values * rms_scale(values) * row_of(gain_ref, gain_row)).astype(LOW)
        x_low[...] = normed
        x_t_ref[...] = normed.T
        total[...] = jnp.zeros_like(total)

    before = dot_nn(x_low[...], up_ref[...])
    cumulative, density = gelu_parts(before)
    active = (before * cumulative).astype(LOW)
    slope_ref[...] = (cumulative + before * density).astype(LOW)
    active_t_ref[...] = active.T
    total[...] += dot_nn(active, down_ref[...])

    @pl.when(step == pl.num_programs(0) - 1)
    def _():
        ffn = total[...]
        ffn_ref[...] = ffn
        normed, _ = layer_parts(ffn)
        vectors = vector_ref[layer].astype(WIDE)
        low = (normed * (1.0 + vectors[1:2]) + vectors[2:3]).astype(LOW)
        inner = dot_nt(low, adapter_ref[layer, 0])
        gate = (inner * gelu_parts(inner)[0]).astype(LOW)
        adapted = dot_nn(gate, adapter_ref[layer, 1]) * up_scale + vectors[0:1]
        out_ref[...] = (x_ref[...] + ffn + adapted).astype(out_ref.dtype)


def feed_forward(
    x, gains, gain_row, w_up, w_down, adapter, vectors, layer, up_scale, out_dtype, blocks=4
):
    length, width = x.shape
    inner = w_up.shape[1]
    block = inner // blocks
    shape = jax.ShapeDtypeStruct
    out, ffn, x_t, active_t, slope = pl.pallas_call(
        functools.partial(feed_forward_kernel, up_scale, layer, gain_row),
        grid=(blocks,),
        in_specs=[
            whole((length, width)),
            whole(gains.shape),
            pl.BlockSpec((width, block), lambda j: (0, j)),
            pl.BlockSpec((block, width), lambda j: (j, 0)),
            whole(adapter.shape),
            whole(vectors.shape),
        ],
        out_specs=[
            whole((length, width)),
            whole((length, width)),
            whole((width, length)),
            pl.BlockSpec((block, length), lambda j: (j, 0)),
            pl.BlockSpec((length, block), lambda j: (0, j)),
        ],
        out_shape=[
            shape((length, width), out_dtype),
            shape((length, width), WIDE),
            shape((width, length), LOW),
            shape((inner, length), LOW),
            shape((length, inner), LOW),
        ],
        scratch_shapes=[pltpu.VMEM((length, width), LOW), pltpu.VMEM((length, width), WIDE)],
        compiler_params=pltpu.CompilerParams(vmem_limit_bytes=VMEM_LIMIT),
        cost_estimate=pl.CostEstimate(
            flops=4 * length * width * inner,
            bytes_accessed=4 * width * inner + 4 * length * inner + 12 * length * width,
            transcendentals=length * inner,
        ),
        name="feed_forward",
    )(x, gains, w_up, w_down, adapter, vectors)
    return out, Fed(ffn, x_t, active_t, slope)


def join_rows(ref):
    blocks, _, rows, columns = ref.shape
    if rows % 16 == 0:
        return ref[...].reshape(blocks * rows, columns)
    parts = [ref[i, 0].astype(WIDE) for i in range(blocks)]
    return jnp.concatenate(parts, axis=0).astype(LOW)


def power_of_two(least):
    return 1 << (least - 1).bit_length()


class TransferRefs(NamedTuple):
    unit: object
    held: object
    into: object
    total: object
    line: object
    send: object
    recv: object


class Transfer:
    def __init__(self, units, small, n_dp, n_gen, rows, width, lags):
        self.units, self.small = units, small
        self.n_dp, self.n_gen = n_dp, n_gen
        self.rows, self.width = rows, width
        self.bits = n_dp.bit_length() - 1
        self.final = self.bits + max(n_gen - 1, 0)
        first, between, last, along = lags
        self.lags = [first] + [between] * (self.bits - 2) + [last] + [along] * (n_gen - 1)
        self.at = [sum(self.lags[:s]) for s in range(self.final + 1)]
        self.slots = units + self.at[self.final]
        self.ring = 2 * max(first, between, last) + 1
        self.line_ring = max(2 * along + 1, along * (n_gen - 1))
        self.unit_ring = power_of_two(first + 1)
        self.sum_ring = power_of_two(along * max(n_gen - 1, 1) + 1)

    def scratch(self):
        block = (self.rows, self.width)
        bits, lags, ring = self.bits, self.lags, self.ring
        stages = max(bits + self.n_gen - 1, 1)
        return TransferRefs(
            unit=pltpu.VMEM((self.unit_ring, self.n_dp) + block, LOW),
            held=[pltpu.VMEM((lags[s], self.n_dp >> s) + block, LOW) for s in range(1, bits)],
            into=[pltpu.VMEM((ring, self.n_dp >> (s + 1)) + block, LOW) for s in range(bits)],
            total=pltpu.VMEM((self.sum_ring,) + block, LOW),
            line=[pltpu.VMEM((self.line_ring,) + block, LOW) for _ in range(self.n_gen - 1)],
            send=pltpu.SemaphoreType.DMA((stages, max(ring, self.line_ring))),
            recv=pltpu.SemaphoreType.DMA((stages, max(ring, self.line_ring))),
        )

    def bind(self, refs):
        self.refs = refs
        self.place = lax.axis_index("dp")
        self.at_line = lax.axis_index("gen")
        self.core = self.place % 2
        self.partners = [self.partner(step) for step in range(self.bits)]
        self.positions = [self.position(index) for index in range(self.n_dp)]

    def partner(self, step):
        if step == 0:
            return self.place + 1 - 2 * self.core
        one, other = 1 << step, 1 << (self.bits - step)
        flipped = [self.place + power * (1 - 2 * ((self.place // power) % 2)) for power in (one, other)]
        return jnp.where(self.core == 0, *flipped)

    def position(self, index):
        if self.bits == 0:
            return 0
        core = index % 2
        place = jnp.where(self.core == core, 1 << (self.bits - 1), 0)
        for step in range(1, self.bits):
            power = 1 << (step if core == 0 else self.bits - step)
            differs = (self.place // power + index // power) % 2
            place = place + differs * (1 << (self.bits - 1 - step))
        return place

    def barrier(self):
        if self.bits + self.n_gen == 1:
            return
        semaphore = pltpu.get_barrier_semaphore()
        for k in range(1, self.n_dp):
            pl.semaphore_signal(
                semaphore, inc=1,
                device_id={"dp": (self.place + k) % self.n_dp, "gen": self.at_line},
                device_id_type=pl.DeviceIdType.MESH,
            )
        amount = self.n_dp - 1
        if self.n_gen > 1:
            ends = ((self.at_line > 0, -1), (self.at_line < self.n_gen - 1, 1))
            for there, towards in ends:
                @pl.when(there)
                def _():
                    pl.semaphore_signal(
                        semaphore, inc=1,
                        device_id={"dp": self.place, "gen": self.at_line + towards},
                        device_id_type=pl.DeviceIdType.MESH,
                    )
                amount = amount + jnp.where(there, 1, 0)
        pl.semaphore_wait(semaphore, amount)

    def sized(self, unit, act):
        if isinstance(unit, int):
            act(16 if unit in self.small else self.rows)
            return
        is_small = unit == self.small[0]
        for one in self.small[1:]:
            is_small = is_small | (unit == one)
        pl.when(is_small)(functools.partial(act, 16))
        pl.when(~is_small)(functools.partial(act, self.rows))

    def halving(self, step, unit, rows):
        refs, many = self.refs, self.n_dp >> (step + 1)
        if step == 0:
            source = refs.unit.at[unit % self.unit_ring, pl.ds(0, many), pl.ds(0, rows)]
        else:
            source = refs.held[step - 1].at[unit % self.lags[step], pl.ds(many, many), pl.ds(0, rows)]
        slot = unit % self.ring
        return pltpu.make_async_remote_copy(
            src_ref=source,
            dst_ref=refs.into[step].at[slot, :, pl.ds(0, rows)],
            send_sem=refs.send.at[step, slot],
            recv_sem=refs.recv.at[step, slot],
            device_id={"dp": self.partners[step], "gen": self.at_line},
            device_id_type=pl.DeviceIdType.MESH,
        )

    def along(self, i, unit, towards, rows):
        slot = unit % self.line_ring
        step = self.bits + i
        return pltpu.make_async_remote_copy(
            src_ref=self.refs.total.at[unit % self.sum_ring, pl.ds(0, rows)],
            dst_ref=self.refs.line[i].at[slot, pl.ds(0, rows)],
            send_sem=self.refs.send.at[step, slot],
            recv_sem=self.refs.recv.at[step, slot],
            device_id={"dp": self.place, "gen": self.at_line + towards},
            device_id_type=pl.DeviceIdType.MESH,
        )

    def roles(self, i):
        count = self.n_gen
        half = count // 2
        if i < half - 1:
            return [(i, 1), (count - 1 - i, -1)], [i + 1, count - 2 - i], True
        if i == half - 1:
            return [(half - 1, 1), (half, -1)], [half - 1, half], True
        j = count - 2 - i
        return [(j + 1, -1), (count - 2 - j, 1)], [j, count - 1 - j], False

    def stage(self, s, unit, out_ref):
        refs, bits = self.refs, self.bits
        if s == 0:
            if bits:
                self.sized(unit, lambda rows: self.halving(0, unit, rows).start())
            return
        if s <= bits:
            self.sized(unit, lambda rows: self.halving(s - 1, unit, rows).wait())
            received = refs.into[s - 1].at[unit % self.ring]
            many = self.n_dp >> s
            if s == 1:
                kept = refs.unit.at[unit % self.unit_ring, pl.ds(many, many)]
            else:
                kept = refs.held[s - 2].at[unit % self.lags[s - 1], pl.ds(0, many)]
            if s < bits:
                refs.held[s - 1][unit % self.lags[s]] = kept[...] + received[...]
                self.sized(unit, lambda rows: self.halving(s, unit, rows).start())
                return
            refs.total[unit % self.sum_ring] = kept[0] + received[0]
        i = s - bits
        total = refs.total.at[unit % self.sum_ring]
        if i > 0:
            senders, receivers, adds = self.roles(i - 1)
            for sender, towards in senders:
                @pl.when(self.at_line == sender)
                def _():
                    self.sized(
                        unit, lambda rows: self.along(i - 1, unit, towards, rows).wait_send()
                    )

            @pl.when((self.at_line == receivers[0]) | (self.at_line == receivers[1]))
            def _():
                back = jnp.where(self.at_line == 0, 1, -1)
                self.sized(unit, lambda rows: self.along(i - 1, unit, back, rows).wait_recv())
                incoming = refs.line[i - 1].at[unit % self.line_ring]
                if adds:
                    total[...] = total[...] + incoming[...]
                else:
                    total[...] = incoming[...]
        if i < self.n_gen - 1:
            senders, _, _ = self.roles(i)
            for sender, towards in senders:
                @pl.when(self.at_line == sender)
                def _():
                    self.sized(unit, lambda rows: self.along(i, unit, towards, rows).start())
        else:
            out_ref[unit] = total[...]

    def put(self, unit, values, start=0):
        target = self.refs.unit.at[unit % self.unit_ring]
        stop = start + values.shape[1]
        for i in range(self.n_dp):
            part = values[i * self.rows : (i + 1) * self.rows].astype(LOW)
            target[self.positions[i], :, start:stop] = part

    def send(self, unit, out_ref):
        if self.bits + self.n_gen == 1:
            out_ref[unit] = self.refs.unit[unit % self.unit_ring, 0]
            return
        self.slot(unit, out_ref)
        self.stage(0, unit, out_ref)

    def drain(self, first, out_ref):
        def one(t, carried):
            self.slot(t, out_ref)
            return carried

        if self.bits + self.n_gen > 1:
            lax.fori_loop(first, self.slots, one, 0)

    def slot(self, t, out_ref):
        for s in reversed(range(1, self.final + 1)):
            unit = t - self.at[s]

            @pl.when((unit >= 0) & (unit < self.units))
            def _():
                self.stage(s, unit, out_ref)


class Shared:
    def __init__(self, plan, refs):
        self.plan, (self.own, self.all, self.sends, self.recvs) = plan, refs

    @staticmethod
    def scratch(n_dp, rows, features):
        many = max(n_dp - 1, 1)
        return (
            pltpu.VMEM((rows, features), LOW),
            pltpu.VMEM((n_dp, rows, features), LOW),
            pltpu.SemaphoreType.DMA((many,)),
            pltpu.SemaphoreType.DMA((many,)),
        )

    def copy(self, k):
        plan = self.plan
        return pltpu.make_async_remote_copy(
            src_ref=self.own,
            dst_ref=self.all.at[plan.place],
            send_sem=self.sends.at[k - 1],
            recv_sem=self.recvs.at[k - 1],
            device_id={"dp": (plan.place + k) % plan.n_dp, "gen": plan.at_line},
            device_id_type=pl.DeviceIdType.MESH,
        )

    def start(self, weights, vectors):
        plan = self.plan
        features = self.own.shape[1]
        rows, more = weights.shape[0], vectors.shape[0]
        for j in range(plan.n_gen):
            @pl.when(plan.at_line == j)
            def _():
                columns = slice(j * features, (j + 1) * features)
                self.own[:rows] = weights[:, columns]
                self.own[rows : rows + more] = vectors[:, columns]
        for k in range(1, plan.n_dp):
            self.copy(k).start()
        self.all[plan.place] = self.own[...]

    def finish(self, weights_ref, vectors_ref):
        for k in range(1, self.plan.n_dp):
            self.copy(k).wait()
        rows = self.plan.rows
        weights_ref[...] = self.all[:, :rows]
        vectors_ref[...] = self.all[:, rows:]


class Gains:
    def __init__(self, plan, refs):
        self.plan, (self.out, self.into, self.sends, self.recvs) = plan, refs

    @staticmethod
    def scratch(n_dp):
        many = max(n_dp - 1, 1)
        return (
            pltpu.VMEM((n_dp, 8, 128), WIDE),
            pltpu.VMEM((n_dp, 8, 128), WIDE),
            pltpu.SemaphoreType.DMA((many,)),
            pltpu.SemaphoreType.DMA((many,)),
        )

    def copy(self, k):
        plan = self.plan
        peer = (plan.place + k) % plan.n_dp
        return pltpu.make_async_remote_copy(
            src_ref=self.out.at[peer],
            dst_ref=self.into.at[plan.place],
            send_sem=self.sends.at[k - 1],
            recv_sem=self.recvs.at[k - 1],
            device_id={"dp": peer, "gen": plan.at_line},
            device_id_type=pl.DeviceIdType.MESH,
        )

    def start(self, gains):
        plan = self.plan
        self.out[...] = jnp.zeros_like(self.out)
        for i in range(plan.n_dp):
            self.out[i, 0:6, 0 : plan.rows] = gains[0:6, i * plan.rows : (i + 1) * plan.rows]
        for k in range(1, plan.n_dp):
            self.copy(k).start()
        self.into[plan.place] = self.out[plan.place]

    def finish(self, out_ref):
        for k in range(1, self.plan.n_dp):
            self.copy(k).wait()
        total = self.into[0]
        for j in range(1, self.plan.n_dp):
            total = total + self.into[j]
        out_ref[...] = total


def gen_greet(line, n_gen):
    semaphore = pltpu.get_barrier_semaphore()
    for k in range(1, n_gen):
        pl.semaphore_signal(
            semaphore, inc=1, device_id={"gen": (line + k) % n_gen},
            device_id_type=pl.DeviceIdType.MESH,
        )


def gen_greeted(n_gen):
    pl.semaphore_wait(pltpu.get_barrier_semaphore(), n_gen - 1)


def gen_copy(source, target, sends, recvs, line, k, n_gen):
    return pltpu.make_async_remote_copy(
        src_ref=source,
        dst_ref=target.at[line],
        send_sem=sends.at[k - 1],
        recv_sem=recvs.at[k - 1],
        device_id={"gen": (line + k) % n_gen},
        device_id_type=pl.DeviceIdType.MESH,
    )


def sum_gen_kernel(n_gen, part_ref, out_ref, parts, sends, recvs):
    line = lax.axis_index("gen")
    gen_greet(line, n_gen)
    gen_greeted(n_gen)
    for k in range(1, n_gen):
        gen_copy(part_ref, parts, sends, recvs, line, k, n_gen).start()
    parts[line] = part_ref[...]
    for k in range(1, n_gen):
        gen_copy(part_ref, parts, sends, recvs, line, k, n_gen).wait()
    total = parts[0]
    for j in range(1, n_gen):
        total = total + parts[j]
    out_ref[...] = total


def sum_gen(part):
    n_gen = lax.axis_size("gen")
    if n_gen == 1:
        return part
    return pl.pallas_call(
        functools.partial(sum_gen_kernel, n_gen),
        in_specs=[pl.BlockSpec(memory_space=pltpu.VMEM)],
        out_specs=pl.BlockSpec(memory_space=pltpu.VMEM),
        out_shape=jax.ShapeDtypeStruct(part.shape, part.dtype),
        scratch_shapes=[
            pltpu.VMEM((n_gen,) + part.shape, part.dtype),
            pltpu.SemaphoreType.DMA((n_gen - 1,)),
            pltpu.SemaphoreType.DMA((n_gen - 1,)),
        ],
        compiler_params=pltpu.CompilerParams(collective_id=2, has_side_effects=True),
        name="sum_gen",
    )(part)


class Operands(NamedTuple):
    cotangent: object
    cross_hidden: object
    dec_hidden: object
    encoded: object
    enc_hidden: object
    dec_rows: object
    enc_rows: object
    enc_qkv: object
    enc_proj: object
    enc_up: object
    enc_down: object
    dec_qkv: object
    dec_self_proj: object
    dec_cross_q: object
    dec_cross_kv: object
    dec_cross_proj: object
    dec_up: object
    dec_down: object
    enc_attn: Attended
    dec_attn: Attended
    cross_attn: Attended
    enc_ffn: Fed
    dec_ffn: Fed
    small: object


class Small(NamedTuple):
    enc_norms: object
    dec_norms: object
    adapters: object
    vectors: object
    wanted: object


class Results(NamedTuple):
    sums: object
    pair_weights: object
    pair_vectors: object
    gains: object
    grad_dec_rows: object
    grad_enc_rows: object


class Held(NamedTuple):
    total: object
    joint_dec: object
    joint_enc: object
    grad_low: object
    grad_a: object
    grad_b: object
    adapters: object
    vectors: object
    gains: object
    transfer: TransferRefs
    shared: object
    own_gains: object


class Backward:
    def __init__(self, plan, up_scale, bottleneck, tasks, refs, small, scratch, out_ref):
        self.plan, self.up_scale, self.bottleneck, self.tasks = plan, up_scale, bottleneck, tasks
        self.refs, self.small, self.scratch, self.out_ref = refs, small, scratch, out_ref

    def send(self, unit):
        self.plan.send(unit, self.out_ref)

    def attention(
        self, first_unit, grad_ref, gain_rows, x, memory, stored, weights, finish, after_first=None
    ):
        cross = memory is not None
        plan, scratch = self.plan, self.scratch
        total_x, total_memory, grad_low = scratch.total, scratch.grad_b, scratch.grad_low
        length, width = x.shape
        groups = width // GROUP
        columns = pl.BlockSpec((length, GROUP), lambda g: (0, g))
        rows = pl.BlockSpec((GROUP, length), lambda g: (g, 0))

        def weight_spec(offset):
            return pl.BlockSpec((width, GROUP), lambda g: (0, offset + g))

        def body(x_t_ref, q_t_ref, k_ref, v_ref, mixed_t_ref, probs_ref, wo_ref, *more):
            if cross:
                x_ref, wq_ref, wk_ref, wv_ref, memory_ref, memory_t_ref = more
            else:
                memory_t_ref = x_t_ref
            step = pl.program_id(0)

            @pl.when(step == 0)
            def _():
                grad_low[...] = grad_ref[...].astype(LOW)
                if cross:
                    total_x[...] = jnp.zeros_like(total_x)
                    total_memory[...] = jnp.zeros_like(total_memory)
                plan.put(first_unit, dot_nn(mixed_t_ref[...], grad_low[...]))
                self.send(first_unit)
                if after_first is not None:
                    after_first()

            grad_mixed = dot_nt(grad_low[...], wo_ref[...]).astype(LOW)
            grad_mixed_t = grad_mixed.T
            lanes = first_half((length, 2 * HD))
            heads = range(4)

            def pair_of(ref, head):
                pair = head // 2
                return ref[:, pair * 2 * HD : (pair + 1) * 2 * HD]

            def rows_of(ref, head):
                return ref[head * HD : (head + 1) * HD, :]

            grad_probs = []
            for head in heads:
                mine = jnp.where(
                    lanes if head % 2 == 0 else ~lanes, pair_of(grad_mixed, head), LOW(0)
                )
                grad_probs.append(dot_nt(mine, pair_of(v_ref, head)))
            mixed_rows = mixed_t_ref[pl.ds(pl.multiple_of(step * GROUP, GROUP), GROUP), :]
            pulled = grad_mixed_t.astype(WIDE) * mixed_rows.astype(WIDE)
            inner = [
                jnp.sum(rows_of(pulled, head), axis=0, keepdims=True) for head in heads
            ]
            inner = jnp.concatenate(inner + inner, axis=0).T
            inner = jnp.stack([inner[:, head : head + 1] for head in heads])
            probs = probs_ref[...].astype(WIDE)
            grad_scores = (probs * (jnp.stack(grad_probs) - inner)).astype(LOW)
            halves = [dot_nn(grad_scores[head], pair_of(k_ref, head)) for head in heads]
            grad_q = [
                jnp.where(lanes, halves[head], halves[head + 1]) * HD ** (-0.5)
                for head in heads[::2]
            ]
            grad_k = [
                dot_nn(rows_of(q_t_ref, head), grad_scores[head]) * HD ** (-0.5) for head in heads
            ]
            grad_v = [dot_nn(rows_of(grad_mixed_t, head), probs_ref[head]) for head in heads]
            low_q = jnp.concatenate(grad_q, axis=1).astype(LOW)
            low_k = jnp.concatenate(grad_k, axis=0).astype(LOW).T
            low_v = jnp.concatenate(grad_v, axis=0).astype(LOW).T
            unit = first_unit + 1 + step
            plan.put(unit, dot_nn(x_t_ref[...], low_q), 0)
            plan.put(unit, dot_nn(memory_t_ref[...], low_k), GROUP)
            plan.put(unit, dot_nn(memory_t_ref[...], low_v), 2 * GROUP)
            self.send(unit)
            if not cross:
                for part, low in enumerate((low_q, low_k, low_v)):
                    finish[part * groups + step] = low
                return
            total_x[...] += dot_nt(low_q, wq_ref[...])
            total_memory[...] += dot_nt(low_k, wk_ref[...]) + dot_nt(low_v, wv_ref[...])

            @pl.when(step == groups - 1)
            def _():
                x_gain, memory_gain = gain_rows
                grad_values, grad_gain = rms_backward(
                    x_ref[...].astype(WIDE), self.gain(x_gain), total_x[...]
                )
                scratch.gains[x_gain : x_gain + 1] = grad_gain
                finish(grad_ref[...] + grad_values)
                grad_values, grad_gain = rms_backward(
                    memory_ref[...], self.gain(memory_gain), total_memory[...]
                )
                scratch.gains[memory_gain : memory_gain + 1] = grad_gain
                scratch.grad_b[...] = grad_values

        whole_tokens, whole_turned = whole((length, width)), whole((width, length))
        pltpu.emit_pipeline(
            body,
            grid=(groups,),
            in_specs=[
                whole_turned, rows, columns, columns, whole_turned,
                pl.BlockSpec((4, length, length), lambda g: (g, 0, 0)),
                pl.BlockSpec((GROUP, width), lambda g: (g, 0)),
            ]
            + (
                [whole_tokens]
                + [weight_spec(offset * groups) for _, offset in weights[:3]]
                + [whole_tokens, whole_turned]
                if cross
                else []
            ),
        )(
            stored.x_t, stored.q_t, stored.keys, stored.values, stored.mixed_t, stored.probs,
            weights[3],
            *(
                [x] + [array for array, _ in weights[:3]] + [memory, stored.memory_t]
                if cross
                else []
            ),
        )

    def input_grad(self, first_slot, joint, grad_ref, gain_row, x, w_joint, target):
        scratch, total = self.scratch, self.scratch.total
        length, width = x.shape
        groups = width // GROUP

        def body(x_ref, wq_ref, wk_ref, wv_ref):
            step = pl.program_id(0)
            self.plan.slot(first_slot + step, self.out_ref)
            result = sum(
                dot_nt(joint[part * groups + step], weight[...])
                for part, weight in enumerate((wq_ref, wk_ref, wv_ref))
            )
            total[...] = jnp.where(step == 0, 0.0, total[...]) + result

            @pl.when(step == groups - 1)
            def _():
                grad_values, grad_gain = rms_backward(
                    x_ref[...].astype(WIDE), self.gain(gain_row), total[...]
                )
                scratch.gains[gain_row : gain_row + 1] = grad_gain
                target[...] = (grad_ref[...] + grad_values).astype(target.dtype)

        def weight_spec(part):
            return pl.BlockSpec((width, GROUP), lambda g: (0, part * groups + g))

        pltpu.emit_pipeline(
            body,
            grid=(groups,),
            in_specs=[whole((length, width))] + [weight_spec(part) for part in range(3)],
        )(x, w_joint, w_joint, w_joint)

    def gain(self, row):
        small = self.small
        return row_of(small.enc_norms, row) if row < 2 else row_of(small.dec_norms, row - 2)

    def feed_forward(
        self, first_unit, grad, x, gain_row, layer, w_up, w_down, stored, finish, after_adapter=None
    ):
        plan, small, scratch, up_scale = self.plan, self.small, self.scratch, self.up_scale
        total, grad_low = scratch.total, scratch.grad_low
        length, width = x.shape
        n_dp, blocks, rows, _ = stored.active_t.shape

        def body(x_ref, ffn_ref, x_t_ref, up_ref, down_ref, active_t_ref, slope_ref, *more):
            grad_ref = more[0] if more else scratch.grad_b
            step = pl.program_id(0)

            @pl.when(step == 0)
            def _():
                grad = grad_ref[...].astype(WIDE)
                vectors = small.vectors[layer].astype(WIDE)
                lower, upper = small.adapters[layer, 0], small.adapters[layer, 1]
                normed, scale = layer_parts(ffn_ref[...])
                gain = 1.0 + vectors[1:2]
                low = (normed * gain + vectors[2:3]).astype(LOW)
                inner = dot_nt(low, lower)
                cumulative, density = gelu_parts(inner)
                gate = (inner * cumulative).astype(LOW)
                scaled = (grad * up_scale).astype(LOW)
                scratch.adapters[layer, 1] = dot_nn(gate.T, scaled)
                grad_gate = dot_nt(scaled, upper)
                grad_inner = (grad_gate * (cumulative + inner * density)).astype(LOW)
                scratch.adapters[layer, 0] = dot_nn(grad_inner.T, low)
                grad_normed = dot_nn(grad_inner, lower)
                keep = scratch.vectors
                keep[3 * layer : 3 * layer + 1] = jnp.sum(grad, axis=0, keepdims=True)
                keep[3 * layer + 1 : 3 * layer + 2] = jnp.sum(
                    grad_normed * normed, axis=0, keepdims=True
                )
                keep[3 * layer + 2 : 3 * layer + 3] = jnp.sum(grad_normed, axis=0, keepdims=True)
                pulled = grad_normed * gain
                pulled = scale * (
                    pulled
                    - jnp.mean(pulled, axis=-1, keepdims=True)
                    - normed * jnp.mean(pulled * normed, axis=-1, keepdims=True)
                )
                grad_low[...] = (grad + pulled).astype(LOW)
                total[...] = jnp.zeros_like(total)
                if after_adapter is not None:
                    after_adapter()

            unit = first_unit + 2 * step
            plan.put(unit, dot_nn(join_rows(active_t_ref), grad_low[...]))
            self.send(unit)
            grad_active = dot_nt(grad_low[...], down_ref[...])
            grad_before = (grad_active * slope_ref[...].astype(WIDE)).astype(LOW)
            plan.put(unit + 1, dot_nn(x_t_ref[...], grad_before))
            self.send(unit + 1)
            total[...] += dot_nt(grad_before, up_ref[...])

            @pl.when(step == blocks - 1)
            def _():
                grad_values, grad_gain = rms_backward(
                    x_ref[...], self.gain(gain_row), total[...]
                )
                scratch.gains[gain_row : gain_row + 1] = grad_gain
                finish(grad_ref[...].astype(WIDE) + grad_values)

        tokens = whole((length, width))
        pltpu.emit_pipeline(
            body,
            grid=(blocks,),
            in_specs=[
                tokens, tokens, whole((width, length)),
                pl.BlockSpec((width, width), lambda j: (0, j)),
                pl.BlockSpec((width, width), lambda j: (j, 0)),
                pl.BlockSpec((n_dp, 1, rows, length), lambda j: (0, j, 0, 0)),
                pl.BlockSpec((length, width), lambda j: (0, j)),
            ]
            + ([] if grad is None else [tokens]),
        )(
            x, stored.ffn, stored.x_t, w_up, w_down, stored.active_t, stored.slope,
            *([] if grad is None else [grad]),
        )

    def own_rows(self, values, rows_per_task, first, count):
        parts = []
        while count:
            task, offset = divmod(first, rows_per_task)
            some = min(count, rows_per_task - offset)
            if task < self.tasks:
                weight = self.small.wanted[0:1, 2 * task : 2 * task + 1]
                parts.append(values[offset : offset + some] * weight)
            else:
                parts.append(jnp.zeros((some, values.shape[1]), WIDE))
            first, count = first + some, count - some
        return parts[0] if len(parts) == 1 else jnp.concatenate(parts, axis=0)

    def send_adapters(self, unit):
        plan, kept, size = self.plan, self.scratch.adapters, self.bottleneck
        values = jnp.concatenate(
            [kept[layer, part, :size] for layer in range(kept.shape[0]) for part in range(2)], axis=0
        )
        target = plan.refs.unit.at[unit % plan.unit_ring]
        for i in range(plan.n_dp):
            part = self.own_rows(values, values.shape[0], i * plan.rows, plan.rows)
            target[plan.positions[i]] = part.astype(LOW)
        self.send(unit)

    def send_vectors(self, unit, vector_rows):
        plan = self.plan
        values = self.scratch.vectors[:6]
        spare = -vector_rows % 16
        for i in range(plan.n_dp):
            part = self.own_rows(values, 6, i * vector_rows, vector_rows)
            if spare:
                part = jnp.concatenate([part, jnp.zeros((spare, plan.width), WIDE)], axis=0)
            target = plan.refs.unit.at[unit % plan.unit_ring, plan.positions[i]]
            target[: part.shape[0]] = part.astype(LOW)
        self.send(unit)


def backward_kernel(plan, up_scale, bottleneck, tasks, vector_rows, trees, *leaves):
    counts = [tree.num_leaves for tree in trees]
    parts, start = [], 0
    for tree, count in zip(trees, counts):
        parts.append(jax.tree.unflatten(tree, leaves[start : start + count]))
        start += count
    refs, out, scratch = parts
    plan.bind(scratch.transfer)
    plan.barrier()
    work = Backward(plan, up_scale, bottleneck, tasks, refs, refs.small, scratch, out.sums)
    shared = Shared(plan, scratch.shared)
    gains = Gains(plan, scratch.own_gains)
    grad_a, grad_b = scratch.grad_a, scratch.grad_b

    def into(ref):
        def finish(values):
            ref[...] = values.astype(ref.dtype)

        return finish

    def adapters():
        work.send_adapters(12)
        work.send_vectors(13, vector_rows)

    def share():
        shared.start(out.sums.at[12], out.sums.at[13, pl.ds(0, 16)])

    early = 13 + plan.at[plan.final] <= 26
    work.feed_forward(
        0, refs.cotangent, refs.cross_hidden, 4, 1, refs.dec_up, refs.dec_down, refs.dec_ffn,
        into(grad_a),
    )
    work.attention(
        8, grad_a, (3, 5), refs.dec_hidden, refs.encoded, refs.cross_attn,
        ((refs.dec_cross_q, 0), (refs.dec_cross_kv, 0), (refs.dec_cross_kv, 1), refs.dec_cross_proj),
        into(grad_a),
    )
    work.feed_forward(
        14, None, refs.enc_hidden, 1, 0, refs.enc_up, refs.enc_down, refs.enc_ffn, into(grad_b),
        after_adapter=adapters,
    )
    work.attention(
        22, grad_a, None, refs.dec_rows, None, refs.dec_attn, (None, None, None, refs.dec_self_proj),
        scratch.joint_dec,
    )
    work.attention(
        26, grad_b, None, refs.enc_rows, None, refs.enc_attn, (None, None, None, refs.enc_proj),
        scratch.joint_enc, after_first=share if early else None,
    )
    work.input_grad(
        30, scratch.joint_dec, grad_a, 2, refs.dec_rows, refs.dec_qkv, out.grad_dec_rows
    )
    work.input_grad(
        33, scratch.joint_enc, grad_b, 0, refs.enc_rows, refs.enc_qkv, out.grad_enc_rows
    )
    gains.start(scratch.gains)
    plan.drain(36, out.sums)
    if not early:
        share()
    gains.finish(out.gains)
    shared.finish(out.pair_weights, out.pair_vectors)


def backward(operands, features, up_scale, bottleneck, tasks, vector_rows):
    n_dp, n_gen = lax.axis_size("dp"), lax.axis_size("gen")
    length, width = operands.enc_rows.shape
    rows = width // n_dp
    plan = Transfer(30, (13,), n_dp, n_gen, rows, width, LAGS)

    def blocked(fed):
        return fed._replace(active_t=fed.active_t.reshape(n_dp, -1, rows, length))

    operands = operands._replace(
        enc_ffn=blocked(operands.enc_ffn), dec_ffn=blocked(operands.dec_ffn)
    )
    tokens = pltpu.VMEM((length, width), WIDE)
    joint = pltpu.VMEM((3 * width // GROUP, length, GROUP), LOW)
    shared_rows = rows + 16
    held = Held(
        total=tokens,
        joint_dec=joint,
        joint_enc=joint,
        grad_low=pltpu.VMEM((length, width), LOW),
        grad_a=tokens,
        grad_b=tokens,
        adapters=pltpu.VMEM(operands.small.adapters.shape, WIDE),
        vectors=pltpu.VMEM((8, width), WIDE),
        gains=pltpu.VMEM((8, width), WIDE),
        transfer=plan.scratch(),
        shared=Shared.scratch(n_dp, shared_rows, features),
        own_gains=Gains.scratch(n_dp),
    )
    shape = jax.ShapeDtypeStruct
    results = Results(
        sums=shape((plan.units, rows, width), LOW),
        pair_weights=shape((n_dp, rows, features), LOW),
        pair_vectors=shape((n_dp, 16, features), LOW),
        gains=shape((8, 128), WIDE),
        grad_dec_rows=shape((length, width), LOW),
        grad_enc_rows=shape((length, width), LOW),
    )
    in_vmem = pl.BlockSpec(memory_space=pltpu.VMEM)
    in_hbm = pl.BlockSpec(memory_space=pl.ANY)
    specs = jax.tree.map(lambda _: in_hbm, operands)
    specs = specs._replace(small=jax.tree.map(lambda _: in_vmem, operands.small))
    flat, in_tree = jax.tree.flatten(operands)
    scratch, scratch_tree = jax.tree.flatten(held)
    out, out_tree = jax.tree.flatten(results)
    remote = n_dp * n_gen > 1
    outs = pl.pallas_call(
        functools.partial(
            backward_kernel, plan, up_scale, bottleneck, tasks, vector_rows,
            (in_tree, out_tree, scratch_tree),
        ),
        in_specs=jax.tree.leaves(specs),
        out_specs=[in_vmem] * len(out),
        out_shape=out,
        scratch_shapes=scratch,
        compiler_params=pltpu.CompilerParams(
            vmem_limit_bytes=VMEM_LIMIT,
            **(dict(collective_id=0, has_side_effects=True) if remote else {}),
        ),
        cost_estimate=pl.CostEstimate(
            flops=100 * length * width * width, bytes_accessed=160 * width * width,
            transcendentals=0,
        ),
        name="backward",
    )(*flat)
    return jax.tree.unflatten(out_tree, outs)


class Gradients(NamedTuple):
    enc_norms: object
    enc_qkv: object
    enc_proj: object
    enc_up: object
    enc_down: object
    dec_norms: object
    dec_qkv: object
    dec_self_proj: object
    dec_cross_q: object
    dec_cross_kv: object
    dec_cross_proj: object
    dec_up: object
    dec_down: object


def unpack_kernel(sums_ref, gains_ref, dec_ref, enc_ref, *outs):
    out = Gradients(*outs[:13])
    outs[13][...] = dec_ref[...]
    outs[14][...] = enc_ref[...]
    size = out.enc_norms.shape[1]
    gains = gains_ref[...]

    @pl.when(pl.program_id(0) == 0)
    def _():
        out.enc_norms[...] = gains[0:2, :size]
        out.dec_norms[...] = gains[2:6, :size]

    def plain(target, unit):
        target[...] = sums_ref[unit].astype(WIDE)

    def joint(target, first, parts):
        for at, part in enumerate(parts):
            for g in range(3):
                start = (3 * at + g) * GROUP
                target[:, start : start + GROUP] = sums_ref[
                    first + g, :, part * GROUP : (part + 1) * GROUP
                ].astype(WIDE)

    def beside(target, first):
        width = sums_ref.shape[2]
        for j in range(target.shape[1] // width):
            target[:, j * width : (j + 1) * width] = sums_ref[first + 2 * j].astype(WIDE)

    def below(target, first):
        for j in range(target.shape[0]):
            target[j] = sums_ref[first + 2 * j].astype(WIDE)

    below(out.dec_down, 0)
    beside(out.dec_up, 1)
    plain(out.dec_cross_proj, 8)
    joint(out.dec_cross_q, 9, (0,))
    joint(out.dec_cross_kv, 9, (1, 2))
    below(out.enc_down, 14)
    beside(out.enc_up, 15)
    plain(out.dec_self_proj, 22)
    joint(out.dec_qkv, 23, (0, 1, 2))
    plain(out.enc_proj, 26)
    joint(out.enc_qkv, 27, (0, 1, 2))


def unpack(sums, gains, grad_dec_rows, grad_enc_rows, inner):
    units, rows, width = sums.shape
    length = grad_dec_rows.shape[0]
    steps = rows // 32 if rows % 32 == 0 else 1
    block = rows // steps
    while length % (16 * steps):
        steps, block = 1, rows
    shape = jax.ShapeDtypeStruct

    def matrix(columns):
        return shape((rows, columns), WIDE), pl.BlockSpec((block, columns), lambda i: (i, 0))

    downs = inner // width
    down = (
        shape((downs, rows, width), WIDE),
        pl.BlockSpec((downs, block, width), lambda i: (0, i, 0)),
    )
    tokens = pl.BlockSpec((length // steps, width), lambda i: (i, 0))

    def norms(count):
        return shape((count, rows), WIDE), whole((count, rows))

    made = Gradients(
        enc_norms=norms(2), enc_qkv=matrix(3 * width), enc_proj=matrix(width),
        enc_up=matrix(inner), enc_down=down, dec_norms=norms(4), dec_qkv=matrix(3 * width),
        dec_self_proj=matrix(width), dec_cross_q=matrix(width), dec_cross_kv=matrix(2 * width),
        dec_cross_proj=matrix(width), dec_up=matrix(inner), dec_down=down,
    )
    outs = pl.pallas_call(
        unpack_kernel,
        grid=(steps,),
        in_specs=[
            pl.BlockSpec((units, block, width), lambda i: (0, i, 0)),
            whole(gains.shape),
            tokens,
            tokens,
        ],
        out_specs=[spec for _, spec in made] + [tokens, tokens],
        out_shape=[one for one, _ in made] + [shape((length, width), LOW)] * 2,
        compiler_params=pltpu.CompilerParams(vmem_limit_bytes=VMEM_LIMIT),
        cost_estimate=pl.CostEstimate(
            flops=0, bytes_accessed=6 * units * rows * width, transcendentals=0
        ),
        name="unpack",
    )(sums, gains, grad_dec_rows, grad_enc_rows)
    grads = Gradients(*outs[:13])
    grads = grads._replace(
        enc_down=grads.enc_down.reshape(-1, width), dec_down=grads.dec_down.reshape(-1, width)
    )
    return grads, outs[13], outs[14]


def gelu_exact(values):
    return jax.nn.gelu(values, approximate=False)


def body(
    enc_input,
    dec_input,
    enc_segments,
    dec_segments,
    task_ids,
    cotangent,
    enc_norms,
    enc_qkv,
    enc_proj,
    enc_up,
    enc_down,
    dec_norms,
    dec_qkv,
    dec_self_proj,
    dec_cross_q,
    dec_cross_kv,
    dec_cross_proj,
    dec_up,
    dec_down,
    task_emb,
    layer_emb,
    proj_task,
    gen_weight,
    gen_vector,
):
    _, length, width = enc_input.shape
    layer_count = layer_emb.shape[0]
    pair_count = task_emb.shape[0] * layer_count
    bottleneck = gen_weight.shape[1] // 2
    up_scale = (width / bottleneck) ** 0.5

    def source_of(task_table, layer_table, projection):
        mixed_in = (
            jnp.dot(task_table, projection, precision=HIGHEST)[:, None, :] + layer_table[None, :, :]
        )
        return gelu_exact(mixed_in).reshape(pair_count, -1)

    source, source_pull = jax.vjp(source_of, task_emb, layer_emb, proj_task)
    source_low = source.astype(LOW)
    pieces, more_pieces = [
        jnp.einsum("th,hkd->tkd", source_low, part, preferred_element_type=WIDE).astype(LOW)
        for part in (gen_weight, gen_vector)
    ]
    first_pair = task_ids[0] * layer_count
    wanted = jnp.arange(8)[:, None] + first_pair == jnp.arange(128)[None, :]
    wanted = wanted.astype(WIDE)

    enc_rows, dec_rows = enc_input[0], dec_input[0]
    enc_joint = [(enc_qkv, 0), (enc_qkv, 1), (enc_qkv, 2)]
    dec_joint = [(dec_qkv, 0), (dec_qkv, 1), (dec_qkv, 2)]
    cross_joint = [(dec_cross_q, 0), (dec_cross_kv, 0), (dec_cross_kv, 1)]
    enc_hidden, enc_stored, adapters, vectors = attention_forward(
        enc_rows, enc_norms, (0, 0), None, enc_segments, enc_segments, enc_joint, enc_proj, False,
        gather=(wanted, pieces, more_pieces, bottleneck),
    )
    dec_hidden, dec_stored = attention_forward(
        dec_rows, dec_norms, (0, 0), None, dec_segments, dec_segments, dec_joint, dec_self_proj, True
    )
    encoded, enc_ffn_stored = feed_forward(
        enc_hidden, enc_norms, 1, enc_up, enc_down, adapters, vectors, 0, up_scale, WIDE
    )
    cross_hidden, cross_stored = attention_forward(
        dec_hidden, dec_norms, (1, 3), encoded, dec_segments, enc_segments, cross_joint,
        dec_cross_proj, False,
    )
    decoded, dec_ffn_stored = feed_forward(
        cross_hidden, dec_norms, 2, dec_up, dec_down, adapters, vectors, 1, up_scale, LOW
    )

    n_dp = lax.axis_size("dp")
    rows = width // n_dp
    features = gen_weight.shape[2]
    vector_rows = -(-pair_count * 3 // n_dp)
    small = Small(enc_norms, dec_norms, adapters, vectors, wanted)
    operands = Operands(
        cotangent[0], cross_hidden, dec_hidden, encoded, enc_hidden, dec_rows, enc_rows,
        enc_qkv, enc_proj, enc_up, enc_down, dec_qkv, dec_self_proj, dec_cross_q, dec_cross_kv,
        dec_cross_proj, dec_up, dec_down,
        enc_stored, dec_stored, cross_stored, enc_ffn_stored, dec_ffn_stored, small,
    )
    result = backward(
        operands, features, up_scale, bottleneck, task_emb.shape[0], vector_rows
    )
    pair_weights = result.pair_weights.reshape(pair_count, 2 * bottleneck, features)
    pair_vectors = result.pair_vectors[:, :vector_rows].reshape(-1, features)
    pair_vectors = pair_vectors[: pair_count * 3].reshape(pair_count, 3, features)
    grad_gen_weight, grad_gen_vector = [
        jnp.einsum("th,tkd->hkd", source_low, part, preferred_element_type=WIDE)
        for part in (pair_weights, pair_vectors)
    ]
    part_source = sum(
        jnp.einsum("tkd,hkd->th", part, made, preferred_element_type=WIDE)
        for part, made in ((pair_weights, gen_weight), (pair_vectors, gen_vector))
    )
    summed = sum_gen(jnp.concatenate([part_source, result.gains], axis=0))
    grad_source, gains = summed[:pair_count], summed[pair_count:]
    grad_task_emb, grad_layer_emb, grad_proj_task = source_pull(grad_source)

    grads, grad_dec_rows, grad_enc_rows = unpack(
        result.sums, gains, result.grad_dec_rows, result.grad_enc_rows, enc_up.shape[1]
    )
    return (
        decoded[None],
        grad_enc_rows[None],
        grad_dec_rows[None],
        *grads,
        grad_task_emb,
        grad_layer_emb,
        grad_proj_task,
        grad_gen_weight,
        grad_gen_vector,
    )


def solution(mesh):
    in_specs = (
        P(("dp", "gen"), None, None),
        P(("dp", "gen"), None, None),
        P(("dp", "gen"), None),
        P(("dp", "gen"), None),
        P(("dp", "gen")),
        P(("dp", "gen"), None, None),
        P(),
        P(),
        P(),
        P(),
        P(),
        P(),
        P(),
        P(),
        P(),
        P(),
        P(),
        P(),
        P(),
        P(),
        P(),
        P(),
        P(None, None, "gen"),
        P(None, None, "gen"),
    )
    out_specs = (
        P(("dp", "gen"), None, None),
        P(("dp", "gen"), None, None),
        P(("dp", "gen"), None, None),
        P(None, "dp"),
        P("dp", None),
        P("dp", None),
        P("dp", None),
        P("dp", None),
        P(None, "dp"),
        P("dp", None),
        P("dp", None),
        P("dp", None),
        P("dp", None),
        P("dp", None),
        P("dp", None),
        P("dp", None),
        P(),
        P(),
        P(),
        P(None, None, "gen"),
        P(None, None, "gen"),
    )
    return jax.shard_map(body, mesh=mesh, in_specs=in_specs, out_specs=out_specs, check_vma=False)
```

```python
import functools
from typing import NamedTuple

import jax
import jax.numpy as jnp
from jax import lax
from jax.experimental import pallas as pl
from jax.experimental.pallas import tpu as pltpu
from jax.sharding import PartitionSpec as P

H = 12
HD = 64
GROUP = 4 * HD
VMEM_LIMIT = 62 * 1024 * 1024
LAGS = (1, 2, 2, 2)
HIGHEST = lax.Precision.HIGHEST
LOW = jnp.bfloat16
WIDE = jnp.float32


def dot_nn(left_side, right_side):
    return jnp.dot(left_side, right_side, preferred_element_type=WIDE)


def dot_nt(left_side, right_side):
    return lax.dot_general(
        left_side, right_side, (((1,), (1,)), ((), ())), preferred_element_type=WIDE
    )


def gelu_parts(values):
    size = jnp.abs(values)
    density = jnp.exp(values * values * -0.5) * 0.3989422804014327
    bottom = 1.0 + 0.2316419 * size
    inverse = pl.reciprocal(bottom, approx=True)
    inverse = inverse * (2.0 - bottom * inverse)
    series = 1.330274429 * inverse - 1.821255978
    series = series * inverse + 1.781477937
    series = series * inverse - 0.356563782
    series = series * inverse + 0.31938153
    tail = series * inverse * density
    return jnp.where(values < 0.0, tail, 1.0 - tail), density


def rms_scale(values):
    return lax.rsqrt(jnp.mean(values * values, axis=-1, keepdims=True) + 1e-06)


def rms_backward(values, norm_gain, grad):
    scale = rms_scale(values)
    normed = values * scale
    pulled = grad * norm_gain
    inner = jnp.mean(normed * pulled, axis=-1, keepdims=True)
    grad_values = scale * (pulled - normed * inner)
    return grad_values, jnp.sum(grad * normed, axis=0, keepdims=True)


def segment_bias(seg_query, seg_key, causal):
    length = seg_query.shape[1]
    column = jnp.broadcast_to(seg_query.astype(WIDE), (128, length)).T[:, :1]
    allowed = column == seg_key.astype(WIDE)
    if causal:
        query_place = lax.broadcasted_iota(jnp.int32, (length, length), 0)
        key_place = lax.broadcasted_iota(jnp.int32, (length, length), 1)
        allowed = allowed & (query_place >= key_place)
    return jnp.where(allowed, 0.0, -1e30)


def row_of(ref, row):
    return ref[row : row + 1].astype(WIDE)


def first_half(shape):
    return lax.broadcasted_iota(jnp.int32, shape, 1) < HD


class Attended(NamedTuple):
    x_t: object
    memory_t: object
    q_t: object
    keys: object
    values: object
    mixed_t: object
    probs: object


class Fed(NamedTuple):
    ffn: object
    x_t: object
    active_t: object
    slope: object


class Gather:
    def __init__(self, n_gen, bottleneck, refs):
        self.n_gen, self.bottleneck, self.line = n_gen, bottleneck, lax.axis_index("gen")
        (
            self.weights, self.pieces, self.more, self.adapters, self.vectors,
            self.asked, self.chosen, self.arrived, self.sems,
        ) = refs

    @staticmethod
    def scratch(n_gen, features):
        return (
            pltpu.VMEM((n_gen, 8, 128), WIDE),
            pltpu.VMEM((n_gen, 2, 64, features), LOW),
            pltpu.VMEM((n_gen, 2, 64, features), LOW),
            pltpu.SemaphoreType.DMA((4, max(n_gen - 1, 1))),
        )

    def ask(self, k):
        sems = self.sems
        return gen_copy(
            self.weights, self.asked, sems.at[0], sems.at[1], self.line, k, self.n_gen
        )

    def answer(self, k):
        sems = self.sems
        return gen_copy(
            self.chosen.at[k], self.arrived, sems.at[2], sems.at[3], self.line, k, self.n_gen
        )

    def pick(self, target, weights):
        for layer in range(2):
            start = 0
            for source in (self.pieces, self.more):
                pairs, rows, features = source.shape
                total = jnp.zeros((rows, features), WIDE)
                for pair in range(pairs):
                    weight = weights[layer : layer + 1, pair : pair + 1]
                    total = total + weight * source[pair].astype(WIDE)
                target[layer, start : start + rows] = total.astype(LOW)
                start += rows

    def begin(self, step):
        if self.n_gen > 1:
            pl.when(step == 0)(lambda: gen_greet(self.line, self.n_gen))

    def end(self, step, steps):
        n_gen, size = self.n_gen, self.bottleneck

        @pl.when(step == 0)
        def _():
            if n_gen > 1:
                gen_greeted(n_gen)
            for k in range(1, n_gen):
                self.ask(k).start()

        @pl.when(step == 1)
        def _():
            for k in range(1, n_gen):
                self.ask(k).wait()
            for k in range(1, n_gen):
                self.pick(self.chosen.at[k], self.asked[(self.line + k) % n_gen])
                self.answer(k).start()
            self.pick(self.arrived.at[self.line], self.weights[...])

        @pl.when(step == steps - 1)
        def _():
            for k in range(1, n_gen):
                self.answer(k).wait()
            rows = 2 * size + 3
            self.adapters[...] = jnp.zeros_like(self.adapters)
            for layer in range(2):
                joined = jnp.concatenate(
                    [self.arrived[j, layer, 0:rows].astype(WIDE) for j in range(n_gen)], axis=1
                ).astype(LOW)
                self.adapters[layer, 0, 0:size] = joined[0:size]
                self.adapters[layer, 1, 0:size] = joined[size : 2 * size]
                self.vectors[layer] = joined[2 * size : 2 * size + 3]


def attention_forward_kernel(
    cross, causal, gather, gain_rows,
    x_ref, gain_ref, memory_ref, memory_gain_ref, seg_q_ref, seg_k_ref,
    wq_ref, wk_ref, wv_ref, wo_ref, *refs,
):
    step = pl.program_id(0)
    more_in = refs[:3] if gather else ()
    refs = refs[len(more_in) :]
    hidden_ref, x_t_ref, memory_t_ref, q_t_ref, k_ref, v_ref, mixed_t_ref, probs_ref = refs[:8]
    more_out = refs[8:10] if gather else ()
    refs = refs[8 + len(more_out) :]
    x_low, memory_low, bias = refs[:3]
    if gather:
        work = Gather(*gather, more_in + more_out + refs[3:])
        work.begin(step)

    @pl.when(step == 0)
    def _():
        values = x_ref[...].astype(WIDE)
        hidden_ref[...] = values
        normed = (values * rms_scale(values) * row_of(gain_ref, gain_rows[0])).astype(LOW)
        x_low[...] = normed
        x_t_ref[...] = normed.T
        if cross:
            values = memory_ref[...].astype(WIDE)
            normed = (values * rms_scale(values) * row_of(memory_gain_ref, gain_rows[1])).astype(LOW)
            memory_low[...] = normed
            memory_t_ref[...] = normed.T
        bias[...] = segment_bias(seg_q_ref[...], seg_k_ref[...], causal)

    source_low = memory_low if cross else x_low
    queries = dot_nn(x_low[...], wq_ref[...]).astype(LOW)
    q_t_ref[...] = queries.T
    k_ref[...] = dot_nn(source_low[...], wk_ref[...]).astype(LOW)
    v_ref[...] = dot_nn(source_low[...], wv_ref[...]).astype(LOW)
    scaled = queries * LOW(HD ** (-0.5))
    length = scaled.shape[0]
    lanes = first_half((length, 2 * HD))
    parts = []
    for pair in range(2):
        columns = slice(pair * 2 * HD, (pair + 1) * 2 * HD)
        two = scaled[:, columns]
        keys = k_ref[:, columns]
        values = v_ref[:, columns]
        halves = []
        for side in range(2):
            mine = jnp.where(lanes if side == 0 else ~lanes, two, LOW(0))
            scores = dot_nt(mine, keys) + bias[...]
            raised = jnp.exp(scores - jnp.max(scores, axis=-1, keepdims=True))
            total = jnp.sum(raised, axis=-1, keepdims=True)
            probs = (raised * (1.0 / total)).astype(LOW)
            probs_ref[2 * pair + side] = probs
            halves.append(dot_nn(probs, values))
        parts.append(jnp.where(lanes, halves[0], halves[1]).astype(LOW))
    mixed = jnp.concatenate(parts, axis=1)
    mixed_t_ref[...] = mixed.T
    hidden_ref[...] += dot_nn(mixed, wo_ref[...])
    if gather:
        work.end(step, pl.num_programs(0))


def whole(shape):
    return pl.BlockSpec(shape, lambda *_: (0,) * len(shape))


def attention_forward(
    x, gains, gain_rows, memory, seg_q, seg_k, weights, w_out, causal, gather=None
):
    n_gen = lax.axis_size("gen")
    more_in, more_out, more_scratch, asked = (), (), (), None
    if gather is not None:
        wanted, pieces, more_pieces, bottleneck = gather
        more_in = (wanted, pieces, more_pieces)
        padded = -bottleneck % 16 + bottleneck
        more_out = (
            jax.ShapeDtypeStruct((2, 2, padded, x.shape[1]), LOW),
            jax.ShapeDtypeStruct((2, 3, x.shape[1]), LOW),
        )
        more_scratch = Gather.scratch(n_gen, pieces.shape[2])
        asked = (n_gen, bottleneck)
    remote = gather is not None and n_gen > 1
    cross = memory is not None
    length, width = x.shape
    groups = width // GROUP
    if not cross:
        memory = x
    shape = jax.ShapeDtypeStruct
    columns = pl.BlockSpec((length, GROUP), lambda g: (0, g))
    rows = pl.BlockSpec((GROUP, length), lambda g: (g, 0))

    def weight_spec(offset):
        return pl.BlockSpec((width, GROUP), lambda g: (0, offset + g))

    memory_spec = whole((length, width)) if cross else whole((16, 128))
    memory_t_shape = (width, length) if cross else (16, 128)
    outs = pl.pallas_call(
        functools.partial(attention_forward_kernel, cross, causal, asked, gain_rows),
        grid=(groups,),
        in_specs=[
            whole((length, width)),
            whole(gains.shape),
            memory_spec,
            whole(gains.shape),
            whole((1, length)),
            whole((1, length)),
            weight_spec(weights[0][1] * groups),
            weight_spec(weights[1][1] * groups),
            weight_spec(weights[2][1] * groups),
            pl.BlockSpec((GROUP, width), lambda g: (g, 0)),
        ]
        + [whole(one.shape) for one in more_in],
        out_specs=[
            whole((length, width)),
            whole((width, length)),
            whole(memory_t_shape),
            rows,
            columns,
            columns,
            rows,
            pl.BlockSpec((4, length, length), lambda g: (g, 0, 0)),
        ]
        + [whole(one.shape) for one in more_out],
        out_shape=[
            shape((length, width), WIDE),
            shape((width, length), LOW),
            shape(memory_t_shape, LOW),
            shape((width, length), LOW),
            shape((length, width), LOW),
            shape((length, width), LOW),
            shape((width, length), LOW),
            shape((H, length, length), LOW),
            *more_out,
        ],
        scratch_shapes=[
            pltpu.VMEM((length, width), LOW),
            pltpu.VMEM((length, width) if cross else (16, 128), LOW),
            pltpu.VMEM((length, length), WIDE),
            *more_scratch,
        ],
        compiler_params=pltpu.CompilerParams(
            vmem_limit_bytes=VMEM_LIMIT,
            **(dict(collective_id=1, has_side_effects=True) if remote else {}),
        ),
        cost_estimate=pl.CostEstimate(
            flops=2 * length * width * (4 * width + 2 * length),
            bytes_accessed=2 * (4 * width * width + H * length * length + 8 * length * width),
            transcendentals=H * length * length,
        ),
        name="attention_forward",
    )(x, gains, memory, gains, seg_q, seg_k,
      weights[0][0], weights[1][0], weights[2][0], w_out, *more_in)
    hidden, x_t, memory_t, q_t, keys, values, mixed_t, probs = outs[:8]
    stored = Attended(x_t, memory_t if cross else None, q_t, keys, values, mixed_t, probs)
    return (hidden, stored) + tuple(outs[8:])


def layer_parts(values):
    centred = values - jnp.mean(values, axis=-1, keepdims=True)
    scale = lax.rsqrt(jnp.mean(centred * centred, axis=-1, keepdims=True) + 1e-05)
    return centred * scale, scale


def feed_forward_kernel(
    up_scale, layer, gain_row,
    x_ref, gain_ref, up_ref, down_ref, adapter_ref, vector_ref,
    out_ref, ffn_ref, x_t_ref, active_t_ref, slope_ref,
    x_low, total,
):
    step = pl.program_id(0)

    @pl.when(step == 0)
    def _():
        values = x_ref[...]
        normed = (values * rms_scale(values) * row_of(gain_ref, gain_row)).astype(LOW)
        x_low[...] = normed
        x_t_ref[...] = normed.T
        total[...] = jnp.zeros_like(total)

    before = dot_nn(x_low[...], up_ref[...])
    cumulative, density = gelu_parts(before)
    active = (before * cumulative).astype(LOW)
    slope_ref[...] = (cumulative + before * density).astype(LOW)
    active_t_ref[...] = active.T
    total[...] += dot_nn(active, down_ref[...])

    @pl.when(step == pl.num_programs(0) - 1)
    def _():
        ffn = total[...]
        ffn_ref[...] = ffn
        normed, _ = layer_parts(ffn)
        vectors = vector_ref[layer].astype(WIDE)
        low = (normed * (1.0 + vectors[1:2]) + vectors[2:3]).astype(LOW)
        inner = dot_nt(low, adapter_ref[layer, 0])
        gate = (inner * gelu_parts(inner)[0]).astype(LOW)
        adapted = dot_nn(gate, adapter_ref[layer, 1]) * up_scale + vectors[0:1]
        out_ref[...] = (x_ref[...] + ffn + adapted).astype(out_ref.dtype)


def feed_forward(
    x, gains, gain_row, w_up, w_down, adapter, vectors, layer, up_scale, out_dtype, blocks=4
):
    length, width = x.shape
    inner = w_up.shape[1]
    block = inner // blocks
    shape = jax.ShapeDtypeStruct
    out, ffn, x_t, active_t, slope = pl.pallas_call(
        functools.partial(feed_forward_kernel, up_scale, layer, gain_row),
        grid=(blocks,),
        in_specs=[
            whole((length, width)),
            whole(gains.shape),
            pl.BlockSpec((width, block), lambda j: (0, j)),
            pl.BlockSpec((block, width), lambda j: (j, 0)),
            whole(adapter.shape),
            whole(vectors.shape),
        ],
        out_specs=[
            whole((length, width)),
            whole((length, width)),
            whole((width, length)),
            pl.BlockSpec((block, length), lambda j: (j, 0)),
            pl.BlockSpec((length, block), lambda j: (0, j)),
        ],
        out_shape=[
            shape((length, width), out_dtype),
            shape((length, width), WIDE),
            shape((width, length), LOW),
            shape((inner, length), LOW),
            shape((length, inner), LOW),
        ],
        scratch_shapes=[pltpu.VMEM((length, width), LOW), pltpu.VMEM((length, width), WIDE)],
        compiler_params=pltpu.CompilerParams(vmem_limit_bytes=VMEM_LIMIT),
        cost_estimate=pl.CostEstimate(
            flops=4 * length * width * inner,
            bytes_accessed=4 * width * inner + 4 * length * inner + 12 * length * width,
            transcendentals=length * inner,
        ),
        name="feed_forward",
    )(x, gains, w_up, w_down, adapter, vectors)
    return out, Fed(ffn, x_t, active_t, slope)


def join_rows(ref):
    blocks, _, rows, columns = ref.shape
    if rows % 16 == 0:
        return ref[...].reshape(blocks * rows, columns)
    parts = [ref[i, 0].astype(WIDE) for i in range(blocks)]
    return jnp.concatenate(parts, axis=0).astype(LOW)


def power_of_two(least):
    return 1 << (least - 1).bit_length()


class TransferRefs(NamedTuple):
    unit: object
    held: object
    into: object
    total: object
    line: object
    send: object
    recv: object


class Transfer:
    def __init__(self, units, small, n_dp, n_gen, rows, width, lags):
        self.units, self.small = units, small
        self.n_dp, self.n_gen = n_dp, n_gen
        self.rows, self.width = rows, width
        self.bits = n_dp.bit_length() - 1
        self.final = self.bits + max(n_gen - 1, 0)
        first, between, last, along = lags
        self.lags = [first] + [between] * (self.bits - 2) + [last] + [along] * (n_gen - 1)
        self.at = [sum(self.lags[:s]) for s in range(self.final + 1)]
        self.slots = units + self.at[self.final]
        self.ring = 2 * max(first, between, last) + 1
        self.line_ring = max(2 * along + 1, along * (n_gen - 1))
        self.unit_ring = power_of_two(first + 2)
        self.sum_ring = power_of_two(along * max(n_gen - 1, 1) + 1)

    def scratch(self):
        block = (self.rows, self.width)
        bits, lags, ring = self.bits, self.lags, self.ring
        stages = max(bits + self.n_gen - 1, 1)
        return TransferRefs(
            unit=pltpu.VMEM((self.unit_ring, self.n_dp) + block, LOW),
            held=[pltpu.VMEM((lags[s], self.n_dp >> s) + block, LOW) for s in range(1, bits)],
            into=[pltpu.VMEM((ring, self.n_dp >> (s + 1)) + block, LOW) for s in range(bits)],
            total=pltpu.VMEM((self.sum_ring,) + block, LOW),
            line=[pltpu.VMEM((self.line_ring,) + block, LOW) for _ in range(self.n_gen - 1)],
            send=pltpu.SemaphoreType.DMA((stages, max(ring, self.line_ring))),
            recv=pltpu.SemaphoreType.DMA((stages, max(ring, self.line_ring))),
        )

    def bind(self, refs):
        self.refs = refs
        self.place = lax.axis_index("dp")
        self.at_line = lax.axis_index("gen")
        self.core = self.place % 2
        self.partners = [self.partner(step) for step in range(self.bits)]
        self.positions = [self.position(index) for index in range(self.n_dp)]

    def partner(self, step):
        if step == 0:
            return self.place + 1 - 2 * self.core
        one, other = 1 << step, 1 << (self.bits - step)
        flipped = [self.place + power * (1 - 2 * ((self.place // power) % 2)) for power in (one, other)]
        return jnp.where(self.core == 0, *flipped)

    def position(self, index):
        if self.bits == 0:
            return 0
        core = index % 2
        place = jnp.where(self.core == core, 1 << (self.bits - 1), 0)
        for step in range(1, self.bits):
            power = 1 << (step if core == 0 else self.bits - step)
            differs = (self.place // power + index // power) % 2
            place = place + differs * (1 << (self.bits - 1 - step))
        return place

    def barrier(self):
        if self.bits + self.n_gen == 1:
            return
        semaphore = pltpu.get_barrier_semaphore()
        for k in range(1, self.n_dp):
            pl.semaphore_signal(
                semaphore, inc=1,
                device_id={"dp": (self.place + k) % self.n_dp, "gen": self.at_line},
                device_id_type=pl.DeviceIdType.MESH,
            )
        amount = self.n_dp - 1
        if self.n_gen > 1:
            ends = ((self.at_line > 0, -1), (self.at_line < self.n_gen - 1, 1))
            for there, towards in ends:
                @pl.when(there)
                def _():
                    pl.semaphore_signal(
                        semaphore, inc=1,
                        device_id={"dp": self.place, "gen": self.at_line + towards},
                        device_id_type=pl.DeviceIdType.MESH,
                    )
                amount = amount + jnp.where(there, 1, 0)
        pl.semaphore_wait(semaphore, amount)

    def sized(self, unit, act):
        if isinstance(unit, int):
            act(16 if unit in self.small else self.rows)
            return
        is_small = unit == self.small[0]
        for one in self.small[1:]:
            is_small = is_small | (unit == one)
        pl.when(is_small)(functools.partial(act, 16))
        pl.when(~is_small)(functools.partial(act, self.rows))

    def halving(self, step, unit, rows):
        refs, many = self.refs, self.n_dp >> (step + 1)
        if step == 0:
            source = refs.unit.at[unit % self.unit_ring, pl.ds(0, many), pl.ds(0, rows)]
        else:
            source = refs.held[step - 1].at[unit % self.lags[step], pl.ds(many, many), pl.ds(0, rows)]
        slot = unit % self.ring
        return pltpu.make_async_remote_copy(
            src_ref=source,
            dst_ref=refs.into[step].at[slot, :, pl.ds(0, rows)],
            send_sem=refs.send.at[step, slot],
            recv_sem=refs.recv.at[step, slot],
            device_id={"dp": self.partners[step], "gen": self.at_line},
            device_id_type=pl.DeviceIdType.MESH,
        )

    def along(self, i, unit, towards, rows):
        slot = unit % self.line_ring
        step = self.bits + i
        return pltpu.make_async_remote_copy(
            src_ref=self.refs.total.at[unit % self.sum_ring, pl.ds(0, rows)],
            dst_ref=self.refs.line[i].at[slot, pl.ds(0, rows)],
            send_sem=self.refs.send.at[step, slot],
            recv_sem=self.refs.recv.at[step, slot],
            device_id={"dp": self.place, "gen": self.at_line + towards},
            device_id_type=pl.DeviceIdType.MESH,
        )

    def roles(self, i):
        count = self.n_gen
        half = count // 2
        if i < half - 1:
            return [(i, 1), (count - 1 - i, -1)], [i + 1, count - 2 - i], True
        if i == half - 1:
            return [(half - 1, 1), (half, -1)], [half - 1, half], True
        j = count - 2 - i
        return [(j + 1, -1), (count - 2 - j, 1)], [j, count - 1 - j], False

    def stage(self, s, unit, out_ref):
        refs, bits = self.refs, self.bits
        if s == 0:
            if bits:
                self.sized(unit, lambda rows: self.halving(0, unit, rows).start())
            return
        if s <= bits:
            self.sized(unit, lambda rows: self.halving(s - 1, unit, rows).wait())
            received = refs.into[s - 1].at[unit % self.ring]
            many = self.n_dp >> s
            if s == 1:
                kept = refs.unit.at[unit % self.unit_ring, pl.ds(many, many)]
            else:
                kept = refs.held[s - 2].at[unit % self.lags[s - 1], pl.ds(0, many)]
            if s < bits:
                refs.held[s - 1][unit % self.lags[s]] = kept[...] + received[...]
                self.sized(unit, lambda rows: self.halving(s, unit, rows).start())
                return
            refs.total[unit % self.sum_ring] = kept[0] + received[0]
        i = s - bits
        total = refs.total.at[unit % self.sum_ring]
        if i > 0:
            senders, receivers, adds = self.roles(i - 1)
            for sender, towards in senders:
                @pl.when(self.at_line == sender)
                def _():
                    self.sized(
                        unit, lambda rows: self.along(i - 1, unit, towards, rows).wait_send()
                    )

            @pl.when((self.at_line == receivers[0]) | (self.at_line == receivers[1]))
            def _():
                back = jnp.where(self.at_line == 0, 1, -1)
                self.sized(unit, lambda rows: self.along(i - 1, unit, back, rows).wait_recv())
                incoming = refs.line[i - 1].at[unit % self.line_ring]
                if adds:
                    total[...] = total[...] + incoming[...]
                else:
                    total[...] = incoming[...]
        if i < self.n_gen - 1:
            senders, _, _ = self.roles(i)
            for sender, towards in senders:
                @pl.when(self.at_line == sender)
                def _():
                    self.sized(unit, lambda rows: self.along(i, unit, towards, rows).start())
        else:
            out_ref[unit] = total[...]

    def put(self, unit, values, start=0):
        target = self.refs.unit.at[unit % self.unit_ring]
        stop = start + values.shape[1]
        for i in range(self.n_dp):
            part = values[i * self.rows : (i + 1) * self.rows].astype(LOW)
            target[self.positions[i], :, start:stop] = part

    def send(self, unit, out_ref):
        if self.bits + self.n_gen == 1:
            out_ref[unit] = self.refs.unit[unit % self.unit_ring, 0]
            return
        self.slot(unit, out_ref)
        self.stage(0, unit, out_ref)

    def drain(self, first, out_ref):
        def one(t, carried):
            self.slot(t, out_ref)
            return carried

        if self.bits + self.n_gen > 1:
            lax.fori_loop(first, self.slots, one, 0)

    def slot(self, t, out_ref):
        for s in reversed(range(1, self.final + 1)):
            unit = t - self.at[s]

            @pl.when((unit >= 0) & (unit < self.units))
            def _():
                self.stage(s, unit, out_ref)


class Shared:
    def __init__(self, plan, refs):
        self.plan, (self.own, self.all, self.sends, self.recvs) = plan, refs

    @staticmethod
    def scratch(n_dp, rows, features):
        many = max(n_dp - 1, 1)
        return (
            pltpu.VMEM((rows, features), LOW),
            pltpu.VMEM((n_dp, rows, features), LOW),
            pltpu.SemaphoreType.DMA((many,)),
            pltpu.SemaphoreType.DMA((many,)),
        )

    def copy(self, k):
        plan = self.plan
        return pltpu.make_async_remote_copy(
            src_ref=self.own,
            dst_ref=self.all.at[plan.place],
            send_sem=self.sends.at[k - 1],
            recv_sem=self.recvs.at[k - 1],
            device_id={"dp": (plan.place + k) % plan.n_dp, "gen": plan.at_line},
            device_id_type=pl.DeviceIdType.MESH,
        )

    def start(self, weights, vectors):
        plan = self.plan
        features = self.own.shape[1]
        rows, more = weights.shape[0], vectors.shape[0]
        for j in range(plan.n_gen):
            @pl.when(plan.at_line == j)
            def _():
                columns = slice(j * features, (j + 1) * features)
                self.own[:rows] = weights[:, columns]
                self.own[rows : rows + more] = vectors[:, columns]
        for k in range(1, plan.n_dp):
            self.copy(k).start()
        self.all[plan.place] = self.own[...]

    def finish(self, weights_ref, vectors_ref):
        for k in range(1, self.plan.n_dp):
            self.copy(k).wait()
        rows = self.plan.rows
        weights_ref[...] = self.all[:, :rows]
        vectors_ref[...] = self.all[:, rows:]


class Gains:
    def __init__(self, plan, refs):
        self.plan, (self.out, self.into, self.sends, self.recvs) = plan, refs

    @staticmethod
    def scratch(n_dp):
        many = max(n_dp - 1, 1)
        return (
            pltpu.VMEM((n_dp, 8, 128), WIDE),
            pltpu.VMEM((n_dp, 8, 128), WIDE),
            pltpu.SemaphoreType.DMA((many,)),
            pltpu.SemaphoreType.DMA((many,)),
        )

    def copy(self, k):
        plan = self.plan
        peer = (plan.place + k) % plan.n_dp
        return pltpu.make_async_remote_copy(
            src_ref=self.out.at[peer],
            dst_ref=self.into.at[plan.place],
            send_sem=self.sends.at[k - 1],
            recv_sem=self.recvs.at[k - 1],
            device_id={"dp": peer, "gen": plan.at_line},
            device_id_type=pl.DeviceIdType.MESH,
        )

    def start(self, gains):
        plan = self.plan
        self.out[...] = jnp.zeros_like(self.out)
        for i in range(plan.n_dp):
            self.out[i, 0:6, 0 : plan.rows] = gains[0:6, i * plan.rows : (i + 1) * plan.rows]
        for k in range(1, plan.n_dp):
            self.copy(k).start()
        self.into[plan.place] = self.out[plan.place]

    def finish(self, out_ref):
        for k in range(1, self.plan.n_dp):
            self.copy(k).wait()
        total = self.into[0]
        for j in range(1, self.plan.n_dp):
            total = total + self.into[j]
        out_ref[...] = total


def gen_greet(line, n_gen):
    semaphore = pltpu.get_barrier_semaphore()
    for k in range(1, n_gen):
        pl.semaphore_signal(
            semaphore, inc=1, device_id={"gen": (line + k) % n_gen},
            device_id_type=pl.DeviceIdType.MESH,
        )


def gen_greeted(n_gen):
    pl.semaphore_wait(pltpu.get_barrier_semaphore(), n_gen - 1)


def gen_copy(source, target, sends, recvs, line, k, n_gen):
    return pltpu.make_async_remote_copy(
        src_ref=source,
        dst_ref=target.at[line],
        send_sem=sends.at[k - 1],
        recv_sem=recvs.at[k - 1],
        device_id={"gen": (line + k) % n_gen},
        device_id_type=pl.DeviceIdType.MESH,
    )


def sum_gen_kernel(n_gen, part_ref, out_ref, parts, sends, recvs):
    line = lax.axis_index("gen")
    gen_greet(line, n_gen)
    gen_greeted(n_gen)
    for k in range(1, n_gen):
        gen_copy(part_ref, parts, sends, recvs, line, k, n_gen).start()
    parts[line] = part_ref[...]
    for k in range(1, n_gen):
        gen_copy(part_ref, parts, sends, recvs, line, k, n_gen).wait()
    total = parts[0]
    for j in range(1, n_gen):
        total = total + parts[j]
    out_ref[...] = total


def sum_gen(part):
    n_gen = lax.axis_size("gen")
    if n_gen == 1:
        return part
    return pl.pallas_call(
        functools.partial(sum_gen_kernel, n_gen),
        in_specs=[pl.BlockSpec(memory_space=pltpu.VMEM)],
        out_specs=pl.BlockSpec(memory_space=pltpu.VMEM),
        out_shape=jax.ShapeDtypeStruct(part.shape, part.dtype),
        scratch_shapes=[
            pltpu.VMEM((n_gen,) + part.shape, part.dtype),
            pltpu.SemaphoreType.DMA((n_gen - 1,)),
            pltpu.SemaphoreType.DMA((n_gen - 1,)),
        ],
        compiler_params=pltpu.CompilerParams(collective_id=2, has_side_effects=True),
        name="sum_gen",
    )(part)


class Operands(NamedTuple):
    cotangent: object
    cross_hidden: object
    dec_hidden: object
    encoded: object
    enc_hidden: object
    dec_rows: object
    enc_rows: object
    enc_qkv: object
    enc_proj: object
    enc_up: object
    enc_down: object
    dec_qkv: object
    dec_self_proj: object
    dec_cross_q: object
    dec_cross_kv: object
    dec_cross_proj: object
    dec_up: object
    dec_down: object
    enc_attn: Attended
    dec_attn: Attended
    cross_attn: Attended
    enc_ffn: Fed
    dec_ffn: Fed
    small: object


class Small(NamedTuple):
    enc_norms: object
    dec_norms: object
    adapters: object
    vectors: object
    wanted: object


class Results(NamedTuple):
    sums: object
    pair_weights: object
    pair_vectors: object
    gains: object
    grad_dec_rows: object
    grad_enc_rows: object


class Held(NamedTuple):
    total: object
    joint_dec: object
    joint_enc: object
    grad_low: object
    grad_a: object
    grad_b: object
    adapters: object
    vectors: object
    gains: object
    transfer: TransferRefs
    shared: object
    own_gains: object


class Backward:
    def __init__(self, plan, up_scale, bottleneck, tasks, refs, small, scratch, out_ref):
        self.plan, self.up_scale, self.bottleneck, self.tasks = plan, up_scale, bottleneck, tasks
        self.refs, self.small, self.scratch, self.out_ref = refs, small, scratch, out_ref

    def send(self, unit):
        self.plan.send(unit, self.out_ref)

    def attention(
        self, first_unit, grad_ref, gain_rows, x, memory, stored, weights, finish, after_first=None
    ):
        cross = memory is not None
        plan, scratch = self.plan, self.scratch
        total_x, total_memory, grad_low = scratch.total, scratch.grad_b, scratch.grad_low
        length, width = x.shape
        groups = width // GROUP
        columns = pl.BlockSpec((length, GROUP), lambda g: (0, g))
        rows = pl.BlockSpec((GROUP, length), lambda g: (g, 0))

        def weight_spec(offset):
            return pl.BlockSpec((width, GROUP), lambda g: (0, offset + g))

        def body(x_t_ref, q_t_ref, k_ref, v_ref, mixed_t_ref, probs_ref, wo_ref, *more):
            if cross:
                x_ref, wq_ref, wk_ref, wv_ref, memory_ref, memory_t_ref = more
            else:
                memory_t_ref = x_t_ref
            step = pl.program_id(0)

            @pl.when(step == 0)
            def _():
                grad_low[...] = grad_ref[...].astype(LOW)
                if cross:
                    total_x[...] = jnp.zeros_like(total_x)
                    total_memory[...] = jnp.zeros_like(total_memory)
                plan.put(first_unit, dot_nn(mixed_t_ref[...], grad_low[...]))
                self.send(first_unit)
                if after_first is not None:
                    after_first()

            grad_mixed = dot_nt(grad_low[...], wo_ref[...]).astype(LOW)
            grad_mixed_t = grad_mixed.T
            lanes = first_half((length, 2 * HD))
            heads = range(4)

            def pair_of(ref, head):
                pair = head // 2
                return ref[:, pair * 2 * HD : (pair + 1) * 2 * HD]

            def rows_of(ref, head):
                return ref[head * HD : (head + 1) * HD, :]

            grad_probs = []
            for head in heads:
                mine = jnp.where(
                    lanes if head % 2 == 0 else ~lanes, pair_of(grad_mixed, head), LOW(0)
                )
                grad_probs.append(dot_nt(mine, pair_of(v_ref, head)))
            mixed_rows = mixed_t_ref[pl.ds(pl.multiple_of(step * GROUP, GROUP), GROUP), :]
            pulled = grad_mixed_t.astype(WIDE) * mixed_rows.astype(WIDE)
            inner = [
                jnp.sum(rows_of(pulled, head), axis=0, keepdims=True) for head in heads
            ]
            inner = jnp.concatenate(inner + inner, axis=0).T
            inner = jnp.stack([inner[:, head : head + 1] for head in heads])
            probs = probs_ref[...].astype(WIDE)
            grad_scores = (probs * (jnp.stack(grad_probs) - inner)).astype(LOW)
            halves = [dot_nn(grad_scores[head], pair_of(k_ref, head)) for head in heads]
            grad_q = [
                jnp.where(lanes, halves[head], halves[head + 1]) * HD ** (-0.5)
                for head in heads[::2]
            ]
            grad_k = [
                dot_nn(rows_of(q_t_ref, head), grad_scores[head]) * HD ** (-0.5) for head in heads
            ]
            grad_v = [dot_nn(rows_of(grad_mixed_t, head), probs_ref[head]) for head in heads]
            low_q = jnp.concatenate(grad_q, axis=1).astype(LOW)
            low_k = jnp.concatenate(grad_k, axis=0).astype(LOW).T
            low_v = jnp.concatenate(grad_v, axis=0).astype(LOW).T
            unit = first_unit + 1 + step
            plan.put(unit, dot_nn(x_t_ref[...], low_q), 0)
            plan.put(unit, dot_nn(memory_t_ref[...], low_k), GROUP)
            plan.put(unit, dot_nn(memory_t_ref[...], low_v), 2 * GROUP)
            self.send(unit)
            if not cross:
                for part, low in enumerate((low_q, low_k, low_v)):
                    finish[part * groups + step] = low
                return
            total_x[...] += dot_nt(low_q, wq_ref[...])
            total_memory[...] += dot_nt(low_k, wk_ref[...]) + dot_nt(low_v, wv_ref[...])

            @pl.when(step == groups - 1)
            def _():
                x_gain, memory_gain = gain_rows
                grad_values, grad_gain = rms_backward(
                    x_ref[...].astype(WIDE), self.gain(x_gain), total_x[...]
                )
                scratch.gains[x_gain : x_gain + 1] = grad_gain
                finish(grad_ref[...] + grad_values)
                grad_values, grad_gain = rms_backward(
                    memory_ref[...], self.gain(memory_gain), total_memory[...]
                )
                scratch.gains[memory_gain : memory_gain + 1] = grad_gain
                scratch.grad_b[...] = grad_values

        whole_tokens, whole_turned = whole((length, width)), whole((width, length))
        pltpu.emit_pipeline(
            body,
            grid=(groups,),
            in_specs=[
                whole_turned, rows, columns, columns, whole_turned,
                pl.BlockSpec((4, length, length), lambda g: (g, 0, 0)),
                pl.BlockSpec((GROUP, width), lambda g: (g, 0)),
            ]
            + (
                [whole_tokens]
                + [weight_spec(offset * groups) for _, offset in weights[:3]]
                + [whole_tokens, whole_turned]
                if cross
                else []
            ),
        )(
            stored.x_t, stored.q_t, stored.keys, stored.values, stored.mixed_t, stored.probs,
            weights[3],
            *(
                [x] + [array for array, _ in weights[:3]] + [memory, stored.memory_t]
                if cross
                else []
            ),
        )

    def input_grad(self, first_slot, joint, grad_ref, gain_row, x, w_joint, target):
        scratch, total = self.scratch, self.scratch.total
        length, width = x.shape
        groups = width // GROUP

        def body(x_ref, wq_ref, wk_ref, wv_ref):
            step = pl.program_id(0)
            self.plan.slot(first_slot + step, self.out_ref)
            result = sum(
                dot_nt(joint[part * groups + step], weight[...])
                for part, weight in enumerate((wq_ref, wk_ref, wv_ref))
            )
            total[...] = jnp.where(step == 0, 0.0, total[...]) + result

            @pl.when(step == groups - 1)
            def _():
                grad_values, grad_gain = rms_backward(
                    x_ref[...].astype(WIDE), self.gain(gain_row), total[...]
                )
                scratch.gains[gain_row : gain_row + 1] = grad_gain
                target[...] = (grad_ref[...] + grad_values).astype(target.dtype)

        def weight_spec(part):
            return pl.BlockSpec((width, GROUP), lambda g: (0, part * groups + g))

        pltpu.emit_pipeline(
            body,
            grid=(groups,),
            in_specs=[whole((length, width))] + [weight_spec(part) for part in range(3)],
        )(x, w_joint, w_joint, w_joint)

    def gain(self, row):
        small = self.small
        return row_of(small.enc_norms, row) if row < 2 else row_of(small.dec_norms, row - 2)

    def feed_forward(
        self, first_unit, grad, x, gain_row, layer, w_up, w_down, stored, finish, after_adapter=None
    ):
        plan, small, scratch, up_scale = self.plan, self.small, self.scratch, self.up_scale
        total, grad_low = scratch.total, scratch.grad_low
        length, width = x.shape
        n_dp, blocks, rows, _ = stored.active_t.shape

        def body(x_ref, ffn_ref, x_t_ref, up_ref, down_ref, active_t_ref, slope_ref, *more):
            grad_ref = more[0] if more else scratch.grad_b
            step = pl.program_id(0)

            @pl.when(step == 0)
            def _():
                grad = grad_ref[...].astype(WIDE)
                vectors = small.vectors[layer].astype(WIDE)
                lower, upper = small.adapters[layer, 0], small.adapters[layer, 1]
                normed, scale = layer_parts(ffn_ref[...])
                gain = 1.0 + vectors[1:2]
                low = (normed * gain + vectors[2:3]).astype(LOW)
                inner = dot_nt(low, lower)
                cumulative, density = gelu_parts(inner)
                gate = (inner * cumulative).astype(LOW)
                scaled = (grad * up_scale).astype(LOW)
                scratch.adapters[layer, 1] = dot_nn(gate.T, scaled)
                grad_gate = dot_nt(scaled, upper)
                grad_inner = (grad_gate * (cumulative + inner * density)).astype(LOW)
                scratch.adapters[layer, 0] = dot_nn(grad_inner.T, low)
                grad_normed = dot_nn(grad_inner, lower)
                keep = scratch.vectors
                keep[3 * layer : 3 * layer + 1] = jnp.sum(grad, axis=0, keepdims=True)
                keep[3 * layer + 1 : 3 * layer + 2] = jnp.sum(
                    grad_normed * normed, axis=0, keepdims=True
                )
                keep[3 * layer + 2 : 3 * layer + 3] = jnp.sum(grad_normed, axis=0, keepdims=True)
                pulled = grad_normed * gain
                pulled = scale * (
                    pulled
                    - jnp.mean(pulled, axis=-1, keepdims=True)
                    - normed * jnp.mean(pulled * normed, axis=-1, keepdims=True)
                )
                grad_low[...] = (grad + pulled).astype(LOW)
                total[...] = jnp.zeros_like(total)
                if after_adapter is not None:
                    after_adapter()

            unit = first_unit + 2 * step
            plan.put(unit, dot_nn(join_rows(active_t_ref), grad_low[...]))
            self.send(unit)
            grad_active = dot_nt(grad_low[...], down_ref[...])
            grad_before = (grad_active * slope_ref[...].astype(WIDE)).astype(LOW)
            plan.put(unit + 1, dot_nn(x_t_ref[...], grad_before))
            self.send(unit + 1)
            total[...] += dot_nt(grad_before, up_ref[...])

            @pl.when(step == blocks - 1)
            def _():
                grad_values, grad_gain = rms_backward(
                    x_ref[...], self.gain(gain_row), total[...]
                )
                scratch.gains[gain_row : gain_row + 1] = grad_gain
                finish(grad_ref[...].astype(WIDE) + grad_values)

        tokens = whole((length, width))
        pltpu.emit_pipeline(
            body,
            grid=(blocks,),
            in_specs=[
                tokens, tokens, whole((width, length)),
                pl.BlockSpec((width, width), lambda j: (0, j)),
                pl.BlockSpec((width, width), lambda j: (j, 0)),
                pl.BlockSpec((n_dp, 1, rows, length), lambda j: (0, j, 0, 0)),
                pl.BlockSpec((length, width), lambda j: (0, j)),
            ]
            + ([] if grad is None else [tokens]),
        )(
            x, stored.ffn, stored.x_t, w_up, w_down, stored.active_t, stored.slope,
            *([] if grad is None else [grad]),
        )

    def own_rows(self, values, rows_per_task, first, count):
        parts = []
        while count:
            task, offset = divmod(first, rows_per_task)
            some = min(count, rows_per_task - offset)
            if task < self.tasks:
                weight = self.small.wanted[0:1, 2 * task : 2 * task + 1]
                parts.append(values[offset : offset + some] * weight)
            else:
                parts.append(jnp.zeros((some, values.shape[1]), WIDE))
            first, count = first + some, count - some
        return parts[0] if len(parts) == 1 else jnp.concatenate(parts, axis=0)

    def send_adapters(self, unit):
        plan, kept, size = self.plan, self.scratch.adapters, self.bottleneck
        values = jnp.concatenate(
            [kept[layer, part, :size] for layer in range(kept.shape[0]) for part in range(2)], axis=0
        )
        target = plan.refs.unit.at[unit % plan.unit_ring]
        for i in range(plan.n_dp):
            part = self.own_rows(values, values.shape[0], i * plan.rows, plan.rows)
            target[plan.positions[i]] = part.astype(LOW)
        self.send(unit)

    def send_vectors(self, unit, vector_rows):
        plan = self.plan
        values = self.scratch.vectors[:6]
        spare = -vector_rows % 16
        for i in range(plan.n_dp):
            part = self.own_rows(values, 6, i * vector_rows, vector_rows)
            if spare:
                part = jnp.concatenate([part, jnp.zeros((spare, plan.width), WIDE)], axis=0)
            target = plan.refs.unit.at[unit % plan.unit_ring, plan.positions[i]]
            target[: part.shape[0]] = part.astype(LOW)
        self.send(unit)


def backward_kernel(plan, up_scale, bottleneck, tasks, vector_rows, trees, *leaves):
    counts = [tree.num_leaves for tree in trees]
    parts, start = [], 0
    for tree, count in zip(trees, counts):
        parts.append(jax.tree.unflatten(tree, leaves[start : start + count]))
        start += count
    refs, out, scratch = parts
    plan.bind(scratch.transfer)
    plan.barrier()
    work = Backward(plan, up_scale, bottleneck, tasks, refs, refs.small, scratch, out.sums)
    shared = Shared(plan, scratch.shared)
    gains = Gains(plan, scratch.own_gains)
    grad_a, grad_b = scratch.grad_a, scratch.grad_b

    def into(ref):
        def finish(values):
            ref[...] = values.astype(ref.dtype)

        return finish

    def adapters():
        work.send_adapters(12)
        work.send_vectors(13, vector_rows)

    def share():
        shared.start(out.sums.at[12], out.sums.at[13, pl.ds(0, 16)])

    early = 13 + plan.at[plan.final] <= 26
    work.feed_forward(
        0, refs.cotangent, refs.cross_hidden, 4, 1, refs.dec_up, refs.dec_down, refs.dec_ffn,
        into(grad_a),
    )
    work.attention(
        8, grad_a, (3, 5), refs.dec_hidden, refs.encoded, refs.cross_attn,
        ((refs.dec_cross_q, 0), (refs.dec_cross_kv, 0), (refs.dec_cross_kv, 1), refs.dec_cross_proj),
        into(grad_a),
    )
    work.feed_forward(
        14, None, refs.enc_hidden, 1, 0, refs.enc_up, refs.enc_down, refs.enc_ffn, into(grad_b),
        after_adapter=adapters,
    )
    work.attention(
        22, grad_a, None, refs.dec_rows, None, refs.dec_attn, (None, None, None, refs.dec_self_proj),
        scratch.joint_dec,
    )
    work.attention(
        26, grad_b, None, refs.enc_rows, None, refs.enc_attn, (None, None, None, refs.enc_proj),
        scratch.joint_enc, after_first=share if early else None,
    )
    work.input_grad(
        30, scratch.joint_dec, grad_a, 2, refs.dec_rows, refs.dec_qkv, out.grad_dec_rows
    )
    work.input_grad(
        33, scratch.joint_enc, grad_b, 0, refs.enc_rows, refs.enc_qkv, out.grad_enc_rows
    )
    gains.start(scratch.gains)
    plan.drain(36, out.sums)
    if not early:
        share()
    gains.finish(out.gains)
    shared.finish(out.pair_weights, out.pair_vectors)


def backward(operands, features, up_scale, bottleneck, tasks, vector_rows):
    n_dp, n_gen = lax.axis_size("dp"), lax.axis_size("gen")
    length, width = operands.enc_rows.shape
    rows = width // n_dp
    plan = Transfer(30, (13,), n_dp, n_gen, rows, width, LAGS)

    def blocked(fed):
        return fed._replace(active_t=fed.active_t.reshape(n_dp, -1, rows, length))

    operands = operands._replace(
        enc_ffn=blocked(operands.enc_ffn), dec_ffn=blocked(operands.dec_ffn)
    )
    tokens = pltpu.VMEM((length, width), WIDE)
    joint = pltpu.VMEM((3 * width // GROUP, length, GROUP), LOW)
    shared_rows = rows + 16
    held = Held(
        total=tokens,
        joint_dec=joint,
        joint_enc=joint,
        grad_low=pltpu.VMEM((length, width), LOW),
        grad_a=tokens,
        grad_b=tokens,
        adapters=pltpu.VMEM(operands.small.adapters.shape, WIDE),
        vectors=pltpu.VMEM((8, width), WIDE),
        gains=pltpu.VMEM((8, width), WIDE),
        transfer=plan.scratch(),
        shared=Shared.scratch(n_dp, shared_rows, features),
        own_gains=Gains.scratch(n_dp),
    )
    shape = jax.ShapeDtypeStruct
    results = Results(
        sums=shape((plan.units, rows, width), LOW),
        pair_weights=shape((n_dp, rows, features), LOW),
        pair_vectors=shape((n_dp, 16, features), LOW),
        gains=shape((8, 128), WIDE),
        grad_dec_rows=shape((length, width), LOW),
        grad_enc_rows=shape((length, width), LOW),
    )
    in_vmem = pl.BlockSpec(memory_space=pltpu.VMEM)
    in_hbm = pl.BlockSpec(memory_space=pl.ANY)
    specs = jax.tree.map(lambda _: in_hbm, operands)
    specs = specs._replace(small=jax.tree.map(lambda _: in_vmem, operands.small))
    flat, in_tree = jax.tree.flatten(operands)
    scratch, scratch_tree = jax.tree.flatten(held)
    out, out_tree = jax.tree.flatten(results)
    remote = n_dp * n_gen > 1
    outs = pl.pallas_call(
        functools.partial(
            backward_kernel, plan, up_scale, bottleneck, tasks, vector_rows,
            (in_tree, out_tree, scratch_tree),
        ),
        in_specs=jax.tree.leaves(specs),
        out_specs=[in_vmem] * len(out),
        out_shape=out,
        scratch_shapes=scratch,
        compiler_params=pltpu.CompilerParams(
            vmem_limit_bytes=VMEM_LIMIT,
            **(dict(collective_id=0, has_side_effects=True) if remote else {}),
        ),
        cost_estimate=pl.CostEstimate(
            flops=100 * length * width * width, bytes_accessed=160 * width * width,
            transcendentals=0,
        ),
        name="backward",
    )(*flat)
    return jax.tree.unflatten(out_tree, outs)


class Gradients(NamedTuple):
    enc_norms: object
    enc_qkv: object
    enc_proj: object
    enc_up: object
    enc_down: object
    dec_norms: object
    dec_qkv: object
    dec_self_proj: object
    dec_cross_q: object
    dec_cross_kv: object
    dec_cross_proj: object
    dec_up: object
    dec_down: object


def unpack_kernel(sums_ref, gains_ref, dec_ref, enc_ref, *outs):
    out = Gradients(*outs[:13])
    outs[13][...] = dec_ref[...]
    outs[14][...] = enc_ref[...]
    size = out.enc_norms.shape[1]
    gains = gains_ref[gains_ref.shape[0] - 8 :, :]

    @pl.when(pl.program_id(0) == 0)
    def _():
        out.enc_norms[...] = gains[0:2, :size]
        out.dec_norms[...] = gains[2:6, :size]

    def plain(target, unit):
        target[...] = sums_ref[unit].astype(WIDE)

    def joint(target, first, parts):
        for at, part in enumerate(parts):
            for g in range(3):
                start = (3 * at + g) * GROUP
                target[:, start : start + GROUP] = sums_ref[
                    first + g, :, part * GROUP : (part + 1) * GROUP
                ].astype(WIDE)

    def beside(target, first):
        width = sums_ref.shape[2]
        for j in range(target.shape[1] // width):
            target[:, j * width : (j + 1) * width] = sums_ref[first + 2 * j].astype(WIDE)

    def below(target, first):
        for j in range(target.shape[0]):
            target[j] = sums_ref[first + 2 * j].astype(WIDE)

    below(out.dec_down, 0)
    beside(out.dec_up, 1)
    plain(out.dec_cross_proj, 8)
    joint(out.dec_cross_q, 9, (0,))
    joint(out.dec_cross_kv, 9, (1, 2))
    below(out.enc_down, 14)
    beside(out.enc_up, 15)
    plain(out.dec_self_proj, 22)
    joint(out.dec_qkv, 23, (0, 1, 2))
    plain(out.enc_proj, 26)
    joint(out.enc_qkv, 27, (0, 1, 2))


def unpack(sums, gains, grad_dec_rows, grad_enc_rows, inner):
    units, rows, width = sums.shape
    length = grad_dec_rows.shape[0]
    steps = rows // 32 if rows % 32 == 0 else 1
    block = rows // steps
    while length % (16 * steps):
        steps, block = 1, rows
    shape = jax.ShapeDtypeStruct

    def matrix(columns):
        return shape((rows, columns), WIDE), pl.BlockSpec((block, columns), lambda i: (i, 0))

    downs = inner // width
    down = (
        shape((downs, rows, width), WIDE),
        pl.BlockSpec((downs, block, width), lambda i: (0, i, 0)),
    )
    tokens = pl.BlockSpec((length // steps, width), lambda i: (i, 0))

    def norms(count):
        return shape((count, rows), WIDE), whole((count, rows))

    made = Gradients(
        enc_norms=norms(2), enc_qkv=matrix(3 * width), enc_proj=matrix(width),
        enc_up=matrix(inner), enc_down=down, dec_norms=norms(4), dec_qkv=matrix(3 * width),
        dec_self_proj=matrix(width), dec_cross_q=matrix(width), dec_cross_kv=matrix(2 * width),
        dec_cross_proj=matrix(width), dec_up=matrix(inner), dec_down=down,
    )
    outs = pl.pallas_call(
        unpack_kernel,
        grid=(steps,),
        in_specs=[
            pl.BlockSpec((units, block, width), lambda i: (0, i, 0)),
            whole(gains.shape),
            tokens,
            tokens,
        ],
        out_specs=[spec for _, spec in made] + [tokens, tokens],
        out_shape=[one for one, _ in made] + [shape((length, width), LOW)] * 2,
        compiler_params=pltpu.CompilerParams(vmem_limit_bytes=VMEM_LIMIT),
        cost_estimate=pl.CostEstimate(
            flops=0, bytes_accessed=6 * units * rows * width, transcendentals=0
        ),
        name="unpack",
    )(sums, gains, grad_dec_rows, grad_enc_rows)
    grads = Gradients(*outs[:13])
    grads = grads._replace(
        enc_down=grads.enc_down.reshape(-1, width), dec_down=grads.dec_down.reshape(-1, width)
    )
    return grads, outs[13], outs[14]


def gelu_exact(values):
    return jax.nn.gelu(values, approximate=False)


def body(
    enc_input,
    dec_input,
    enc_segments,
    dec_segments,
    task_ids,
    cotangent,
    enc_norms,
    enc_qkv,
    enc_proj,
    enc_up,
    enc_down,
    dec_norms,
    dec_qkv,
    dec_self_proj,
    dec_cross_q,
    dec_cross_kv,
    dec_cross_proj,
    dec_up,
    dec_down,
    task_emb,
    layer_emb,
    proj_task,
    gen_weight,
    gen_vector,
):
    _, length, width = enc_input.shape
    layer_count = layer_emb.shape[0]
    pair_count = task_emb.shape[0] * layer_count
    bottleneck = gen_weight.shape[1] // 2
    up_scale = (width / bottleneck) ** 0.5

    def source_of(task_table, layer_table, projection):
        mixed_in = (
            jnp.dot(task_table, projection, precision=HIGHEST)[:, None, :] + layer_table[None, :, :]
        )
        return gelu_exact(mixed_in).reshape(pair_count, -1)

    source, source_pull = jax.vjp(source_of, task_emb, layer_emb, proj_task)
    source_low = source.astype(LOW)
    pieces, more_pieces = [
        jnp.einsum("th,hkd->tkd", source_low, part, preferred_element_type=WIDE).astype(LOW)
        for part in (gen_weight, gen_vector)
    ]
    first_pair = task_ids[0] * layer_count
    wanted = jnp.arange(8)[:, None] + first_pair == jnp.arange(128)[None, :]
    wanted = wanted.astype(WIDE)

    enc_rows, dec_rows = enc_input[0], dec_input[0]
    enc_joint = [(enc_qkv, 0), (enc_qkv, 1), (enc_qkv, 2)]
    dec_joint = [(dec_qkv, 0), (dec_qkv, 1), (dec_qkv, 2)]
    cross_joint = [(dec_cross_q, 0), (dec_cross_kv, 0), (dec_cross_kv, 1)]
    enc_hidden, enc_stored, adapters, vectors = attention_forward(
        enc_rows, enc_norms, (0, 0), None, enc_segments, enc_segments, enc_joint, enc_proj, False,
        gather=(wanted, pieces, more_pieces, bottleneck),
    )
    dec_hidden, dec_stored = attention_forward(
        dec_rows, dec_norms, (0, 0), None, dec_segments, dec_segments, dec_joint, dec_self_proj, True
    )
    encoded, enc_ffn_stored = feed_forward(
        enc_hidden, enc_norms, 1, enc_up, enc_down, adapters, vectors, 0, up_scale, WIDE
    )
    cross_hidden, cross_stored = attention_forward(
        dec_hidden, dec_norms, (1, 3), encoded, dec_segments, enc_segments, cross_joint,
        dec_cross_proj, False,
    )
    decoded, dec_ffn_stored = feed_forward(
        cross_hidden, dec_norms, 2, dec_up, dec_down, adapters, vectors, 1, up_scale, LOW
    )

    n_dp = lax.axis_size("dp")
    rows = width // n_dp
    features = gen_weight.shape[2]
    vector_rows = -(-pair_count * 3 // n_dp)
    small = Small(enc_norms, dec_norms, adapters, vectors, wanted)
    operands = Operands(
        cotangent[0], cross_hidden, dec_hidden, encoded, enc_hidden, dec_rows, enc_rows,
        enc_qkv, enc_proj, enc_up, enc_down, dec_qkv, dec_self_proj, dec_cross_q, dec_cross_kv,
        dec_cross_proj, dec_up, dec_down,
        enc_stored, dec_stored, cross_stored, enc_ffn_stored, dec_ffn_stored, small,
    )
    result = backward(
        operands, features, up_scale, bottleneck, task_emb.shape[0], vector_rows
    )
    pair_weights = result.pair_weights.reshape(pair_count, 2 * bottleneck, features)
    pair_vectors = result.pair_vectors[:, :vector_rows].reshape(-1, features)
    pair_vectors = pair_vectors[: pair_count * 3].reshape(pair_count, 3, features)
    grad_gen_weight, grad_gen_vector = [
        jnp.einsum("th,tkd->hkd", source_low, part, preferred_element_type=WIDE)
        for part in (pair_weights, pair_vectors)
    ]
    part_source = sum(
        jnp.einsum("tkd,hkd->th", part, made, preferred_element_type=WIDE)
        for part, made in ((pair_weights, gen_weight), (pair_vectors, gen_vector))
    )
    summed = sum_gen(jnp.concatenate([part_source, result.gains], axis=0))
    grad_task_emb, grad_layer_emb, grad_proj_task = source_pull(summed[:pair_count])

    grads, grad_dec_rows, grad_enc_rows = unpack(
        result.sums, summed, result.grad_dec_rows, result.grad_enc_rows, enc_up.shape[1]
    )
    return (
        decoded[None],
        grad_enc_rows[None],
        grad_dec_rows[None],
        *grads,
        grad_task_emb,
        grad_layer_emb,
        grad_proj_task,
        grad_gen_weight,
        grad_gen_vector,
    )


def solution(mesh):
    in_specs = (
        P(("dp", "gen"), None, None),
        P(("dp", "gen"), None, None),
        P(("dp", "gen"), None),
        P(("dp", "gen"), None),
        P(("dp", "gen")),
        P(("dp", "gen"), None, None),
        P(),
        P(),
        P(),
        P(),
        P(),
        P(),
        P(),
        P(),
        P(),
        P(),
        P(),
        P(),
        P(),
        P(),
        P(),
        P(),
        P(None, None, "gen"),
        P(None, None, "gen"),
    )
    out_specs = (
        P(("dp", "gen"), None, None),
        P(("dp", "gen"), None, None),
        P(("dp", "gen"), None, None),
        P(None, "dp"),
        P("dp", None),
        P("dp", None),
        P("dp", None),
        P("dp", None),
        P(None, "dp"),
        P("dp", None),
        P("dp", None),
        P("dp", None),
        P("dp", None),
        P("dp", None),
        P("dp", None),
        P("dp", None),
        P(),
        P(),
        P(),
        P(None, None, "gen"),
        P(None, None, "gen"),
    )
    return jax.shard_map(body, mesh=mesh, in_specs=in_specs, out_specs=out_specs, check_vma=False)
```
